32 devices in a mesh: gx: 8 (over y, x, core), gy: 4 (over z).
Axes of the slice: x: 2, y: 2, z: 4, core: 2. Of those that a mesh axis runs over, the one named last changes fastest.
Arguments:
- labels: int32 [64, 128, 64], P('gx', 'gy'), may hold values from 0 to 3
- seed_noise: float32 [4, 64, 128, 64], P(None, 'gx', 'gy'), may hold values from 0.05 to 1
- conc: float32 [64, 128, 64], P('gx', 'gy'), may hold values from 0.1 to 0.9
- curvature: float32 [4], replicated, may hold values from 1 to 4
- quartic: float32 [4], replicated, may hold values from 2 to 16
- wells: float32 [4], replicated, may hold values from 0.1 to 0.9
- lame: float32 [2, 4], replicated, may hold values from 0.5 to 2
- eigen: float32 [4, 6], replicated, may hold values from -3 to 3
Outputs:
- phase_next: float32 [4, 64, 128, 64], P(None, 'gx', 'gy')
- conc_next: float32 [64, 128, 64], P('gx', 'gy')
- stress: float32 [6, 64, 128, 64], P(None, 'gx', 'gy')
The draws below stay inside these ranges and needn't reach their ends.
All inputs are finite; a program needn't handle non-finite values.
Results may differ from the reference program's by a relative error of at most 0.0003.
Values sent between devices are 32-bit elements; how exact they have to be, the bound alone decides.
A program may use at most 128 MiB of HBM per device.

```python
import math
import jax
import jax.numpy as jnp
from jax import lax

NZ = 64
NEWTON = 5
ITERS = 2
NX = 64
NY = 128


def touch_ends(values, key, smallest, top_value):
    index_at = [jax.random.randint(jax.random.fold_in(key, axis), (), 0, length) for axis, length in enumerate(values.shape)]
    main_axis = values.shape.index(max(values.shape))
    neighbour = index_at[:main_axis] + [(index_at[main_axis] + 1) % values.shape[main_axis]] + index_at[main_axis + 1:]
    return values.at[tuple(index_at)].set(smallest).at[tuple(neighbour)].set(top_value)


def levels(rng, shape, pieces, least, top_value):
    loudness, own = 1.0, jax.random.fold_in(rng, 6)
    for position, blocks in pieces:
        steps = jnp.exp(jax.random.uniform(jax.random.fold_in(own, position), (blocks,), jnp.float32, least / len(pieces), top_value / len(pieces)))
        loudness = loudness * jnp.repeat(steps, shape[position] // blocks).reshape([-1 if axis == position else 1 for axis in range(len(shape))])
    return loudness


def scatter_about(own_key, shape, width, reach, kind=jnp.bfloat16):
    return jnp.clip(width * jax.random.normal(own_key, shape, jnp.float32), -reach, reach).astype(kind)


def setup_inputs(seed: int = 0) -> dict:
    seeds = jax.random.split(jax.random.key(seed), 9)
    return {
        "labels": touch_ends(jax.random.randint(seeds[0], (NX, NY, NZ), 0, 4), jax.random.fold_in(seeds[0], 1), 0, 3).astype(jnp.int32),
        "seed_noise": jnp.clip(0.05 + 0.95 * jax.random.uniform(seeds[1], (4, NX, NY, NZ), jnp.float32) ** levels(seeds[1], (4, NX, NY, NZ), ((1, 8), (2, 4)), -0.2, 0.2), 0.05, 1.0),
        "conc": jnp.clip(0.1 + 0.79999997 * jax.random.uniform(seeds[2], (NX, NY, NZ), jnp.float32) ** levels(seeds[2], (NX, NY, NZ), ((0, 8), (1, 4)), -0.2, 0.2), 0.1, 0.9),
        "curvature": jnp.clip(jnp.exp(jax.random.uniform(seeds[3], (4,), jnp.float32, math.log(1.0), math.log(4.0))), 1.0, 4.0),
        "quartic": jnp.clip(jnp.exp(jax.random.uniform(seeds[4], (4,), jnp.float32, math.log(2.0), math.log(16.0))), 2.0, 16.0),
        "wells": jnp.clip(jax.random.uniform(seeds[5], (4,), jnp.float32, 0.1, 0.9), 0.1, 0.9),
        "lame": jnp.clip(jnp.exp(jax.random.uniform(seeds[6], (2, 4), jnp.float32, math.log(0.5), math.log(2.0))), 0.5, 2.0),
        "eigen": scatter_about(seeds[7], (4, 6), 0.3, 3.0, jnp.float32),
    }


step_phase = 0.06
step_conc = 0.005


def column(values):
    return values.reshape(4, 1, 1, 1)


def phases_from(labels, seed_noise):
    marks = lax.broadcasted_iota(jnp.int32, (4, 1, 1, 1), 0)
    raw = seed_noise + 2.0 * (labels[None] == marks).astype(seed_noise.dtype)
    return raw / jnp.sum(raw, axis=0, keepdims=True)


def partition(phase, conc, curvature, quartic, wells):
    coef_a = column(curvature)
    coef_b = column(quartic)
    centre = column(wells)
    part = jnp.broadcast_to(conc[None], phase.shape)
    deviate = part - centre
    chem = jnp.sum(phase * (coef_a * deviate + coef_b * deviate ** 3), axis=0)
    for _ in range(NEWTON):
        deviate = part - centre
        slope = coef_a * deviate + coef_b * deviate ** 3 - chem[None]
        stiff = coef_a + 3.0 * coef_b * deviate * deviate
        shift = (conc - jnp.sum(phase * part, axis=0) + jnp.sum(phase * slope / stiff, axis=0)) / jnp.sum(phase / stiff, axis=0)
        part = part + (shift[None] - slope) / stiff
        chem = chem + shift
    return part, chem


def stress_of(strain, eigen_field, lam_field, shear_field):
    elastic = strain - eigen_field
    trace = elastic[0] + elastic[1] + elastic[2]
    normal = (lax.broadcasted_iota(jnp.int32, (6, 1, 1, 1), 0) < 3).astype(strain.dtype)
    return 2.0 * shear_field[None] * elastic + (lam_field * trace)[None] * normal


def green(tau, freq_x, freq_y, freq_z, zero, lam0, mu0):
    vec_x = tau[0] * freq_x + tau[5] * freq_y + tau[4] * freq_z
    vec_y = tau[5] * freq_x + tau[1] * freq_y + tau[3] * freq_z
    vec_z = tau[4] * freq_x + tau[3] * freq_y + tau[2] * freq_z
    inner = freq_x * vec_x + freq_y * vec_y + freq_z * vec_z
    square = freq_x * freq_x + freq_y * freq_y + freq_z * freq_z + zero
    first = 1.0 / (2.0 * mu0 * square)
    second = (lam0 + mu0) / (mu0 * (lam0 + 2.0 * mu0)) * inner / (square * square)
    pairs = ((freq_x, vec_x, freq_x, vec_x), (freq_y, vec_y, freq_y, vec_y), (freq_z, vec_z, freq_z, vec_z),
             (freq_y, vec_y, freq_z, vec_z), (freq_x, vec_x, freq_z, vec_z), (freq_x, vec_x, freq_y, vec_y))
    result = [(fk * vh + fh * vk) * first - fk * fh * second for fk, vk, fh, vh in pairs]
    return jnp.stack(result, axis=0)


def signed_freq(length, axis, dtype):
    index = jnp.arange(length, dtype=jnp.int32)
    index = jnp.where(index >= length // 2, index - length, index)
    kept = jnp.where(index == -(length // 2), 0, index).astype(jnp.int32)
    dims_shape = [1, 1, 1]
    dims_shape[axis] = length
    return (kept.astype(dtype) / length).reshape(dims_shape)


def laplace(field):
    total = -6.0 * field
    for axis in (1, 2, 3):
        total = total + jnp.roll(field, 1, axis) + jnp.roll(field, -1, axis)
    return total


def reference(labels, seed_noise, conc, curvature, quartic, wells, lame, eigen):
    dtype = seed_noise.dtype
    phase = phases_from(labels, seed_noise)
    part, chem = partition(phase, conc, curvature, quartic, wells)
    lam_field = jnp.sum(phase * column(lame[0]), axis=0)
    shear_field = jnp.sum(phase * column(lame[1]), axis=0)
    eigen_field = jnp.einsum("ap,axyz->pxyz", eigen, phase, precision=lax.Precision.HIGHEST)
    lam0 = 0.5 * (jnp.max(lame[0]) + jnp.min(lame[0]))
    mu0 = 0.5 * (jnp.max(lame[1]) + jnp.min(lame[1]))
    freq_x = signed_freq(NX, 0, dtype)
    freq_y = signed_freq(NY, 1, dtype)
    freq_z = signed_freq(NZ, 2, dtype)
    zero = ((freq_x == 0.0) & (freq_y == 0.0) & (freq_z == 0.0)).astype(dtype)
    strain = jnp.zeros((6, NX, NY, NZ), dtype)
    for _ in range(ITERS):
        stress = stress_of(strain, eigen_field, lam_field, shear_field)
        spectrum = jnp.fft.fftn(stress, axes=(1, 2, 3))
        upd_real = green(jnp.real(spectrum), freq_x, freq_y, freq_z, zero, lam0, mu0)
        upd_imag = green(jnp.imag(spectrum), freq_x, freq_y, freq_z, zero, lam0, mu0)
        change = jnp.real(jnp.fft.ifftn(lax.complex(upd_real, upd_imag), axes=(1, 2, 3)))
        strain = strain - change.astype(dtype)
    stress = stress_of(strain, eigen_field, lam_field, shear_field)
    deviate = part - column(wells)
    energy = 0.5 * column(curvature) * deviate ** 2 + 0.25 * column(quartic) * deviate ** 4
    chemical = energy - chem[None] * part
    elastic = strain - eigen_field
    trace = elastic[0] + elastic[1] + elastic[2]
    squares = elastic[0] ** 2 + elastic[1] ** 2 + elastic[2] ** 2 + 2.0 * (elastic[3] ** 2 + elastic[4] ** 2 + elastic[5] ** 2)
    weight = jnp.array([1.0, 1.0, 1.0, 2.0, 2.0, 2.0], dtype)
    coupling = jnp.einsum("ap,pxyz->axyz", eigen * weight[None], stress, precision=lax.Precision.HIGHEST)
    stored = 0.5 * (column(lame[0]) * trace[None] ** 2 + 2.0 * column(lame[1]) * squares[None]) - coupling
    total_sq = jnp.sum(phase * phase, axis=0)
    barrier = 2.0 * phase * (total_sq[None] - phase * phase)
    force = chemical + stored + barrier - laplace(phase)
    phase_next = phase - step_phase * (force - jnp.mean(force, axis=0, keepdims=True))
    conc_next = conc + step_conc * laplace(chem[None])[0]
    return phase_next, conc_next, stress
```

```python
import functools
import math

import jax
import jax.numpy as jnp
import numpy as np
from jax import lax
from jax.experimental import pallas as pl
from jax.experimental.pallas import tpu as pltpu
from jax.sharding import PartitionSpec as P

NEWTON = 5
ITERS = 2


step_phase = 0.06
step_conc = 0.005


def with_halo(x, sides, width):
    for axis, dim in sides:
        count, length = (lax.axis_size(axis), x.shape[dim])
        up = [(i, (i + 1) % count) for i in range(count)]
        down = [(j, i) for i, j in up]
        last = lax.slice_in_dim(x, length - width, length, axis=dim)
        initial = lax.slice_in_dim(x, 0, width, axis=dim)
        before = lax.ppermute(last, axis, up)
        after = lax.ppermute(initial, axis, down)
        x = jnp.concatenate([before, x, after], axis=dim)
    return x


def column(values):
    return values.reshape(4, 1, 1, 1)


def phases_from(labels, seed_noise):
    marks = lax.broadcasted_iota(jnp.int32, (4, 1, 1, 1), 0)
    raw = seed_noise + 2.0 * (labels[None] == marks).astype(seed_noise.dtype)
    return raw / jnp.sum(raw, axis=0, keepdims=True)


def partition(phase, conc, curvature, quartic, wells):
    coef_a = column(curvature)
    coef_b = column(quartic)
    centre = column(wells)
    part = jnp.broadcast_to(conc[None], phase.shape)
    deviate = part - centre
    chem = jnp.sum(phase * (coef_a * deviate + coef_b * deviate**3), axis=0)
    for _ in range(NEWTON):
        deviate = part - centre
        slope = coef_a * deviate + coef_b * deviate**3 - chem[None]
        stiff = coef_a + 3.0 * coef_b * deviate * deviate
        shift = (
            conc - jnp.sum(phase * part, axis=0) + jnp.sum(phase * slope / stiff, axis=0)
        ) / jnp.sum(phase / stiff, axis=0)
        part = part + (shift[None] - slope) / stiff
        chem = chem + shift
    return (part, chem)


def stress_of(strain, eigen_field, lam_field, shear_field):
    elastic = strain - eigen_field
    trace = elastic[0] + elastic[1] + elastic[2]
    normal = (lax.broadcasted_iota(jnp.int32, (6, 1, 1, 1), 0) < 3).astype(strain.dtype)
    return 2.0 * shear_field[None] * elastic + (lam_field * trace)[None] * normal


def green(tau, freq_x, freq_y, freq_z, zero, lam0, mu0):
    vec_x = tau[0] * freq_x + tau[5] * freq_y + tau[4] * freq_z
    vec_y = tau[5] * freq_x + tau[1] * freq_y + tau[3] * freq_z
    vec_z = tau[4] * freq_x + tau[3] * freq_y + tau[2] * freq_z
    inner = freq_x * vec_x + freq_y * vec_y + freq_z * vec_z
    square = freq_x * freq_x + freq_y * freq_y + freq_z * freq_z + zero
    first = 1.0 / (2.0 * mu0 * square)
    second = (lam0 + mu0) / (mu0 * (lam0 + 2.0 * mu0)) * inner / (square * square)
    pairs = (
        (freq_x, vec_x, freq_x, vec_x),
        (freq_y, vec_y, freq_y, vec_y),
        (freq_z, vec_z, freq_z, vec_z),
        (freq_y, vec_y, freq_z, vec_z),
        (freq_x, vec_x, freq_z, vec_z),
        (freq_x, vec_x, freq_y, vec_y),
    )
    result = [(fk * vh + fh * vk) * first - fk * fh * second for fk, vk, fh, vh in pairs]
    return jnp.stack(result, axis=0)


def tables(length):
    grid = lax.broadcasted_iota(jnp.int32, (length, length), 0) * lax.broadcasted_iota(
        jnp.int32, (length, length), 1
    )
    angle = (grid % length).astype(jnp.float32) * (2.0 * math.pi / length)
    return (jnp.cos(angle), jnp.sin(angle))


def apply_table(table, data, axis):
    if axis == 3:
        flat = data.reshape(-1, data.shape[3])
        result = jnp.dot(
            flat, table.T, precision=lax.Precision.HIGHEST, preferred_element_type=jnp.float32
        )
        return result.reshape(data.shape[:3] + (table.shape[0],))
    moved = jnp.moveaxis(data, axis, 0)
    rest = moved.shape[1:]
    flat = moved.reshape(moved.shape[0], -1)
    result = jnp.dot(
        table, flat, precision=lax.Precision.HIGHEST, preferred_element_type=jnp.float32
    )
    return jnp.moveaxis(result.reshape((table.shape[0],) + rest), 0, axis)


def transform(pair, axis, inverse):
    real, imag = pair
    length = real.shape[axis]
    cosine, sine = tables(length)
    if inverse:
        new_real = (apply_table(cosine, real, axis) - apply_table(sine, imag, axis)) / length
        new_imag = (apply_table(cosine, imag, axis) + apply_table(sine, real, axis)) / length
    else:
        new_real = apply_table(cosine, real, axis) + apply_table(sine, imag, axis)
        new_imag = apply_table(cosine, imag, axis) - apply_table(sine, real, axis)
    return (new_real, new_imag)


def spectrum(stress):
    length = stress.shape[3]
    cosine, sine = tables(length)
    real = apply_table(cosine, stress, 3)
    imag = -apply_table(sine, stress, 3)
    real, imag = transform(
        (
            lax.all_to_all(real, "gy", split_axis=3, concat_axis=2, tiled=True),
            lax.all_to_all(imag, "gy", split_axis=3, concat_axis=2, tiled=True),
        ),
        axis=2,
        inverse=False,
    )
    real, imag = transform(
        (
            lax.all_to_all(real, "gx", split_axis=2, concat_axis=1, tiled=True),
            lax.all_to_all(imag, "gx", split_axis=2, concat_axis=1, tiled=True),
        ),
        axis=1,
        inverse=False,
    )
    return (real, imag)


def recover(pair):
    pair = transform(pair, 1, True)
    pair = transform(
        (
            lax.all_to_all(pair[0], "gx", split_axis=1, concat_axis=2, tiled=True),
            lax.all_to_all(pair[1], "gx", split_axis=1, concat_axis=2, tiled=True),
        ),
        axis=2,
        inverse=True,
    )
    result = transform(
        (
            lax.all_to_all(pair[0], "gy", split_axis=2, concat_axis=3, tiled=True),
            lax.all_to_all(pair[1], "gy", split_axis=2, concat_axis=3, tiled=True),
        ),
        axis=3,
        inverse=True,
    )
    return result


def frequencies(count, offset, length, axis):
    index = lax.iota(jnp.int32, count) + offset
    index = jnp.where(index >= length // 2, index - length, index)
    kept = jnp.where(index == -(length // 2), 0, index)
    dims_shape = [1, 1, 1]
    dims_shape[axis] = count
    return (kept.astype(jnp.float32) / length).reshape(dims_shape)


def wave_numbers(dims, full_x, full_y, full_z):
    offsets = (jnp.int32(0), lax.axis_index("gx") * dims[2], lax.axis_index("gy") * dims[3])
    freq_x = frequencies(dims[1], offsets[0], full_x, 0)
    freq_y = frequencies(dims[2], offsets[1], full_y, 1)
    freq_z = frequencies(dims[3], offsets[2], full_z, 2)
    zero = ((freq_x == 0.0) & (freq_y == 0.0) & (freq_z == 0.0)).astype(jnp.float32)
    return (freq_x, freq_y, freq_z, zero)


def slots_fit(full_z):
    count = lax.axis_size("gx") * lax.axis_size("gy")
    return full_z % 2 == 0 and (full_z // 2) % count == 0


def angles(length):
    grid = np.outer(np.arange(length), np.arange(length)) % length
    return grid * (2.0 * math.pi / length)


def z_tables(length):
    half = length // 2
    angle = angles(length)[:half]
    real = np.cos(angle)
    imag = -np.sin(angle)
    imag[0] = np.cos(math.pi * np.arange(length))
    forward = np.stack([real, imag], axis=1).astype(np.float32)
    weight = np.full((half, 1, 1), 2.0 / length)
    weight[0] = 1.0 / length
    return forward, (np.stack([real, imag], axis=1) * weight).astype(np.float32)


def complex_table(length, inverse):
    angle = angles(length)
    cosine, sine = np.cos(angle), np.sin(angle)
    if inverse:
        table = np.array([[cosine, -sine], [sine, cosine]]) / length
    else:
        table = np.array([[cosine, sine], [-sine, cosine]])
    return table.transpose(0, 2, 1, 3).astype(np.float32)


def contract(spec, *operands):
    return jnp.einsum(
        spec, *operands, precision=lax.Precision.HIGH, preferred_element_type=jnp.float32
    )


def fluctuation(stress, full_x, full_y, full_z, lam0, mu0):
    count_x, count_y = lax.axis_size("gx"), lax.axis_size("gy")
    count = count_x * count_y
    _, size_x, size_y, _ = stress.shape
    slots = full_z // 2 // count
    forward_z, inverse_z = z_tables(full_z)
    data = contract("krz,cxyz->krcxy", forward_z, stress)
    data = lax.all_to_all(data, ("gx", "gy"), split_axis=0, concat_axis=0, tiled=True)
    data = data.reshape(count_x, count_y, slots, 2, 6, size_x, size_y)
    data = data.transpose(2, 3, 4, 0, 5, 1, 6).reshape(slots, 2, 6, full_x, full_y)
    data = contract("sLrl,krcly->kscLy", complex_table(full_x, False), data)
    data = contract("sLrl,krcxl->kscxL", complex_table(full_y, False), data)
    data = data.transpose(2, 1, 3, 4, 0)
    freq_x = frequencies(full_x, 0, full_x, 0)
    freq_y = frequencies(full_y, 0, full_y, 1)
    position = lax.axis_index("gx") * count_y + lax.axis_index("gy")
    freq_z = frequencies(slots, position * slots, full_z, 2)
    zero = ((freq_x == 0.0) & (freq_y == 0.0) & (freq_z == 0.0)).astype(jnp.float32)
    data = jnp.stack([green(data[:, r], freq_x, freq_y, freq_z, zero, lam0, mu0) for r in (0, 1)], 1)
    data = data.transpose(4, 1, 0, 2, 3)
    data = contract("sLrl,krcxl->kscxL", complex_table(full_y, True), data)
    data = contract("sLrl,krcly->kscLy", complex_table(full_x, True), data)
    data = data.reshape(slots, 2, 6, count_x, size_x, count_y, size_y)
    data = data.transpose(3, 5, 0, 1, 2, 4, 6).reshape(count * slots, 2, 6, size_x, size_y)
    data = lax.all_to_all(data, ("gx", "gy"), split_axis=0, concat_axis=0, tiled=True)
    return contract("krz,krcxy->cxyz", inverse_z, data)


def fluctuation_general(stress, full_x, full_y, full_z, lam0, mu0):
    real, imag = spectrum(stress)
    freq_x, freq_y, freq_z, zero = wave_numbers(real.shape, full_x, full_y, full_z)
    upd_real = green(real, freq_x, freq_y, freq_z, zero, lam0, mu0)
    upd_imag = green(imag, freq_x, freq_y, freq_z, zero, lam0, mu0)
    packed = (upd_real[0::2] - upd_imag[1::2], upd_imag[0::2] + upd_real[1::2])
    back_real, back_imag = recover(packed)
    return jnp.stack([back_real, back_imag], axis=1).reshape(stress.shape)


MESH = pl.DeviceIdType.MESH
LANES = 128
ROWS = 8


def kernel_fits(shape):
    count_x, count_y = lax.axis_size("gx"), lax.axis_size("gy")
    size_x, size_y, full_z = shape
    return (
        full_z == 2 * count_x * count_y
        and count_x == ROWS
        and count_y * size_y == LANES
        and size_x * size_y == 2 * LANES
        and (count_x * count_y) % 16 == 0
    )


def split(value):
    high = value.astype(jnp.bfloat16)
    return high, (value - high.astype(jnp.float32)).astype(jnp.bfloat16)


def split_table(table):
    high = np.asarray(table, np.float32).astype(jnp.bfloat16)
    low = (np.asarray(table, np.float64) - high.astype(np.float64)).astype(jnp.bfloat16)
    return high, low


def table_left(table):
    high, low = split_table(table)
    return np.concatenate([high, high, low], axis=1)


def table_right(table):
    high, low = split_table(table)
    return np.stack([high, low])


def left_product(table, value):
    high, low = split(value)
    stacked = jnp.concatenate([high, low, high], axis=0)
    return jnp.dot(table, stacked, preferred_element_type=jnp.float32)


def right_product(value, table):
    high, low = split(value)
    product = functools.partial(jnp.dot, preferred_element_type=jnp.float32)
    return product(high, table[0]) + (product(low, table[0]) + product(high, table[1]))


def kernel_tables(size_x, full_x, full_y, full_z):
    forward, inverse = z_tables(full_z)
    forward = forward.transpose(1, 0, 2).reshape(full_z, full_z)
    inverse = inverse.transpose(2, 1, 0).reshape(full_z, full_z)
    count_x = full_x // size_x
    order = np.arange(full_x).reshape(count_x, size_x).T.reshape(-1)
    to_x = complex_table(full_x, False).transpose(0, 1, 2, 3)
    forward_x = to_x.transpose(0, 1, 2, 3)[:, :, :, order]
    inverse_x = complex_table(full_x, True)[:, order]
    forward_y = complex_table(full_y, False)
    inverse_y = complex_table(full_y, True)
    flat = lambda table, length: table.reshape(2 * length, 2 * length)
    return (
        table_left(forward),
        table_left(flat(forward_x, full_x)),
        table_right(flat(forward_y, full_y).T),
        table_right(flat(inverse_y, full_y).T),
        table_left(flat(inverse_x, full_x)),
        table_left(inverse),
    )


def position():
    return lax.axis_index("gx") * lax.axis_size("gy") + lax.axis_index("gy")


def coordinates(index):
    count_y = lax.axis_size("gy")
    return (index // count_y, index % count_y)


def greet():
    count = lax.axis_size("gx") * lax.axis_size("gy")
    me = position()
    barrier = pltpu.get_barrier_semaphore()

    def hello(step, carry):
        other = lax.rem(me + step, count)
        pl.semaphore_signal(barrier, inc=1, device_id=coordinates(other), device_id_type=MESH)
        return carry

    lax.fori_loop(1, count, hello, 0)
    pl.semaphore_wait(barrier, count - 1)


def exchange_copy(sent, received, send_sem, recv_sem, source, target):
    rows = sent.shape[0] // (lax.axis_size("gx") * lax.axis_size("gy"))
    return pltpu.make_async_remote_copy(
        src_ref=sent.at[pl.ds(pl.multiple_of(target * rows, 8), rows)],
        dst_ref=received.at[pl.ds(pl.multiple_of(source * rows, 8), rows)],
        send_sem=send_sem.at[target],
        recv_sem=recv_sem.at[source],
        device_id=coordinates(target),
        device_id_type=MESH,
    )


def exchange_start(sent, received, send_sem, recv_sem):
    count = lax.axis_size("gx") * lax.axis_size("gy")
    me = position()
    rows = sent.shape[0] // count

    def send(step, carry):
        target = lax.rem(me + step, count)
        exchange_copy(sent, received, send_sem, recv_sem, me, target).start()
        return carry

    lax.fori_loop(1, count, send, 0)
    own = pl.ds(pl.multiple_of(me * rows, 8), rows)
    received[own, :] = sent[own, :]


def exchange_wait(sent, received, send_sem, recv_sem, arrived):
    count = lax.axis_size("gx") * lax.axis_size("gy")
    me = position()

    def wait(step, carry):
        other = lax.rem(me + step, count)
        if arrived:
            exchange_copy(sent, received, send_sem, recv_sem, other, other).wait_recv()
        else:
            exchange_copy(sent, received, send_sem, recv_sem, me, other).wait_send()
        return carry

    lax.fori_loop(1, count, wait, 0)


def swap_blocks(parts):
    count = len(parts)
    width = LANES // count
    block = lax.broadcasted_iota(jnp.int32, parts[0].shape, 1) // width
    result = []
    for a in range(count):
        total = None
        for b, part in enumerate(parts):
            shift = (width * (b - a)) % LANES
            moved = pltpu.roll(part, shift, 1) if shift else part
            total = moved if total is None else jnp.where(block == b, moved, total)
        result.append(total)
    return result


def halves(z_ref, t_ref, sent):
    slots = z_ref.shape[0] // 2
    rows = 4 * 6
    for c in range(6):
        result = left_product(z_ref[...], t_ref[c])
        for r in range(2):
            for h in range(2):
                piece = result[r * slots:(r + 1) * slots, h * LANES:(h + 1) * LANES]
                sent[pl.ds(c * 4 + r * 2 + h, slots, stride=rows), :] = piece


def plane_rows(received, c, r, count_y):
    rows = 4 * 6
    result = []
    for h in range(2):
        first = c * 4 + r * 2 + h
        parts = [
            received[pl.ds(j * rows + first, ROWS, stride=rows * count_y), :]
            for j in range(count_y)
        ]
        result += swap_blocks(parts)
    return jnp.concatenate(result, axis=0)


def plane_store(sent, value, c, r, count_y):
    rows = 4 * 6
    for h in range(2):
        first = c * 4 + r * 2 + h
        parts = [
            value[(h * count_y + a) * ROWS:(h * count_y + a + 1) * ROWS] for a in range(count_y)
        ]
        for j, part in enumerate(swap_blocks(parts)):
            sent[pl.ds(j * rows + first, ROWS, stride=rows * count_y), :] = part


def plane_green(received, sent, fx_ref, fy_ref, iy_ref, ix_ref, coefs, full_x, full_y, full_z):
    count_y = lax.axis_size("gy")
    rows_x = []
    for c in range(6):
        both = [plane_rows(received, c, r, count_y) for r in range(2)]
        rows_x.append(jnp.concatenate(both, axis=0))
    spec = left_product(fx_ref[...], jnp.concatenate(rows_x, axis=1))
    lanes = []
    for c in range(6):
        part = spec[:, c * full_y:(c + 1) * full_y]
        lanes.append(jnp.concatenate([part[:full_x], part[full_x:]], axis=1))
    spec = right_product(jnp.concatenate(lanes, axis=0), fy_ref)
    first, second, freq_x, freq_y, freq_z = coefs
    tau = [spec[c * full_x:(c + 1) * full_x] for c in range(6)]
    vec_x = tau[0] * freq_x + tau[5] * freq_y + tau[4] * freq_z
    vec_y = tau[5] * freq_x + tau[1] * freq_y + tau[3] * freq_z
    vec_z = tau[4] * freq_x + tau[3] * freq_y + tau[2] * freq_z
    inner = (freq_x * vec_x + freq_y * vec_y + freq_z * vec_z) * second
    pairs = (
        (freq_x, vec_x, freq_x, vec_x),
        (freq_y, vec_y, freq_y, vec_y),
        (freq_z, vec_z, freq_z, vec_z),
        (freq_y, vec_y, freq_z, vec_z),
        (freq_x, vec_x, freq_z, vec_z),
        (freq_x, vec_x, freq_y, vec_y),
    )
    spec = [(fk * vh + fh * vk) * first - fk * fh * inner for fk, vk, fh, vh in pairs]
    spec = right_product(jnp.concatenate(spec, axis=0), iy_ref)
    lanes = []
    for c in range(6):
        part = spec[c * full_x:(c + 1) * full_x]
        lanes.append(jnp.concatenate([part[:, :full_y], part[:, full_y:]], axis=0))
    plane = left_product(ix_ref[...], jnp.concatenate(lanes, axis=1))
    for c in range(6):
        for r in range(2):
            value = plane[r * full_x:(r + 1) * full_x, c * full_y:(c + 1) * full_y]
            plane_store(sent, value, c, r, count_y)


def wave_parts(lame_ref, full_x, full_y, full_z):
    shape = (full_x, 2 * full_y)
    row = lax.broadcasted_iota(jnp.int32, shape, 0)
    lane = lax.broadcasted_iota(jnp.int32, shape, 1) % full_y

    def weight(index, length):
        signed = jnp.where(index >= length // 2, index - length, index)
        signed = jnp.where(signed == -(length // 2), 0, signed)
        return signed.astype(jnp.float32) * (1.0 / length)

    freq_x = weight(row, full_x)
    freq_y = weight(lane, full_y)
    freq_z = weight(jnp.full(shape, position(), jnp.int32), full_z)
    square = freq_x * freq_x + freq_y * freq_y + freq_z * freq_z
    square = jnp.where(square == 0.0, 1.0, square)

    def middle(which):
        values = [jnp.full(shape, lame_ref[which, a], jnp.float32) for a in range(4)]
        top = functools.reduce(jnp.maximum, values)
        return 0.5 * (top + functools.reduce(jnp.minimum, values))

    lam0, mu0 = middle(0), middle(1)
    first = 1.0 / (2.0 * mu0 * square)
    second = (lam0 + mu0) / (mu0 * (lam0 + 2.0 * mu0)) / (square * square)
    return first, second, freq_x, freq_y, freq_z


def elastic_chunk(at, strain_ref, field_ref):
    elastic = [strain_ref[p, at, :] - field_ref[2 + p, at, :] for p in range(6)]
    lam, shear2 = field_ref[0, at, :], 2.0 * field_ref[1, at, :]
    trace = elastic[0] + elastic[1] + elastic[2]
    stress = [shear2 * e for e in elastic]
    stress = [stress[p] + lam * trace if p < 3 else stress[p] for p in range(6)]
    return elastic, trace, stress


def elastic_kernel(
    full_x, full_y, phase_ref, lame_ref, eigen_ref, mz_ref, fx_ref, fy_ref, iy_ref, ix_ref, wz_ref,
    stress_ref, stored_ref, field_ref, strain_ref, t_ref, *buffers
):
    full_z = phase_ref.shape[1]
    exchanges = 2 * ITERS
    sent, received = buffers[:exchanges], buffers[exchanges:2 * exchanges]
    send_sems, recv_sems = buffers[2 * exchanges:3 * exchanges], buffers[3 * exchanges:]
    greet()
    chunks = full_z // ROWS

    def fields(step, carry):
        at = pl.ds(pl.multiple_of(step * ROWS, ROWS), ROWS)
        phase = [phase_ref[a, at, :] for a in range(4)]
        for which in range(2):
            field_ref[which, at, :] = sum(phase[a] * lame_ref[which, a] for a in range(4))
        for p in range(6):
            field_ref[2 + p, at, :] = sum(phase[a] * eigen_ref[a, p] for a in range(4))
            strain_ref[p, at, :] = jnp.zeros_like(phase[0])
        return carry

    lax.fori_loop(0, chunks, fields, 0)
    coefs = wave_parts(lame_ref, full_x, full_y, full_z)
    for turn in range(ITERS):
        there, back = 2 * turn, 2 * turn + 1

        def stresses(step, carry):
            at = pl.ds(pl.multiple_of(step * ROWS, ROWS), ROWS)
            _, _, stress = elastic_chunk(at, strain_ref, field_ref)
            for p in range(6):
                t_ref[p, at, :] = stress[p]
            return carry

        lax.fori_loop(0, chunks, stresses, 0)
        halves(mz_ref, t_ref, sent[there])
        exchange_start(sent[there], received[there], send_sems[there], recv_sems[there])
        exchange_wait(sent[there], received[there], send_sems[there], recv_sems[there], True)
        plane_green(
            received[there], sent[back], fx_ref, fy_ref, iy_ref, ix_ref, coefs,
            full_x, full_y, full_z,
        )
        exchange_start(sent[back], received[back], send_sems[back], recv_sems[back])
        exchange_wait(sent[back], received[back], send_sems[back], recv_sems[back], True)
        slots = full_z // 2
        for c in range(6):
            value = jnp.concatenate([
                jnp.concatenate([
                    received[back][pl.ds(c * 4 + r * 2 + h, slots, stride=24), :] for h in range(2)
                ], axis=1) for r in range(2)
            ], axis=0)
            strain_ref[c] = strain_ref[c] - left_product(wz_ref[...], value)

    def finish(step, carry):
        at = pl.ds(pl.multiple_of(step * ROWS, ROWS), ROWS)
        elastic, trace, stress = elastic_chunk(at, strain_ref, field_ref)
        for p in range(6):
            stress_ref[p, at, :] = stress[p]
        squares = sum(e * e for e in elastic[:3]) + 2.0 * sum(e * e for e in elastic[3:])
        for a in range(4):
            coupling = sum(
                stress[p] * (eigen_ref[a, p] * (1.0 if p < 3 else 2.0)) for p in range(6)
            )
            stored = 0.5 * lame_ref[0, a] * trace * trace + lame_ref[1, a] * squares
            stored_ref[a, at, :] = stored - coupling
        return carry

    lax.fori_loop(0, chunks, finish, 0)
    for t in range(exchanges):
        exchange_wait(sent[t], received[t], send_sems[t], recv_sems[t], False)


def elastic_call(phase, lame, eigen, full_x, full_y):
    _, size_x, size_y, full_z = phase.shape
    cells = size_x * size_y
    count = full_z // 2
    tables = [jnp.asarray(t) for t in kernel_tables(size_x, full_x, full_y, full_z)]
    spread = phase.reshape(4, cells, full_z).transpose(0, 2, 1)
    vmem = pl.BlockSpec(memory_space=pltpu.VMEM)
    smem = pl.BlockSpec(memory_space=pltpu.SMEM)
    exchanges = 2 * ITERS
    big = pltpu.VMEM((count * 24, LANES), jnp.float32)
    stress, stored = pl.pallas_call(
        functools.partial(elastic_kernel, full_x, full_y),
        out_shape=(
            jax.ShapeDtypeStruct((6, full_z, cells), jnp.float32),
            jax.ShapeDtypeStruct((4, full_z, cells), jnp.float32),
        ),
        in_specs=[vmem, smem, smem] + [vmem] * 6,
        out_specs=(vmem, vmem),
        scratch_shapes=[
            pltpu.VMEM((8, full_z, cells), jnp.float32),
            pltpu.VMEM((6, full_z, cells), jnp.float32),
            pltpu.VMEM((6, full_z, cells), jnp.float32),
        ]
        + [big] * (2 * exchanges)
        + [pltpu.SemaphoreType.DMA((count,))] * (2 * exchanges),
        compiler_params=pltpu.CompilerParams(
            collective_id=0, has_side_effects=True, vmem_limit_bytes=40 * 1024 * 1024
        ),
    )(spread, lame, eigen, *tables)
    place = lambda x: x.transpose(0, 2, 1).reshape((-1, size_x, size_y, full_z))
    return place(stress), place(stored)


def laplace_padded(padded):
    centre = padded[:, 1:-1, 1:-1, :]
    total = -6.0 * centre
    total = total + padded[:, 2:, 1:-1, :] + padded[:, :-2, 1:-1, :]
    total = total + padded[:, 1:-1, 2:, :] + padded[:, 1:-1, :-2, :]
    total = total + jnp.roll(centre, 1, 3) + jnp.roll(centre, -1, 3)
    return total


def shards(labels, seed_noise, conc, curvature, quartic, wells, lame, eigen):
    phase = phases_from(labels, seed_noise)
    part, chem = partition(phase, conc, curvature, quartic, wells)
    stacked = jnp.concatenate([phase, chem[None]], axis=0)
    padded = with_halo(stacked, (("gx", 1), ("gy", 2)), 1)
    lam_field = jnp.sum(phase * column(lame[0]), axis=0)
    shear_field = jnp.sum(phase * column(lame[1]), axis=0)
    eigen_field = jnp.einsum("ap,axyz->pxyz", eigen, phase, precision=lax.Precision.HIGHEST)
    lam0 = 0.5 * (jnp.max(lame[0]) + jnp.min(lame[0]))
    mu0 = 0.5 * (jnp.max(lame[1]) + jnp.min(lame[1]))
    full_x = labels.shape[0] * lax.axis_size("gx")
    full_y = labels.shape[1] * lax.axis_size("gy")
    full_z = labels.shape[2]
    if kernel_fits(labels.shape):
        stress, stored = elastic_call(phase, lame, eigen, full_x, full_y)
    else:
        strain = jnp.zeros((6,) + labels.shape, jnp.float32)
        step = fluctuation if slots_fit(full_z) else fluctuation_general
        for _ in range(ITERS):
            stress = stress_of(strain, eigen_field, lam_field, shear_field)
            strain = strain - step(stress, full_x, full_y, full_z, lam0, mu0)
        stress = stress_of(strain, eigen_field, lam_field, shear_field)
        elastic = strain - eigen_field
        trace = elastic[0] + elastic[1] + elastic[2]
        squares = (
            elastic[0] ** 2
            + elastic[1] ** 2
            + elastic[2] ** 2
            + 2.0 * (elastic[3] ** 2 + elastic[4] ** 2 + elastic[5] ** 2)
        )
        weight = jnp.array([1.0, 1.0, 1.0, 2.0, 2.0, 2.0], jnp.float32)
        coupling = jnp.einsum(
            "ap,pxyz->axyz", eigen * weight[None], stress, precision=lax.Precision.HIGHEST
        )
        stored = (
            0.5 * (column(lame[0]) * trace[None] ** 2 + 2.0 * column(lame[1]) * squares[None])
            - coupling
        )
    deviate = part - column(wells)
    energy = 0.5 * column(curvature) * deviate**2 + 0.25 * column(quartic) * deviate**4
    chemical = energy - chem[None] * part
    total_sq = jnp.sum(phase * phase, axis=0)
    barrier = 2.0 * phase * (total_sq[None] - phase * phase)
    laplacian = laplace_padded(padded)
    force = chemical + stored + barrier - laplacian[:4]
    phase_next = phase - step_phase * (force - jnp.mean(force, axis=0, keepdims=True))
    conc_next = conc + step_conc * laplacian[4]
    return (phase_next, conc_next, stress)


def solution(mesh):
    in_specs = (
        P("gx", "gy", None),
        P(None, "gx", "gy", None),
        P("gx", "gy", None),
        P(),
        P(),
        P(),
        P(),
        P(),
    )
    out_specs = (P(None, "gx", "gy", None), P("gx", "gy", None), P(None, "gx", "gy", None))
    return jax.shard_map(shards, mesh=mesh, in_specs=in_specs, out_specs=out_specs, check_vma=False)
```

```python
import functools
import math

import jax
import jax.numpy as jnp
import numpy as np
from jax import lax
from jax.experimental import pallas as pl
from jax.experimental.pallas import tpu as pltpu
from jax.sharding import PartitionSpec as P

NEWTON = 5
ITERS = 2


step_phase = 0.06
step_conc = 0.005


def with_halo(x, sides, width):
    for axis, dim in sides:
        count, length = (lax.axis_size(axis), x.shape[dim])
        up = [(i, (i + 1) % count) for i in range(count)]
        down = [(j, i) for i, j in up]
        last = lax.slice_in_dim(x, length - width, length, axis=dim)
        initial = lax.slice_in_dim(x, 0, width, axis=dim)
        before = lax.ppermute(last, axis, up)
        after = lax.ppermute(initial, axis, down)
        x = jnp.concatenate([before, x, after], axis=dim)
    return x


def column(values):
    return values.reshape(4, 1, 1, 1)


def phases_from(labels, seed_noise):
    marks = lax.broadcasted_iota(jnp.int32, (4, 1, 1, 1), 0)
    raw = seed_noise + 2.0 * (labels[None] == marks).astype(seed_noise.dtype)
    return raw / jnp.sum(raw, axis=0, keepdims=True)


def partition(phase, conc, curvature, quartic, wells):
    coef_a = column(curvature)
    coef_b = column(quartic)
    centre = column(wells)
    part = jnp.broadcast_to(conc[None], phase.shape)
    deviate = part - centre
    chem = jnp.sum(phase * (coef_a * deviate + coef_b * deviate**3), axis=0)
    for _ in range(NEWTON):
        deviate = part - centre
        slope = coef_a * deviate + coef_b * deviate**3 - chem[None]
        stiff = coef_a + 3.0 * coef_b * deviate * deviate
        shift = (
            conc - jnp.sum(phase * part, axis=0) + jnp.sum(phase * slope / stiff, axis=0)
        ) / jnp.sum(phase / stiff, axis=0)
        part = part + (shift[None] - slope) / stiff
        chem = chem + shift
    return (part, chem)


def stress_of(strain, eigen_field, lam_field, shear_field):
    elastic = strain - eigen_field
    trace = elastic[0] + elastic[1] + elastic[2]
    normal = (lax.broadcasted_iota(jnp.int32, (6, 1, 1, 1), 0) < 3).astype(strain.dtype)
    return 2.0 * shear_field[None] * elastic + (lam_field * trace)[None] * normal


def green(tau, freq_x, freq_y, freq_z, zero, lam0, mu0):
    vec_x = tau[0] * freq_x + tau[5] * freq_y + tau[4] * freq_z
    vec_y = tau[5] * freq_x + tau[1] * freq_y + tau[3] * freq_z
    vec_z = tau[4] * freq_x + tau[3] * freq_y + tau[2] * freq_z
    inner = freq_x * vec_x + freq_y * vec_y + freq_z * vec_z
    square = freq_x * freq_x + freq_y * freq_y + freq_z * freq_z + zero
    first = 1.0 / (2.0 * mu0 * square)
    second = (lam0 + mu0) / (mu0 * (lam0 + 2.0 * mu0)) * inner / (square * square)
    pairs = (
        (freq_x, vec_x, freq_x, vec_x),
        (freq_y, vec_y, freq_y, vec_y),
        (freq_z, vec_z, freq_z, vec_z),
        (freq_y, vec_y, freq_z, vec_z),
        (freq_x, vec_x, freq_z, vec_z),
        (freq_x, vec_x, freq_y, vec_y),
    )
    result = [(fk * vh + fh * vk) * first - fk * fh * second for fk, vk, fh, vh in pairs]
    return jnp.stack(result, axis=0)


def tables(length):
    grid = lax.broadcasted_iota(jnp.int32, (length, length), 0) * lax.broadcasted_iota(
        jnp.int32, (length, length), 1
    )
    angle = (grid % length).astype(jnp.float32) * (2.0 * math.pi / length)
    return (jnp.cos(angle), jnp.sin(angle))


def apply_table(table, data, axis):
    if axis == 3:
        flat = data.reshape(-1, data.shape[3])
        result = jnp.dot(
            flat, table.T, precision=lax.Precision.HIGHEST, preferred_element_type=jnp.float32
        )
        return result.reshape(data.shape[:3] + (table.shape[0],))
    moved = jnp.moveaxis(data, axis, 0)
    rest = moved.shape[1:]
    flat = moved.reshape(moved.shape[0], -1)
    result = jnp.dot(
        table, flat, precision=lax.Precision.HIGHEST, preferred_element_type=jnp.float32
    )
    return jnp.moveaxis(result.reshape((table.shape[0],) + rest), 0, axis)


def transform(pair, axis, inverse):
    real, imag = pair
    length = real.shape[axis]
    cosine, sine = tables(length)
    if inverse:
        new_real = (apply_table(cosine, real, axis) - apply_table(sine, imag, axis)) / length
        new_imag = (apply_table(cosine, imag, axis) + apply_table(sine, real, axis)) / length
    else:
        new_real = apply_table(cosine, real, axis) + apply_table(sine, imag, axis)
        new_imag = apply_table(cosine, imag, axis) - apply_table(sine, real, axis)
    return (new_real, new_imag)


def spectrum(stress):
    length = stress.shape[3]
    cosine, sine = tables(length)
    real = apply_table(cosine, stress, 3)
    imag = -apply_table(sine, stress, 3)
    real, imag = transform(
        (
            lax.all_to_all(real, "gy", split_axis=3, concat_axis=2, tiled=True),
            lax.all_to_all(imag, "gy", split_axis=3, concat_axis=2, tiled=True),
        ),
        axis=2,
        inverse=False,
    )
    real, imag = transform(
        (
            lax.all_to_all(real, "gx", split_axis=2, concat_axis=1, tiled=True),
            lax.all_to_all(imag, "gx", split_axis=2, concat_axis=1, tiled=True),
        ),
        axis=1,
        inverse=False,
    )
    return (real, imag)


def recover(pair):
    pair = transform(pair, 1, True)
    pair = transform(
        (
            lax.all_to_all(pair[0], "gx", split_axis=1, concat_axis=2, tiled=True),
            lax.all_to_all(pair[1], "gx", split_axis=1, concat_axis=2, tiled=True),
        ),
        axis=2,
        inverse=True,
    )
    result = transform(
        (
            lax.all_to_all(pair[0], "gy", split_axis=2, concat_axis=3, tiled=True),
            lax.all_to_all(pair[1], "gy", split_axis=2, concat_axis=3, tiled=True),
        ),
        axis=3,
        inverse=True,
    )
    return result


def frequencies(count, offset, length, axis):
    index = lax.iota(jnp.int32, count) + offset
    index = jnp.where(index >= length // 2, index - length, index)
    kept = jnp.where(index == -(length // 2), 0, index)
    dims_shape = [1, 1, 1]
    dims_shape[axis] = count
    return (kept.astype(jnp.float32) / length).reshape(dims_shape)


def wave_numbers(dims, full_x, full_y, full_z):
    offsets = (jnp.int32(0), lax.axis_index("gx") * dims[2], lax.axis_index("gy") * dims[3])
    freq_x = frequencies(dims[1], offsets[0], full_x, 0)
    freq_y = frequencies(dims[2], offsets[1], full_y, 1)
    freq_z = frequencies(dims[3], offsets[2], full_z, 2)
    zero = ((freq_x == 0.0) & (freq_y == 0.0) & (freq_z == 0.0)).astype(jnp.float32)
    return (freq_x, freq_y, freq_z, zero)


def slots_fit(full_z):
    count = lax.axis_size("gx") * lax.axis_size("gy")
    return full_z % 2 == 0 and (full_z // 2) % count == 0


def angles(length):
    grid = np.outer(np.arange(length), np.arange(length)) % length
    return grid * (2.0 * math.pi / length)


def z_tables(length):
    half = length // 2
    angle = angles(length)[:half]
    real = np.cos(angle)
    imag = -np.sin(angle)
    imag[0] = np.cos(math.pi * np.arange(length))
    forward = np.stack([real, imag], axis=1).astype(np.float32)
    weight = np.full((half, 1, 1), 2.0 / length)
    weight[0] = 1.0 / length
    return forward, (np.stack([real, imag], axis=1) * weight).astype(np.float32)


def complex_table(length, inverse):
    angle = angles(length)
    cosine, sine = np.cos(angle), np.sin(angle)
    if inverse:
        table = np.array([[cosine, -sine], [sine, cosine]]) / length
    else:
        table = np.array([[cosine, sine], [-sine, cosine]])
    return table.transpose(0, 2, 1, 3).astype(np.float32)


def contract(spec, *operands):
    return jnp.einsum(
        spec, *operands, precision=lax.Precision.HIGH, preferred_element_type=jnp.float32
    )


def fluctuation(stress, full_x, full_y, full_z, lam0, mu0):
    count_x, count_y = lax.axis_size("gx"), lax.axis_size("gy")
    count = count_x * count_y
    _, size_x, size_y, _ = stress.shape
    slots = full_z // 2 // count
    forward_z, inverse_z = z_tables(full_z)
    data = contract("krz,cxyz->krcxy", forward_z, stress)
    data = lax.all_to_all(data, ("gx", "gy"), split_axis=0, concat_axis=0, tiled=True)
    data = data.reshape(count_x, count_y, slots, 2, 6, size_x, size_y)
    data = data.transpose(2, 3, 4, 0, 5, 1, 6).reshape(slots, 2, 6, full_x, full_y)
    data = contract("sLrl,krcly->kscLy", complex_table(full_x, False), data)
    data = contract("sLrl,krcxl->kscxL", complex_table(full_y, False), data)
    data = data.transpose(2, 1, 3, 4, 0)
    freq_x = frequencies(full_x, 0, full_x, 0)
    freq_y = frequencies(full_y, 0, full_y, 1)
    position = lax.axis_index("gx") * count_y + lax.axis_index("gy")
    freq_z = frequencies(slots, position * slots, full_z, 2)
    zero = ((freq_x == 0.0) & (freq_y == 0.0) & (freq_z == 0.0)).astype(jnp.float32)
    data = jnp.stack([green(data[:, r], freq_x, freq_y, freq_z, zero, lam0, mu0) for r in (0, 1)], 1)
    data = data.transpose(4, 1, 0, 2, 3)
    data = contract("sLrl,krcxl->kscxL", complex_table(full_y, True), data)
    data = contract("sLrl,krcly->kscLy", complex_table(full_x, True), data)
    data = data.reshape(slots, 2, 6, count_x, size_x, count_y, size_y)
    data = data.transpose(3, 5, 0, 1, 2, 4, 6).reshape(count * slots, 2, 6, size_x, size_y)
    data = lax.all_to_all(data, ("gx", "gy"), split_axis=0, concat_axis=0, tiled=True)
    return contract("krz,krcxy->cxyz", inverse_z, data)


def fluctuation_general(stress, full_x, full_y, full_z, lam0, mu0):
    real, imag = spectrum(stress)
    freq_x, freq_y, freq_z, zero = wave_numbers(real.shape, full_x, full_y, full_z)
    upd_real = green(real, freq_x, freq_y, freq_z, zero, lam0, mu0)
    upd_imag = green(imag, freq_x, freq_y, freq_z, zero, lam0, mu0)
    packed = (upd_real[0::2] - upd_imag[1::2], upd_imag[0::2] + upd_real[1::2])
    back_real, back_imag = recover(packed)
    return jnp.stack([back_real, back_imag], axis=1).reshape(stress.shape)


MESH = pl.DeviceIdType.MESH
LANES = 128
ROWS = 8


def kernel_fits(shape):
    count_x, count_y = lax.axis_size("gx"), lax.axis_size("gy")
    size_x, size_y, full_z = shape
    return (
        full_z == 2 * count_x * count_y
        and count_x == ROWS
        and count_y * size_y == LANES
        and size_x * size_y == 2 * LANES
        and (count_x * count_y) % 16 == 0
    )


def split(value):
    high = value.astype(jnp.bfloat16)
    return high, (value - high.astype(jnp.float32)).astype(jnp.bfloat16)


def split_table(table):
    high = np.asarray(table, np.float32).astype(jnp.bfloat16)
    low = (np.asarray(table, np.float64) - high.astype(np.float64)).astype(jnp.bfloat16)
    return high, low


def table_left(table):
    high, low = split_table(table)
    return np.concatenate([high, high, low], axis=1)


def table_right(table):
    high, low = split_table(table)
    return np.stack([high, low])


def left_product(table, value):
    high, low = split(value)
    stacked = jnp.concatenate([high, low, high], axis=0)
    return jnp.dot(table, stacked, preferred_element_type=jnp.float32)


def right_product(value, table):
    high, low = split(value)
    product = functools.partial(jnp.dot, preferred_element_type=jnp.float32)
    return product(high, table[0]) + (product(low, table[0]) + product(high, table[1]))


def kernel_tables(size_x, full_x, full_y, full_z):
    forward, inverse = z_tables(full_z)
    forward = forward.transpose(1, 0, 2).reshape(full_z, full_z)
    inverse = inverse.transpose(2, 1, 0).reshape(full_z, full_z)
    count_x = full_x // size_x
    order = np.arange(full_x).reshape(count_x, size_x).T.reshape(-1)
    to_x = complex_table(full_x, False).transpose(0, 1, 2, 3)
    forward_x = to_x.transpose(0, 1, 2, 3)[:, :, :, order]
    inverse_x = complex_table(full_x, True)[:, order]
    forward_y = complex_table(full_y, False)
    inverse_y = complex_table(full_y, True)
    flat = lambda table, length: table.reshape(2 * length, 2 * length)
    return (
        table_left(forward),
        table_left(flat(forward_x, full_x)),
        table_right(flat(forward_y, full_y).T),
        table_right(flat(inverse_y, full_y).T),
        table_left(flat(inverse_x, full_x)),
        table_left(inverse),
    )


def position():
    return lax.axis_index("gx") * lax.axis_size("gy") + lax.axis_index("gy")


def coordinates(index):
    count_y = lax.axis_size("gy")
    return (index // count_y, index % count_y)


def greet():
    count = lax.axis_size("gx") * lax.axis_size("gy")
    me = position()
    barrier = pltpu.get_barrier_semaphore()

    def hello(step, carry):
        other = lax.rem(me + step, count)
        pl.semaphore_signal(barrier, inc=1, device_id=coordinates(other), device_id_type=MESH)
        return carry

    lax.fori_loop(1, count, hello, 0)


def greeted():
    count = lax.axis_size("gx") * lax.axis_size("gy")
    pl.semaphore_wait(pltpu.get_barrier_semaphore(), count - 1)


def exchange_copy(pack, source, target):
    sent, received, send_sem, recv_sem = pack
    rows = sent.shape[0] // (lax.axis_size("gx") * lax.axis_size("gy"))
    return pltpu.make_async_remote_copy(
        src_ref=sent.at[pl.ds(pl.multiple_of(target * rows, 8), rows)],
        dst_ref=received.at[pl.ds(pl.multiple_of(source * rows, 8), rows)],
        send_sem=send_sem.at[target],
        recv_sem=recv_sem.at[source],
        device_id=coordinates(target),
        device_id_type=MESH,
    )


def exchange_start(pack):
    sent, received = pack[:2]
    count = lax.axis_size("gx") * lax.axis_size("gy")
    me = position()
    rows = sent.shape[0] // count

    def send(step, carry):
        exchange_copy(pack, me, lax.rem(me + step, count)).start()
        return carry

    lax.fori_loop(1, count, send, 0)
    own = pl.ds(pl.multiple_of(me * rows, 8), rows)
    received[own, :] = sent[own, :]


def exchange_wait(pack, arrived):
    count = lax.axis_size("gx") * lax.axis_size("gy")
    me = position()

    def wait(step, carry):
        other = lax.rem(me + step, count)
        if arrived:
            exchange_copy(pack, other, other).wait_recv()
        else:
            exchange_copy(pack, me, other).wait_send()
        return carry

    lax.fori_loop(1, count, wait, 0)


def swap_blocks(parts):
    count = len(parts)
    width = LANES // count
    block = lax.broadcasted_iota(jnp.int32, parts[0].shape, 1) // width
    result = []
    for a in range(count):
        total = None
        for b, part in enumerate(parts):
            shift = (width * (b - a)) % LANES
            moved = pltpu.roll(part, shift, 1) if shift else part
            total = moved if total is None else jnp.where(block == b, moved, total)
        result.append(total)
    return result


GROUPS = ((0, 4), (4, 6))


def halves(z_ref, t_ref, sent, group):
    slots = z_ref.shape[0] // 2
    rows = 4 * (group[1] - group[0])
    for c in range(*group):
        result = left_product(z_ref[...], t_ref[c])
        for r in range(2):
            for h in range(2):
                piece = result[r * slots:(r + 1) * slots, h * LANES:(h + 1) * LANES]
                first = (c - group[0]) * 4 + r * 2 + h
                sent[pl.ds(first, slots, stride=rows), :] = piece


def plane_rows(received, c, r, count_y, rows):
    result = []
    for h in range(2):
        first = c * 4 + r * 2 + h
        parts = [
            received[pl.ds(j * rows + first, ROWS, stride=rows * count_y), :]
            for j in range(count_y)
        ]
        result += swap_blocks(parts)
    return jnp.concatenate(result, axis=0)


def plane_store(sent, value, c, r, count_y, rows):
    for h in range(2):
        first = c * 4 + r * 2 + h
        parts = [
            value[(h * count_y + a) * ROWS:(h * count_y + a + 1) * ROWS] for a in range(count_y)
        ]
        for j, part in enumerate(swap_blocks(parts)):
            sent[pl.ds(j * rows + first, ROWS, stride=rows * count_y), :] = part


def plane_forward(received, plane_ref, fx_ref, fy_ref, group, full_x, full_y):
    count_y = lax.axis_size("gy")
    number = group[1] - group[0]
    rows_x = []
    for c in range(number):
        both = [plane_rows(received, c, r, count_y, 4 * number) for r in range(2)]
        rows_x.append(jnp.concatenate(both, axis=0))
    spec = left_product(fx_ref[...], jnp.concatenate(rows_x, axis=1))
    lanes = []
    for c in range(number):
        part = spec[:, c * full_y:(c + 1) * full_y]
        lanes.append(jnp.concatenate([part[:full_x], part[full_x:]], axis=1))
    spec = right_product(jnp.concatenate(lanes, axis=0), fy_ref)
    plane_ref[group[0] * full_x:group[1] * full_x, :] = spec


def plane_green(plane_ref, wave_ref, full_x, full_z):
    freq_z = lax.convert_element_type(position(), jnp.float32) * (1.0 / full_z)

    def chunk(step, carry):
        start = pl.multiple_of(step * ROWS, ROWS)
        at = pl.ds(start, ROWS)
        where = [pl.ds(pl.multiple_of(c * full_x + start, ROWS), ROWS) for c in range(6)]
        first, second, freq_x, freq_y = [wave_ref[w, at, :] for w in range(4)]
        tau = [plane_ref[where[c], :] for c in range(6)]
        vec_x = tau[0] * freq_x + tau[5] * freq_y + tau[4] * freq_z
        vec_y = tau[5] * freq_x + tau[1] * freq_y + tau[3] * freq_z
        vec_z = tau[4] * freq_x + tau[3] * freq_y + tau[2] * freq_z
        inner = (freq_x * vec_x + freq_y * vec_y + freq_z * vec_z) * second
        pairs = (
            (freq_x, vec_x, freq_x, vec_x),
            (freq_y, vec_y, freq_y, vec_y),
            (freq_z, vec_z, freq_z, vec_z),
            (freq_y, vec_y, freq_z, vec_z),
            (freq_x, vec_x, freq_z, vec_z),
            (freq_x, vec_x, freq_y, vec_y),
        )
        for c, (fk, vk, fh, vh) in enumerate(pairs):
            plane_ref[where[c], :] = (fk * vh + fh * vk) * first - fk * fh * inner
        return carry

    lax.fori_loop(0, full_x // ROWS, chunk, 0)


def plane_back(plane_ref, sent, iy_ref, ix_ref, group, full_x, full_y):
    count_y = lax.axis_size("gy")
    number = group[1] - group[0]
    spec = right_product(plane_ref[group[0] * full_x:group[1] * full_x, :], iy_ref)
    lanes = []
    for c in range(number):
        part = spec[c * full_x:(c + 1) * full_x]
        lanes.append(jnp.concatenate([part[:, :full_y], part[:, full_y:]], axis=0))
    plane = left_product(ix_ref[...], jnp.concatenate(lanes, axis=1))
    for c in range(number):
        for r in range(2):
            value = plane[r * full_x:(r + 1) * full_x, c * full_y:(c + 1) * full_y]
            plane_store(sent, value, c, r, count_y, 4 * number)


def strain_update(received, wz_ref, strain_ref, group):
    slots = wz_ref.shape[0] // 2
    rows = 4 * (group[1] - group[0])
    for c in range(*group):
        value = jnp.concatenate([
            jnp.concatenate([
                received[pl.ds((c - group[0]) * 4 + r * 2 + h, slots, stride=rows), :]
                for h in range(2)
            ], axis=1) for r in range(2)
        ], axis=0)
        strain_ref[c] = strain_ref[c] - left_product(wz_ref[...], value)


def wave_parts(lame_ref, full_x, full_y, full_z):
    shape = (full_x, 2 * full_y)
    row = lax.broadcasted_iota(jnp.int32, shape, 0)
    lane = lax.broadcasted_iota(jnp.int32, shape, 1) % full_y

    def weight(index, length):
        signed = jnp.where(index >= length // 2, index - length, index)
        signed = jnp.where(signed == -(length // 2), 0, signed)
        return signed.astype(jnp.float32) * (1.0 / length)

    freq_x = weight(row, full_x)
    freq_y = weight(lane, full_y)
    freq_z = weight(jnp.full(shape, position(), jnp.int32), full_z)
    square = freq_x * freq_x + freq_y * freq_y + freq_z * freq_z
    square = jnp.where(square == 0.0, 1.0, square)

    def middle(which):
        values = [jnp.full(shape, lame_ref[which, a], jnp.float32) for a in range(4)]
        top = functools.reduce(jnp.maximum, values)
        return 0.5 * (top + functools.reduce(jnp.minimum, values))

    lam0, mu0 = middle(0), middle(1)
    first = 1.0 / (2.0 * mu0 * square)
    second = (lam0 + mu0) / (mu0 * (lam0 + 2.0 * mu0)) / (square * square)
    return first, second, freq_x, freq_y, freq_z


def elastic_chunk(at, strain_ref, field_ref):
    elastic = [strain_ref[p, at, :] - field_ref[2 + p, at, :] for p in range(6)]
    lam, shear2 = field_ref[0, at, :], 2.0 * field_ref[1, at, :]
    trace = elastic[0] + elastic[1] + elastic[2]
    stress = [shear2 * e for e in elastic]
    stress = [stress[p] + lam * trace if p < 3 else stress[p] for p in range(6)]
    return elastic, trace, stress


def half(h):
    return slice(h * LANES, (h + 1) * LANES)


def turned(value, shift):
    shift = shift % LANES
    return pltpu.roll(value, shift, 1) if shift else value


def lane_block(shape, width):
    return lax.broadcasted_iota(jnp.int32, shape, 1) // width


def lane_place(shape, width):
    return lax.broadcasted_iota(jnp.int32, shape, 1) % width


def halo_pack(phase_ref, chem_ref, x_up, x_down, y_up, y_down, width):
    full_z = phase_ref.shape[1]
    blocks = LANES // width
    fold = full_z // blocks
    block = lane_block((full_z, LANES), width)
    place = lane_place((full_z, LANES), width)
    fields = [phase_ref[f] for f in range(4)] + [chem_ref[...]]
    for face, h, own in ((x_up, 1, blocks - 1), (x_down, 0, 0)):
        total = turned(fields[0][:, half(h)], -width * own)
        for f in range(1, 4):
            total = jnp.where(block == f, turned(fields[f][:, half(h)], width * (f - own)), total)
        face[:full_z, :] = total
        parts = [fields[4][k * fold:(k + 1) * fold, half(h)] for k in range(blocks)]
        total = turned(parts[0], -width * own)
        for k in range(1, blocks):
            total = jnp.where(block[:fold] == k, turned(parts[k], width * (k - own)), total)
        face[full_z:, :] = total
    for face, own in ((y_up, width - 1), (y_down, 0)):
        total = jnp.zeros((full_z, LANES), jnp.float32)
        for f in range(5):
            for h in range(2):
                slot = 8 * h + f
                total = jnp.where(place == slot, turned(fields[f][:, half(h)], slot - own), total)
        face[...] = total


def halo_laplace(f, field, x_before, x_after, y_before, y_after, width):
    full_z = field.shape[0]
    blocks = LANES // width
    fold = full_z // blocks
    block = lane_block((full_z, LANES), width)
    place = lane_place((full_z, LANES), width)

    def face(ref, own):
        if f < 4:
            return turned(ref[:full_z, :], width * (own - f))
        folded = ref[full_z:, :]
        return jnp.concatenate([turned(folded, width * (own - k)) for k in range(blocks)], axis=0)

    sides = [field[:, half(h)] for h in range(2)]
    right = [turned(side, width) for side in sides]
    left = [turned(side, -width) for side in sides]
    last = blocks - 1
    result = []
    for h in range(2):
        slot = 8 * h + f
        side = sides[h]
        below = jnp.where(block == 0, face(x_before, 0) if h == 0 else right[0], right[h])
        above = jnp.where(block == last, left[1] if h == 0 else face(x_after, last), left[h])
        total = below + above - 6.0 * side
        total += jnp.where(place == 0, turned(y_before[...], -slot), turned(side, 1))
        after = turned(y_after[...], width - 1 - slot)
        total += jnp.where(place == width - 1, after, turned(side, -1))
        total += pltpu.roll(side, 1, 0) + pltpu.roll(side, full_z - 1, 0)
        result.append(total)
    return result


def newton_chunk(phase, conc, scalars):
    curve, quart, wells = scalars
    part = [conc for _ in range(4)]
    dev = [conc - wells[a] for a in range(4)]
    chem = sum(
        phase[a] * (curve[a] * dev[a] + quart[a] * (dev[a] * dev[a] * dev[a])) for a in range(4)
    )
    for _ in range(NEWTON):
        dev = [part[a] - wells[a] for a in range(4)]
        square = [d * d for d in dev]
        slope = [dev[a] * (curve[a] + quart[a] * square[a]) - chem for a in range(4)]
        soft = [1.0 / (curve[a] + (3.0 * quart[a]) * square[a]) for a in range(4)]
        weight = [phase[a] * soft[a] for a in range(4)]
        top = conc - sum(phase[a] * part[a] for a in range(4))
        top = top + sum(weight[a] * slope[a] for a in range(4))
        shift = top / sum(weight)
        part = [part[a] + (shift - slope[a]) * soft[a] for a in range(4)]
        chem = chem + shift
    dev = [part[a] - wells[a] for a in range(4)]
    square = [d * d for d in dev]
    total = sum(p * p for p in phase)
    local = []
    for a in range(4):
        energy = square[a] * (0.5 * curve[a] + (0.25 * quart[a]) * square[a])
        barrier = 2.0 * phase[a] * (total - phase[a] * phase[a])
        local.append(energy - chem * part[a] + barrier)
    return chem, local


def step_kernel(
    full_x, full_y, labels_ref, noise_ref, raw_conc_ref, curve_ref, quart_ref, wells_ref, lame_ref,
    eigen_ref, mz_ref, fx_ref, fy_ref, iy_ref, ix_ref, wz_ref,
    next_ref, conc_next_ref, stress_ref,
    phase_ref, conc_ref, chem_ref, local_ref, field_ref, strain_ref, t_ref, plane_ref, wave_ref,
    *buffers
):
    full_z = phase_ref.shape[1]
    chunks = full_z // ROWS
    width = full_y // lax.axis_size("gy")
    number = 2 * ITERS * len(GROUPS)
    packs = [buffers[4 * n:4 * n + 4] for n in range(number)]
    packs = [packs[n:n + len(GROUPS)] for n in range(0, number, len(GROUPS))]
    halo_sent, halo_got = buffers[4 * number:4 * number + 4], buffers[4 * number + 4:4 * number + 8]
    halo_send, halo_recv = buffers[4 * number + 8:]
    greet()

    for h in range(2):
        at = pl.ds(h * LANES, LANES)
        label = labels_ref[at, :]
        raw = [noise_ref[a, at, :] + jnp.where(label == a, 2.0, 0.0) for a in range(4)]
        total = raw[0] + raw[1] + raw[2] + raw[3]
        for a in range(4):
            phase_ref[a, :, half(h)] = (raw[a] / total).T
        conc_ref[:, half(h)] = raw_conc_ref[at, :].T

    def rows_at(step):
        return pl.ds(pl.multiple_of(step * ROWS, ROWS), ROWS)

    def fields(step, carry):
        at = rows_at(step)
        phase = [phase_ref[a, at, :] for a in range(4)]
        for which in range(2):
            field_ref[which, at, :] = sum(phase[a] * lame_ref[which, a] for a in range(4))
        for p in range(6):
            field_ref[2 + p, at, :] = sum(phase[a] * eigen_ref[a, p] for a in range(4))
            strain_ref[p, at, :] = jnp.zeros_like(phase[0])
        _, _, stress = elastic_chunk(at, strain_ref, field_ref)
        for p in range(6):
            t_ref[p, at, :] = stress[p]
        return carry

    def stresses(step, carry):
        at = rows_at(step)
        _, _, stress = elastic_chunk(at, strain_ref, field_ref)
        for p in range(6):
            t_ref[p, at, :] = stress[p]
        return carry

    def newton(step, carry):
        at = rows_at(step)
        phase = [phase_ref[a, at, :] for a in range(4)]
        scalars = [[ref[a] for a in range(4)] for ref in (curve_ref, quart_ref, wells_ref)]
        chem, local = newton_chunk(phase, conc_ref[at, :], scalars)
        chem_ref[at, :] = chem
        for a in range(4):
            local_ref[a, at, :] = local[a]
        return carry

    def halo_copies():
        i, j = lax.axis_index("gx"), lax.axis_index("gy")
        count_x, count_y = lax.axis_size("gx"), lax.axis_size("gy")
        targets = (
            (lax.rem(i + 1, count_x), j),
            (lax.rem(i + count_x - 1, count_x), j),
            (i, lax.rem(j + 1, count_y)),
            (i, lax.rem(j + count_y - 1, count_y)),
        )
        return [
            pltpu.make_async_remote_copy(
                src_ref=halo_sent[n],
                dst_ref=halo_got[n],
                send_sem=halo_send.at[n],
                recv_sem=halo_recv.at[n],
                device_id=target,
                device_id_type=MESH,
            )
            for n, target in enumerate(targets)
        ]

    def beside_first():
        for w, value in enumerate(wave_parts(lame_ref, full_x, full_y, full_z)[:4]):
            wave_ref[w] = value
        lax.fori_loop(0, chunks, newton, 0)
        halo_pack(phase_ref, chem_ref, *halo_sent, width)
        for copy in halo_copies():
            copy.start()

    def beside_second():
        for copy in halo_copies():
            copy.wait_recv()
        for f in range(5):
            field = phase_ref[f] if f < 4 else chem_ref[...]
            spread = halo_laplace(f, field, *halo_got, width)
            for h in range(2):
                if f < 4:
                    local_ref[f, :, half(h)] = local_ref[f, :, half(h)] - spread[h]
                else:
                    conc_next_ref[:, half(h)] = conc_ref[:, half(h)] + step_conc * spread[h]

    for turn in range(ITERS):
        there, back = packs[2 * turn], packs[2 * turn + 1]
        lax.fori_loop(0, chunks, stresses if turn else fields, 0)
        for pack, group in zip(there, GROUPS):
            halves(mz_ref, t_ref, pack[0], group)
            if turn == 0 and group is GROUPS[0]:
                greeted()
            exchange_start(pack)
        if turn == 0:
            beside_first()
        for pack, group in zip(there, GROUPS):
            exchange_wait(pack, True)
            plane_forward(pack[1], plane_ref, fx_ref, fy_ref, group, full_x, full_y)
        plane_green(plane_ref, wave_ref, full_x, full_z)
        for pack, group in zip(back, GROUPS):
            plane_back(plane_ref, pack[0], iy_ref, ix_ref, group, full_x, full_y)
            exchange_start(pack)
        if turn == 0:
            beside_second()
        for pack, group in zip(back, GROUPS):
            exchange_wait(pack, True)
            strain_update(pack[1], wz_ref, strain_ref, group)

    def finish(step, carry):
        at = rows_at(step)
        elastic, trace, stress = elastic_chunk(at, strain_ref, field_ref)
        for p in range(6):
            stress_ref[p, at, :] = stress[p]
        squares = sum(e * e for e in elastic[:3]) + 2.0 * sum(e * e for e in elastic[3:])
        force = []
        for a in range(4):
            coupling = sum(
                stress[p] * (eigen_ref[a, p] * (1.0 if p < 3 else 2.0)) for p in range(6)
            )
            stored = 0.5 * lame_ref[0, a] * trace * trace + lame_ref[1, a] * squares
            force.append(local_ref[a, at, :] + (stored - coupling))
        mean = 0.25 * (force[0] + force[1] + force[2] + force[3])
        for a in range(4):
            next_ref[a, at, :] = phase_ref[a, at, :] - step_phase * (force[a] - mean)
        return carry

    lax.fori_loop(0, chunks, finish, 0)
    for group_packs in packs:
        for pack in group_packs:
            exchange_wait(pack, False)
    for copy in halo_copies():
        copy.wait_send()


def step_call(labels, seed_noise, conc, curvature, quartic, wells, lame, eigen, full_x, full_y):
    size_x, size_y, full_z = labels.shape
    cells = size_x * size_y
    count = full_z // 2
    tables = [jnp.asarray(t) for t in kernel_tables(size_x, full_x, full_y, full_z)]
    vmem = pl.BlockSpec(memory_space=pltpu.VMEM)
    smem = pl.BlockSpec(memory_space=pltpu.SMEM)
    scratch = lambda *shape: pltpu.VMEM(shape, jnp.float32)
    buffers = []
    for _ in range(2 * ITERS):
        for group in GROUPS:
            rows = 4 * (group[1] - group[0]) * count
            buffers += [scratch(rows, LANES), scratch(rows, LANES)]
            buffers += [pltpu.SemaphoreType.DMA((count,))] * 2
    x_face = scratch(full_z + full_z * size_y // LANES, LANES)
    y_face = scratch(full_z, LANES)
    buffers += [x_face, x_face, y_face, y_face] * 2 + [pltpu.SemaphoreType.DMA((4,))] * 2
    whole = lambda *lead: jax.ShapeDtypeStruct(lead + (full_z, cells), jnp.float32)
    result = pl.pallas_call(
        functools.partial(step_kernel, full_x, full_y),
        out_shape=(whole(4), whole(), whole(6)),
        in_specs=[vmem] * 3 + [smem] * 5 + [vmem] * 6,
        out_specs=(vmem, vmem, vmem),
        scratch_shapes=[
            scratch(4, full_z, cells),
            scratch(full_z, cells),
            scratch(full_z, cells),
            scratch(4, full_z, cells),
            scratch(8, full_z, cells),
            scratch(6, full_z, cells),
            scratch(6, full_z, cells),
            scratch(6 * full_x, 2 * full_y),
            scratch(4, full_x, 2 * full_y),
        ]
        + buffers,
        compiler_params=pltpu.CompilerParams(
            collective_id=0, has_side_effects=True, vmem_limit_bytes=40 * 1024 * 1024
        ),
    )(
        labels.reshape(cells, full_z), seed_noise.reshape(4, cells, full_z),
        conc.reshape(cells, full_z), curvature, quartic, wells, lame, eigen, *tables
    )
    place = lambda x: jnp.swapaxes(x, -1, -2).reshape(x.shape[:-2] + (size_x, size_y, full_z))
    return tuple(place(x) for x in result)


def laplace_padded(padded):
    centre = padded[:, 1:-1, 1:-1, :]
    total = -6.0 * centre
    total = total + padded[:, 2:, 1:-1, :] + padded[:, :-2, 1:-1, :]
    total = total + padded[:, 1:-1, 2:, :] + padded[:, 1:-1, :-2, :]
    total = total + jnp.roll(centre, 1, 3) + jnp.roll(centre, -1, 3)
    return total


def shards(labels, seed_noise, conc, curvature, quartic, wells, lame, eigen):
    full_x = labels.shape[0] * lax.axis_size("gx")
    full_y = labels.shape[1] * lax.axis_size("gy")
    full_z = labels.shape[2]
    if kernel_fits(labels.shape):
        return step_call(
            labels, seed_noise, conc, curvature, quartic, wells, lame, eigen, full_x, full_y
        )
    phase = phases_from(labels, seed_noise)
    part, chem = partition(phase, conc, curvature, quartic, wells)
    stacked = jnp.concatenate([phase, chem[None]], axis=0)
    padded = with_halo(stacked, (("gx", 1), ("gy", 2)), 1)
    lam_field = jnp.sum(phase * column(lame[0]), axis=0)
    shear_field = jnp.sum(phase * column(lame[1]), axis=0)
    eigen_field = jnp.einsum("ap,axyz->pxyz", eigen, phase, precision=lax.Precision.HIGHEST)
    lam0 = 0.5 * (jnp.max(lame[0]) + jnp.min(lame[0]))
    mu0 = 0.5 * (jnp.max(lame[1]) + jnp.min(lame[1]))
    strain = jnp.zeros((6,) + labels.shape, jnp.float32)
    step = fluctuation if slots_fit(full_z) else fluctuation_general
    for _ in range(ITERS):
        stress = stress_of(strain, eigen_field, lam_field, shear_field)
        strain = strain - step(stress, full_x, full_y, full_z, lam0, mu0)
    stress = stress_of(strain, eigen_field, lam_field, shear_field)
    elastic = strain - eigen_field
    trace = elastic[0] + elastic[1] + elastic[2]
    squares = (
        elastic[0] ** 2
        + elastic[1] ** 2
        + elastic[2] ** 2
        + 2.0 * (elastic[3] ** 2 + elastic[4] ** 2 + elastic[5] ** 2)
    )
    weight = jnp.array([1.0, 1.0, 1.0, 2.0, 2.0, 2.0], jnp.float32)
    coupling = jnp.einsum(
        "ap,pxyz->axyz", eigen * weight[None], stress, precision=lax.Precision.HIGHEST
    )
    stored = (
        0.5 * (column(lame[0]) * trace[None] ** 2 + 2.0 * column(lame[1]) * squares[None])
        - coupling
    )
    deviate = part - column(wells)
    energy = 0.5 * column(curvature) * deviate**2 + 0.25 * column(quartic) * deviate**4
    chemical = energy - chem[None] * part
    total_sq = jnp.sum(phase * phase, axis=0)
    barrier = 2.0 * phase * (total_sq[None] - phase * phase)
    laplacian = laplace_padded(padded)
    force = chemical + stored + barrier - laplacian[:4]
    phase_next = phase - step_phase * (force - jnp.mean(force, axis=0, keepdims=True))
    conc_next = conc + step_conc * laplacian[4]
    return (phase_next, conc_next, stress)


def solution(mesh):
    in_specs = (
        P("gx", "gy", None),
        P(None, "gx", "gy", None),
        P("gx", "gy", None),
        P(),
        P(),
        P(),
        P(),
        P(),
    )
    out_specs = (P(None, "gx", "gy", None), P("gx", "gy", None), P(None, "gx", "gy", None))
    return jax.shard_map(shards, mesh=mesh, in_specs=in_specs, out_specs=out_specs, check_vma=False)
```

```python
import functools
import math

import jax
import jax.numpy as jnp
import numpy as np
from jax import lax
from jax.experimental import pallas as pl
from jax.experimental.pallas import tpu as pltpu
from jax.sharding import PartitionSpec as P

NEWTON = 5
ITERS = 2


step_phase = 0.06
step_conc = 0.005


def with_halo(x, sides, width):
    for axis, dim in sides:
        count, length = (lax.axis_size(axis), x.shape[dim])
        up = [(i, (i + 1) % count) for i in range(count)]
        down = [(j, i) for i, j in up]
        last = lax.slice_in_dim(x, length - width, length, axis=dim)
        initial = lax.slice_in_dim(x, 0, width, axis=dim)
        before = lax.ppermute(last, axis, up)
        after = lax.ppermute(initial, axis, down)
        x = jnp.concatenate([before, x, after], axis=dim)
    return x


def column(values):
    return values.reshape(4, 1, 1, 1)


def phases_from(labels, seed_noise):
    marks = lax.broadcasted_iota(jnp.int32, (4, 1, 1, 1), 0)
    raw = seed_noise + 2.0 * (labels[None] == marks).astype(seed_noise.dtype)
    return raw / jnp.sum(raw, axis=0, keepdims=True)


def partition(phase, conc, curvature, quartic, wells):
    coef_a = column(curvature)
    coef_b = column(quartic)
    centre = column(wells)
    part = jnp.broadcast_to(conc[None], phase.shape)
    deviate = part - centre
    chem = jnp.sum(phase * (coef_a * deviate + coef_b * deviate**3), axis=0)
    for _ in range(NEWTON):
        deviate = part - centre
        slope = coef_a * deviate + coef_b * deviate**3 - chem[None]
        stiff = coef_a + 3.0 * coef_b * deviate * deviate
        shift = (
            conc - jnp.sum(phase * part, axis=0) + jnp.sum(phase * slope / stiff, axis=0)
        ) / jnp.sum(phase / stiff, axis=0)
        part = part + (shift[None] - slope) / stiff
        chem = chem + shift
    return (part, chem)


def stress_of(strain, eigen_field, lam_field, shear_field):
    elastic = strain - eigen_field
    trace = elastic[0] + elastic[1] + elastic[2]
    normal = (lax.broadcasted_iota(jnp.int32, (6, 1, 1, 1), 0) < 3).astype(strain.dtype)
    return 2.0 * shear_field[None] * elastic + (lam_field * trace)[None] * normal


def green(tau, freq_x, freq_y, freq_z, zero, lam0, mu0):
    vec_x = tau[0] * freq_x + tau[5] * freq_y + tau[4] * freq_z
    vec_y = tau[5] * freq_x + tau[1] * freq_y + tau[3] * freq_z
    vec_z = tau[4] * freq_x + tau[3] * freq_y + tau[2] * freq_z
    inner = freq_x * vec_x + freq_y * vec_y + freq_z * vec_z
    square = freq_x * freq_x + freq_y * freq_y + freq_z * freq_z + zero
    first = 1.0 / (2.0 * mu0 * square)
    second = (lam0 + mu0) / (mu0 * (lam0 + 2.0 * mu0)) * inner / (square * square)
    pairs = (
        (freq_x, vec_x, freq_x, vec_x),
        (freq_y, vec_y, freq_y, vec_y),
        (freq_z, vec_z, freq_z, vec_z),
        (freq_y, vec_y, freq_z, vec_z),
        (freq_x, vec_x, freq_z, vec_z),
        (freq_x, vec_x, freq_y, vec_y),
    )
    result = [(fk * vh + fh * vk) * first - fk * fh * second for fk, vk, fh, vh in pairs]
    return jnp.stack(result, axis=0)


def tables(length):
    grid = lax.broadcasted_iota(jnp.int32, (length, length), 0) * lax.broadcasted_iota(
        jnp.int32, (length, length), 1
    )
    angle = (grid % length).astype(jnp.float32) * (2.0 * math.pi / length)
    return (jnp.cos(angle), jnp.sin(angle))


def apply_table(table, data, axis):
    if axis == 3:
        flat = data.reshape(-1, data.shape[3])
        result = jnp.dot(
            flat, table.T, precision=lax.Precision.HIGHEST, preferred_element_type=jnp.float32
        )
        return result.reshape(data.shape[:3] + (table.shape[0],))
    moved = jnp.moveaxis(data, axis, 0)
    rest = moved.shape[1:]
    flat = moved.reshape(moved.shape[0], -1)
    result = jnp.dot(
        table, flat, precision=lax.Precision.HIGHEST, preferred_element_type=jnp.float32
    )
    return jnp.moveaxis(result.reshape((table.shape[0],) + rest), 0, axis)


def transform(pair, axis, inverse):
    real, imag = pair
    length = real.shape[axis]
    cosine, sine = tables(length)
    if inverse:
        new_real = (apply_table(cosine, real, axis) - apply_table(sine, imag, axis)) / length
        new_imag = (apply_table(cosine, imag, axis) + apply_table(sine, real, axis)) / length
    else:
        new_real = apply_table(cosine, real, axis) + apply_table(sine, imag, axis)
        new_imag = apply_table(cosine, imag, axis) - apply_table(sine, real, axis)
    return (new_real, new_imag)


def spectrum(stress):
    length = stress.shape[3]
    cosine, sine = tables(length)
    real = apply_table(cosine, stress, 3)
    imag = -apply_table(sine, stress, 3)
    real, imag = transform(
        (
            lax.all_to_all(real, "gy", split_axis=3, concat_axis=2, tiled=True),
            lax.all_to_all(imag, "gy", split_axis=3, concat_axis=2, tiled=True),
        ),
        axis=2,
        inverse=False,
    )
    real, imag = transform(
        (
            lax.all_to_all(real, "gx", split_axis=2, concat_axis=1, tiled=True),
            lax.all_to_all(imag, "gx", split_axis=2, concat_axis=1, tiled=True),
        ),
        axis=1,
        inverse=False,
    )
    return (real, imag)


def recover(pair):
    pair = transform(pair, 1, True)
    pair = transform(
        (
            lax.all_to_all(pair[0], "gx", split_axis=1, concat_axis=2, tiled=True),
            lax.all_to_all(pair[1], "gx", split_axis=1, concat_axis=2, tiled=True),
        ),
        axis=2,
        inverse=True,
    )
    result = transform(
        (
            lax.all_to_all(pair[0], "gy", split_axis=2, concat_axis=3, tiled=True),
            lax.all_to_all(pair[1], "gy", split_axis=2, concat_axis=3, tiled=True),
        ),
        axis=3,
        inverse=True,
    )
    return result


def frequencies(count, offset, length, axis):
    index = lax.iota(jnp.int32, count) + offset
    index = jnp.where(index >= length // 2, index - length, index)
    kept = jnp.where(index == -(length // 2), 0, index)
    dims_shape = [1, 1, 1]
    dims_shape[axis] = count
    return (kept.astype(jnp.float32) / length).reshape(dims_shape)


def wave_numbers(dims, full_x, full_y, full_z):
    offsets = (jnp.int32(0), lax.axis_index("gx") * dims[2], lax.axis_index("gy") * dims[3])
    freq_x = frequencies(dims[1], offsets[0], full_x, 0)
    freq_y = frequencies(dims[2], offsets[1], full_y, 1)
    freq_z = frequencies(dims[3], offsets[2], full_z, 2)
    zero = ((freq_x == 0.0) & (freq_y == 0.0) & (freq_z == 0.0)).astype(jnp.float32)
    return (freq_x, freq_y, freq_z, zero)


def slots_fit(full_z):
    count = lax.axis_size("gx") * lax.axis_size("gy")
    return full_z % 2 == 0 and (full_z // 2) % count == 0


def angles(length):
    grid = np.outer(np.arange(length), np.arange(length)) % length
    return grid * (2.0 * math.pi / length)


def z_tables(length):
    half = length // 2
    angle = angles(length)[:half]
    real = np.cos(angle)
    imag = -np.sin(angle)
    imag[0] = np.cos(math.pi * np.arange(length))
    forward = np.stack([real, imag], axis=1).astype(np.float32)
    weight = np.full((half, 1, 1), 2.0 / length)
    weight[0] = 1.0 / length
    return forward, (np.stack([real, imag], axis=1) * weight).astype(np.float32)


def complex_table(length, inverse):
    angle = angles(length)
    cosine, sine = np.cos(angle), np.sin(angle)
    if inverse:
        table = np.array([[cosine, -sine], [sine, cosine]]) / length
    else:
        table = np.array([[cosine, sine], [-sine, cosine]])
    return table.transpose(0, 2, 1, 3).astype(np.float32)


def contract(spec, *operands):
    return jnp.einsum(
        spec, *operands, precision=lax.Precision.HIGH, preferred_element_type=jnp.float32
    )


def fluctuation(stress, full_x, full_y, full_z, lam0, mu0):
    count_x, count_y = lax.axis_size("gx"), lax.axis_size("gy")
    count = count_x * count_y
    _, size_x, size_y, _ = stress.shape
    slots = full_z // 2 // count
    forward_z, inverse_z = z_tables(full_z)
    data = contract("krz,cxyz->krcxy", forward_z, stress)
    data = lax.all_to_all(data, ("gx", "gy"), split_axis=0, concat_axis=0, tiled=True)
    data = data.reshape(count_x, count_y, slots, 2, 6, size_x, size_y)
    data = data.transpose(2, 3, 4, 0, 5, 1, 6).reshape(slots, 2, 6, full_x, full_y)
    data = contract("sLrl,krcly->kscLy", complex_table(full_x, False), data)
    data = contract("sLrl,krcxl->kscxL", complex_table(full_y, False), data)
    data = data.transpose(2, 1, 3, 4, 0)
    freq_x = frequencies(full_x, 0, full_x, 0)
    freq_y = frequencies(full_y, 0, full_y, 1)
    position = lax.axis_index("gx") * count_y + lax.axis_index("gy")
    freq_z = frequencies(slots, position * slots, full_z, 2)
    zero = ((freq_x == 0.0) & (freq_y == 0.0) & (freq_z == 0.0)).astype(jnp.float32)
    data = jnp.stack([green(data[:, r], freq_x, freq_y, freq_z, zero, lam0, mu0) for r in (0, 1)], 1)
    data = data.transpose(4, 1, 0, 2, 3)
    data = contract("sLrl,krcxl->kscxL", complex_table(full_y, True), data)
    data = contract("sLrl,krcly->kscLy", complex_table(full_x, True), data)
    data = data.reshape(slots, 2, 6, count_x, size_x, count_y, size_y)
    data = data.transpose(3, 5, 0, 1, 2, 4, 6).reshape(count * slots, 2, 6, size_x, size_y)
    data = lax.all_to_all(data, ("gx", "gy"), split_axis=0, concat_axis=0, tiled=True)
    return contract("krz,krcxy->cxyz", inverse_z, data)


def fluctuation_general(stress, full_x, full_y, full_z, lam0, mu0):
    real, imag = spectrum(stress)
    freq_x, freq_y, freq_z, zero = wave_numbers(real.shape, full_x, full_y, full_z)
    upd_real = green(real, freq_x, freq_y, freq_z, zero, lam0, mu0)
    upd_imag = green(imag, freq_x, freq_y, freq_z, zero, lam0, mu0)
    packed = (upd_real[0::2] - upd_imag[1::2], upd_imag[0::2] + upd_real[1::2])
    back_real, back_imag = recover(packed)
    return jnp.stack([back_real, back_imag], axis=1).reshape(stress.shape)


MESH = pl.DeviceIdType.MESH
LANES = 128
ROWS = 8


def kernel_fits(shape):
    count_x, count_y = lax.axis_size("gx"), lax.axis_size("gy")
    size_x, size_y, full_z = shape
    return (
        full_z == 2 * count_x * count_y
        and count_x == ROWS
        and count_y * size_y == LANES
        and size_x * size_y == 2 * LANES
        and (count_x * count_y) % 16 == 0
    )


def split(value):
    high = value.astype(jnp.bfloat16)
    return high, (value - high.astype(jnp.float32)).astype(jnp.bfloat16)


def split_table(table):
    high = np.asarray(table, np.float32).astype(jnp.bfloat16)
    low = (np.asarray(table, np.float64) - high.astype(np.float64)).astype(jnp.bfloat16)
    return high, low


def table_left(table):
    high, low = split_table(table)
    return np.concatenate([high, high, low], axis=1)


def table_right(table):
    high, low = split_table(table)
    return np.stack([high, low])


def left_product(table, value):
    high, low = split(value)
    stacked = jnp.concatenate([high, low, high], axis=0)
    return jnp.dot(table, stacked, preferred_element_type=jnp.float32)


def right_product(value, table):
    high, low = split(value)
    product = functools.partial(jnp.dot, preferred_element_type=jnp.float32)
    return product(high, table[0]) + (product(low, table[0]) + product(high, table[1]))


def kernel_tables(size_x, full_x, full_y, full_z):
    forward, inverse = z_tables(full_z)
    forward = forward.transpose(1, 0, 2).reshape(full_z, full_z)
    inverse = inverse.transpose(2, 1, 0).reshape(full_z, full_z)
    count_x = full_x // size_x
    order = np.arange(full_x).reshape(count_x, size_x).T.reshape(-1)
    to_x = complex_table(full_x, False).transpose(0, 1, 2, 3)
    forward_x = to_x.transpose(0, 1, 2, 3)[:, :, :, order]
    inverse_x = complex_table(full_x, True)[:, order]
    forward_y = complex_table(full_y, False)
    inverse_y = complex_table(full_y, True)
    flat = lambda table, length: table.reshape(2 * length, 2 * length)
    return (
        table_left(forward),
        table_left(flat(forward_x, full_x)),
        table_right(flat(forward_y, full_y).T),
        table_right(flat(inverse_y, full_y).T),
        table_left(flat(inverse_x, full_x)),
        table_left(inverse),
    )


def position():
    return lax.axis_index("gx") * lax.axis_size("gy") + lax.axis_index("gy")


def for_others(action):
    count_x, count_y = lax.axis_size("gx"), lax.axis_size("gy")
    i, j = lax.axis_index("gx"), lax.axis_index("gy")
    turns = [j] + [lax.rem(j + step, count_y) for step in range(1, count_y)]
    for other in turns[1:]:
        action(i, other)

    def row(step, carry):
        far = lax.rem(i + step, count_x)
        for other in turns:
            action(far, other)
        return carry

    lax.fori_loop(1, count_x, row, 0)


def greet():
    barrier = pltpu.get_barrier_semaphore()
    for_others(
        lambda i, j: pl.semaphore_signal(barrier, inc=1, device_id=(i, j), device_id_type=MESH)
    )


def greeted():
    count = lax.axis_size("gx") * lax.axis_size("gy")
    pl.semaphore_wait(pltpu.get_barrier_semaphore(), count - 1)


def exchange_start(pack):
    sent, received, send_sem, recv_sem = pack
    count_y = lax.axis_size("gy")
    rows = sent.shape[0] // (lax.axis_size("gx") * count_y)
    own = pl.ds(pl.multiple_of(position() * rows, 8), rows)

    def send(i, j):
        pltpu.make_async_remote_copy(
            src_ref=sent.at[pl.ds(pl.multiple_of((i * count_y + j) * rows, 8), rows)],
            dst_ref=received.at[own],
            send_sem=send_sem,
            recv_sem=recv_sem,
            device_id=(i, j),
            device_id_type=MESH,
        ).start()

    for_others(send)
    received[own, :] = sent[own, :]


def exchange_all(pack):
    sent, received, send_sem, recv_sem = pack
    count_x, count_y = lax.axis_size("gx"), lax.axis_size("gy")
    rows = sent.shape[0] // (count_x * count_y) * (count_x * count_y - 1)
    return pltpu.make_async_remote_copy(
        src_ref=sent.at[pl.ds(0, rows)],
        dst_ref=received.at[pl.ds(0, rows)],
        send_sem=send_sem,
        recv_sem=recv_sem,
        device_id=(lax.rem(lax.axis_index("gx") + 1, count_x), lax.axis_index("gy")),
        device_id_type=MESH,
    )


def exchange_wait(pack, arrived):
    if arrived:
        exchange_all(pack).wait_recv()
    else:
        exchange_all(pack).wait_send()


def swap_blocks(parts):
    count = len(parts)
    width = LANES // count
    block = lax.broadcasted_iota(jnp.int32, parts[0].shape, 1) // width
    result = []
    for a in range(count):
        total = None
        for b, part in enumerate(parts):
            shift = (width * (b - a)) % LANES
            moved = pltpu.roll(part, shift, 1) if shift else part
            total = moved if total is None else jnp.where(block == b, moved, total)
        result.append(total)
    return result


GROUPS = ((0, 4), (4, 6))


def halves(z_ref, t_ref, sent, group):
    slots = z_ref.shape[0] // 2
    rows = 4 * (group[1] - group[0])
    for c in range(*group):
        result = left_product(z_ref[...], t_ref[c])
        for r in range(2):
            for h in range(2):
                piece = result[r * slots:(r + 1) * slots, h * LANES:(h + 1) * LANES]
                first = (c - group[0]) * 4 + r * 2 + h
                sent[pl.ds(first, slots, stride=rows), :] = piece


def plane_rows(received, c, r, count_y, rows):
    result = []
    for h in range(2):
        first = c * 4 + r * 2 + h
        parts = [
            received[pl.ds(j * rows + first, ROWS, stride=rows * count_y), :]
            for j in range(count_y)
        ]
        result += swap_blocks(parts)
    return jnp.concatenate(result, axis=0)


def plane_store(sent, value, c, r, count_y, rows):
    for h in range(2):
        first = c * 4 + r * 2 + h
        parts = [
            value[(h * count_y + a) * ROWS:(h * count_y + a + 1) * ROWS] for a in range(count_y)
        ]
        for j, part in enumerate(swap_blocks(parts)):
            sent[pl.ds(j * rows + first, ROWS, stride=rows * count_y), :] = part


def plane_forward(received, plane_ref, fx_ref, fy_ref, group, full_x, full_y):
    count_y = lax.axis_size("gy")
    number = group[1] - group[0]
    rows_x = []
    for c in range(number):
        both = [plane_rows(received, c, r, count_y, 4 * number) for r in range(2)]
        rows_x.append(jnp.concatenate(both, axis=0))
    spec = left_product(fx_ref[...], jnp.concatenate(rows_x, axis=1))
    lanes = []
    for c in range(number):
        part = spec[:, c * full_y:(c + 1) * full_y]
        lanes.append(jnp.concatenate([part[:full_x], part[full_x:]], axis=1))
    spec = right_product(jnp.concatenate(lanes, axis=0), fy_ref)
    plane_ref[group[0] * full_x:group[1] * full_x, :] = spec


def plane_green(plane_ref, wave_ref, full_x, full_z):
    freq_z = lax.convert_element_type(position(), jnp.float32) * (1.0 / full_z)

    def chunk(step, carry):
        start = pl.multiple_of(step * ROWS, ROWS)
        at = pl.ds(start, ROWS)
        where = [pl.ds(pl.multiple_of(c * full_x + start, ROWS), ROWS) for c in range(6)]
        first, second, freq_x, freq_y = [wave_ref[w, at, :] for w in range(4)]
        tau = [plane_ref[where[c], :] for c in range(6)]
        vec_x = tau[0] * freq_x + tau[5] * freq_y + tau[4] * freq_z
        vec_y = tau[5] * freq_x + tau[1] * freq_y + tau[3] * freq_z
        vec_z = tau[4] * freq_x + tau[3] * freq_y + tau[2] * freq_z
        inner = (freq_x * vec_x + freq_y * vec_y + freq_z * vec_z) * second
        pairs = (
            (freq_x, vec_x, freq_x, vec_x),
            (freq_y, vec_y, freq_y, vec_y),
            (freq_z, vec_z, freq_z, vec_z),
            (freq_y, vec_y, freq_z, vec_z),
            (freq_x, vec_x, freq_z, vec_z),
            (freq_x, vec_x, freq_y, vec_y),
        )
        for c, (fk, vk, fh, vh) in enumerate(pairs):
            plane_ref[where[c], :] = (fk * vh + fh * vk) * first - fk * fh * inner
        return carry

    lax.fori_loop(0, full_x // ROWS, chunk, 0)


def plane_back(plane_ref, sent, iy_ref, ix_ref, group, full_x, full_y):
    count_y = lax.axis_size("gy")
    number = group[1] - group[0]
    spec = right_product(plane_ref[group[0] * full_x:group[1] * full_x, :], iy_ref)
    lanes = []
    for c in range(number):
        part = spec[c * full_x:(c + 1) * full_x]
        lanes.append(jnp.concatenate([part[:, :full_y], part[:, full_y:]], axis=0))
    plane = left_product(ix_ref[...], jnp.concatenate(lanes, axis=1))
    for c in range(number):
        for r in range(2):
            value = plane[r * full_x:(r + 1) * full_x, c * full_y:(c + 1) * full_y]
            plane_store(sent, value, c, r, count_y, 4 * number)


def strain_update(received, wz_ref, strain_ref, group):
    slots = wz_ref.shape[0] // 2
    rows = 4 * (group[1] - group[0])
    for c in range(*group):
        value = jnp.concatenate([
            jnp.concatenate([
                received[pl.ds((c - group[0]) * 4 + r * 2 + h, slots, stride=rows), :]
                for h in range(2)
            ], axis=1) for r in range(2)
        ], axis=0)
        strain_ref[c] = strain_ref[c] - left_product(wz_ref[...], value)


def wave_parts(lame_ref, full_x, full_y, full_z):
    shape = (full_x, 2 * full_y)
    row = lax.broadcasted_iota(jnp.int32, shape, 0)
    lane = lax.broadcasted_iota(jnp.int32, shape, 1) % full_y

    def weight(index, length):
        signed = jnp.where(index >= length // 2, index - length, index)
        signed = jnp.where(signed == -(length // 2), 0, signed)
        return signed.astype(jnp.float32) * (1.0 / length)

    freq_x = weight(row, full_x)
    freq_y = weight(lane, full_y)
    freq_z = weight(jnp.full(shape, position(), jnp.int32), full_z)
    square = freq_x * freq_x + freq_y * freq_y + freq_z * freq_z
    square = jnp.where(square == 0.0, 1.0, square)

    def middle(which):
        values = [jnp.full(shape, lame_ref[which, a], jnp.float32) for a in range(4)]
        top = functools.reduce(jnp.maximum, values)
        return 0.5 * (top + functools.reduce(jnp.minimum, values))

    lam0, mu0 = middle(0), middle(1)
    first = 1.0 / (2.0 * mu0 * square)
    second = (lam0 + mu0) / (mu0 * (lam0 + 2.0 * mu0)) / (square * square)
    return first, second, freq_x, freq_y, freq_z


def elastic_chunk(at, strain_ref, field_ref):
    elastic = [strain_ref[p, at, :] - field_ref[2 + p, at, :] for p in range(6)]
    lam, shear2 = field_ref[0, at, :], 2.0 * field_ref[1, at, :]
    trace = elastic[0] + elastic[1] + elastic[2]
    stress = [shear2 * e for e in elastic]
    stress = [stress[p] + lam * trace if p < 3 else stress[p] for p in range(6)]
    return elastic, trace, stress


def half(h):
    return slice(h * LANES, (h + 1) * LANES)


def turned(value, shift):
    shift = shift % LANES
    return pltpu.roll(value, shift, 1) if shift else value


def lane_block(shape, width):
    return lax.broadcasted_iota(jnp.int32, shape, 1) // width


def lane_place(shape, width):
    return lax.broadcasted_iota(jnp.int32, shape, 1) % width


def halo_pack(phase_ref, chem_ref, x_up, x_down, y_up, y_down, width):
    full_z = phase_ref.shape[1]
    blocks = LANES // width
    fold = full_z // blocks
    block = lane_block((full_z, LANES), width)
    place = lane_place((full_z, LANES), width)
    fields = [phase_ref[f] for f in range(4)] + [chem_ref[...]]
    for face, h, own in ((x_up, 1, blocks - 1), (x_down, 0, 0)):
        total = turned(fields[0][:, half(h)], -width * own)
        for f in range(1, 4):
            total = jnp.where(block == f, turned(fields[f][:, half(h)], width * (f - own)), total)
        face[:full_z, :] = total
        parts = [fields[4][k * fold:(k + 1) * fold, half(h)] for k in range(blocks)]
        total = turned(parts[0], -width * own)
        for k in range(1, blocks):
            total = jnp.where(block[:fold] == k, turned(parts[k], width * (k - own)), total)
        face[full_z:, :] = total
    for face, own in ((y_up, width - 1), (y_down, 0)):
        total = jnp.zeros((full_z, LANES), jnp.float32)
        for f in range(5):
            for h in range(2):
                slot = 8 * h + f
                total = jnp.where(place == slot, turned(fields[f][:, half(h)], slot - own), total)
        face[...] = total


def halo_laplace(f, field, x_before, x_after, y_before, y_after, width):
    full_z = field.shape[0]
    blocks = LANES // width
    fold = full_z // blocks
    block = lane_block((full_z, LANES), width)
    place = lane_place((full_z, LANES), width)

    def face(ref, own):
        if f < 4:
            return turned(ref[:full_z, :], width * (own - f))
        folded = ref[full_z:, :]
        return jnp.concatenate([turned(folded, width * (own - k)) for k in range(blocks)], axis=0)

    sides = [field[:, half(h)] for h in range(2)]
    right = [turned(side, width) for side in sides]
    left = [turned(side, -width) for side in sides]
    last = blocks - 1
    result = []
    for h in range(2):
        slot = 8 * h + f
        side = sides[h]
        below = jnp.where(block == 0, face(x_before, 0) if h == 0 else right[0], right[h])
        above = jnp.where(block == last, left[1] if h == 0 else face(x_after, last), left[h])
        total = below + above - 6.0 * side
        total += jnp.where(place == 0, turned(y_before[...], -slot), turned(side, 1))
        after = turned(y_after[...], width - 1 - slot)
        total += jnp.where(place == width - 1, after, turned(side, -1))
        total += pltpu.roll(side, 1, 0) + pltpu.roll(side, full_z - 1, 0)
        result.append(total)
    return result


def newton_chunk(phase, conc, scalars):
    curve, quart, wells = scalars
    part = [conc for _ in range(4)]
    dev = [conc - wells[a] for a in range(4)]
    chem = sum(
        phase[a] * (curve[a] * dev[a] + quart[a] * (dev[a] * dev[a] * dev[a])) for a in range(4)
    )
    for _ in range(NEWTON):
        dev = [part[a] - wells[a] for a in range(4)]
        square = [d * d for d in dev]
        slope = [dev[a] * (curve[a] + quart[a] * square[a]) - chem for a in range(4)]
        soft = [1.0 / (curve[a] + (3.0 * quart[a]) * square[a]) for a in range(4)]
        weight = [phase[a] * soft[a] for a in range(4)]
        top = conc - sum(phase[a] * part[a] for a in range(4))
        top = top + sum(weight[a] * slope[a] for a in range(4))
        shift = top / sum(weight)
        part = [part[a] + (shift - slope[a]) * soft[a] for a in range(4)]
        chem = chem + shift
    dev = [part[a] - wells[a] for a in range(4)]
    square = [d * d for d in dev]
    total = sum(p * p for p in phase)
    local = []
    for a in range(4):
        energy = square[a] * (0.5 * curve[a] + (0.25 * quart[a]) * square[a])
        barrier = 2.0 * phase[a] * (total - phase[a] * phase[a])
        local.append(energy - chem * part[a] + barrier)
    return chem, local


def step_kernel(
    full_x, full_y, labels_in, noise_in, raw_conc_in, curve_ref, quart_ref, wells_ref, lame_ref,
    eigen_ref, mz_in, fx_in, fy_in, iy_in, ix_in, wz_in,
    next_ref, conc_next_ref, stress_ref,
    labels_ref, noise_ref, raw_conc_ref, mz_ref, fx_ref, fy_ref, iy_ref, ix_ref, wz_ref, load_sem,
    phase_ref, conc_ref, chem_ref, local_ref, field_ref, strain_ref, t_ref, plane_ref, wave_ref,
    *buffers
):
    full_z = phase_ref.shape[1]
    chunks = full_z // ROWS
    width = full_y // lax.axis_size("gy")
    number = 2 * ITERS * len(GROUPS)
    packs = [buffers[4 * n:4 * n + 4] for n in range(number)]
    packs = [packs[n:n + len(GROUPS)] for n in range(0, number, len(GROUPS))]
    halo_sent, halo_got = buffers[4 * number:4 * number + 4], buffers[4 * number + 4:4 * number + 8]
    halo_send, halo_recv = buffers[4 * number + 8:]
    loads = [
        pltpu.make_async_copy(source, target, load_sem.at[n])
        for n, (source, target) in enumerate((
            (noise_in, noise_ref), (labels_in, labels_ref), (raw_conc_in, raw_conc_ref),
            (mz_in, mz_ref), (fx_in, fx_ref), (fy_in, fy_ref), (iy_in, iy_ref), (ix_in, ix_ref),
            (wz_in, wz_ref),
        ))
    ]
    for load in loads:
        load.start()
    greet()
    for load in loads[:3]:
        load.wait()

    for h in range(2):
        at = pl.ds(h * LANES, LANES)
        label = labels_ref[at, :]
        raw = [noise_ref[a, at, :] + jnp.where(label == a, 2.0, 0.0) for a in range(4)]
        total = raw[0] + raw[1] + raw[2] + raw[3]
        for a in range(4):
            phase_ref[a, :, half(h)] = (raw[a] / total).T
        conc_ref[:, half(h)] = raw_conc_ref[at, :].T

    def rows_at(step):
        return pl.ds(pl.multiple_of(step * ROWS, ROWS), ROWS)

    def fields(step, carry):
        at = rows_at(step)
        phase = [phase_ref[a, at, :] for a in range(4)]
        for which in range(2):
            field_ref[which, at, :] = sum(phase[a] * lame_ref[which, a] for a in range(4))
        for p in range(6):
            field_ref[2 + p, at, :] = sum(phase[a] * eigen_ref[a, p] for a in range(4))
            strain_ref[p, at, :] = jnp.zeros_like(phase[0])
        _, _, stress = elastic_chunk(at, strain_ref, field_ref)
        for p in range(6):
            t_ref[p, at, :] = stress[p]
        return carry

    def stresses(step, carry):
        at = rows_at(step)
        _, _, stress = elastic_chunk(at, strain_ref, field_ref)
        for p in range(6):
            t_ref[p, at, :] = stress[p]
        return carry

    def newton(step, carry):
        at = rows_at(step)
        phase = [phase_ref[a, at, :] for a in range(4)]
        scalars = [[ref[a] for a in range(4)] for ref in (curve_ref, quart_ref, wells_ref)]
        chem, local = newton_chunk(phase, conc_ref[at, :], scalars)
        chem_ref[at, :] = chem
        for a in range(4):
            local_ref[a, at, :] = local[a]
        return carry

    def halo_copies():
        i, j = lax.axis_index("gx"), lax.axis_index("gy")
        count_x, count_y = lax.axis_size("gx"), lax.axis_size("gy")
        targets = (
            (lax.rem(i + 1, count_x), j),
            (lax.rem(i + count_x - 1, count_x), j),
            (i, lax.rem(j + 1, count_y)),
            (i, lax.rem(j + count_y - 1, count_y)),
        )
        return [
            pltpu.make_async_remote_copy(
                src_ref=halo_sent[n],
                dst_ref=halo_got[n],
                send_sem=halo_send.at[n],
                recv_sem=halo_recv.at[n],
                device_id=target,
                device_id_type=MESH,
            )
            for n, target in enumerate(targets)
        ]

    def beside_first():
        for w, value in enumerate(wave_parts(lame_ref, full_x, full_y, full_z)[:4]):
            wave_ref[w] = value
        lax.fori_loop(0, chunks, newton, 0)
        halo_pack(phase_ref, chem_ref, *halo_sent, width)
        for copy in halo_copies():
            copy.start()
        for load in loads[4:]:
            load.wait()

    def beside_second():
        for copy in halo_copies():
            copy.wait_recv()
        for f in range(5):
            field = phase_ref[f] if f < 4 else chem_ref[...]
            spread = halo_laplace(f, field, *halo_got, width)
            for h in range(2):
                if f < 4:
                    local_ref[f, :, half(h)] = local_ref[f, :, half(h)] - spread[h]
                else:
                    conc_next_ref[:, half(h)] = conc_ref[:, half(h)] + step_conc * spread[h]

    for turn in range(ITERS):
        there, back = packs[2 * turn], packs[2 * turn + 1]
        lax.fori_loop(0, chunks, stresses if turn else fields, 0)
        if turn == 0:
            loads[3].wait()
        for pack, group in zip(there, GROUPS):
            halves(mz_ref, t_ref, pack[0], group)
            if turn == 0 and group is GROUPS[0]:
                greeted()
            exchange_start(pack)
        if turn == 0:
            beside_first()
        for pack, group in zip(there, GROUPS):
            exchange_wait(pack, True)
            plane_forward(pack[1], plane_ref, fx_ref, fy_ref, group, full_x, full_y)
        plane_green(plane_ref, wave_ref, full_x, full_z)
        for pack, group in zip(back, GROUPS):
            plane_back(plane_ref, pack[0], iy_ref, ix_ref, group, full_x, full_y)
            exchange_start(pack)
        if turn == 0:
            beside_second()
        for pack, group in zip(back, GROUPS):
            exchange_wait(pack, True)
            strain_update(pack[1], wz_ref, strain_ref, group)

    def finish(step, carry):
        at = rows_at(step)
        elastic, trace, stress = elastic_chunk(at, strain_ref, field_ref)
        for p in range(6):
            stress_ref[p, at, :] = stress[p]
        squares = sum(e * e for e in elastic[:3]) + 2.0 * sum(e * e for e in elastic[3:])
        force = []
        for a in range(4):
            coupling = sum(
                stress[p] * (eigen_ref[a, p] * (1.0 if p < 3 else 2.0)) for p in range(6)
            )
            stored = 0.5 * lame_ref[0, a] * trace * trace + lame_ref[1, a] * squares
            force.append(local_ref[a, at, :] + (stored - coupling))
        mean = 0.25 * (force[0] + force[1] + force[2] + force[3])
        for a in range(4):
            next_ref[a, at, :] = phase_ref[a, at, :] - step_phase * (force[a] - mean)
        return carry

    lax.fori_loop(0, chunks, finish, 0)
    for group_packs in packs:
        for pack in group_packs:
            exchange_wait(pack, False)
    for copy in halo_copies():
        copy.wait_send()


def step_call(labels, seed_noise, conc, curvature, quartic, wells, lame, eigen, full_x, full_y):
    size_x, size_y, full_z = labels.shape
    cells = size_x * size_y
    count = full_z // 2
    tables = [jnp.asarray(t) for t in kernel_tables(size_x, full_x, full_y, full_z)]
    vmem = pl.BlockSpec(memory_space=pltpu.VMEM)
    smem = pl.BlockSpec(memory_space=pltpu.SMEM)
    hbm = pl.BlockSpec(memory_space=pltpu.HBM)
    scratch = lambda *shape: pltpu.VMEM(shape, jnp.float32)
    buffers = []
    for _ in range(2 * ITERS):
        for group in GROUPS:
            rows = 4 * (group[1] - group[0]) * count
            buffers += [scratch(rows, LANES), scratch(rows, LANES)]
            buffers += [pltpu.SemaphoreType.DMA] * 2
    x_face = scratch(full_z + full_z * size_y // LANES, LANES)
    y_face = scratch(full_z, LANES)
    buffers += [x_face, x_face, y_face, y_face] * 2 + [pltpu.SemaphoreType.DMA((4,))] * 2
    whole = lambda *lead: jax.ShapeDtypeStruct(lead + (full_z, cells), jnp.float32)
    result = pl.pallas_call(
        functools.partial(step_kernel, full_x, full_y),
        out_shape=(whole(4), whole(), whole(6)),
        in_specs=[hbm] * 3 + [smem] * 5 + [hbm] * 6,
        out_specs=(vmem, vmem, vmem),
        scratch_shapes=[pltpu.VMEM((cells, full_z), jnp.int32)]
        + [scratch(4, cells, full_z), scratch(cells, full_z)]
        + [pltpu.VMEM(table.shape, table.dtype) for table in tables]
        + [pltpu.SemaphoreType.DMA((3 + len(tables),))]
        + [
            scratch(4, full_z, cells),
            scratch(full_z, cells),
            scratch(full_z, cells),
            scratch(4, full_z, cells),
            scratch(8, full_z, cells),
            scratch(6, full_z, cells),
            scratch(6, full_z, cells),
            scratch(6 * full_x, 2 * full_y),
            scratch(4, full_x, 2 * full_y),
        ]
        + buffers,
        compiler_params=pltpu.CompilerParams(
            collective_id=0, has_side_effects=True, vmem_limit_bytes=56 * 1024 * 1024
        ),
    )(
        labels.reshape(cells, full_z), seed_noise.reshape(4, cells, full_z),
        conc.reshape(cells, full_z), curvature, quartic, wells, lame, eigen, *tables
    )
    place = lambda x: jnp.swapaxes(x, -1, -2).reshape(x.shape[:-2] + (size_x, size_y, full_z))
    return tuple(place(x) for x in result)


def laplace_padded(padded):
    centre = padded[:, 1:-1, 1:-1, :]
    total = -6.0 * centre
    total = total + padded[:, 2:, 1:-1, :] + padded[:, :-2, 1:-1, :]
    total = total + padded[:, 1:-1, 2:, :] + padded[:, 1:-1, :-2, :]
    total = total + jnp.roll(centre, 1, 3) + jnp.roll(centre, -1, 3)
    return total


def shards(labels, seed_noise, conc, curvature, quartic, wells, lame, eigen):
    full_x = labels.shape[0] * lax.axis_size("gx")
    full_y = labels.shape[1] * lax.axis_size("gy")
    full_z = labels.shape[2]
    if kernel_fits(labels.shape):
        return step_call(
            labels, seed_noise, conc, curvature, quartic, wells, lame, eigen, full_x, full_y
        )
    phase = phases_from(labels, seed_noise)
    part, chem = partition(phase, conc, curvature, quartic, wells)
    stacked = jnp.concatenate([phase, chem[None]], axis=0)
    padded = with_halo(stacked, (("gx", 1), ("gy", 2)), 1)
    lam_field = jnp.sum(phase * column(lame[0]), axis=0)
    shear_field = jnp.sum(phase * column(lame[1]), axis=0)
    eigen_field = jnp.einsum("ap,axyz->pxyz", eigen, phase, precision=lax.Precision.HIGHEST)
    lam0 = 0.5 * (jnp.max(lame[0]) + jnp.min(lame[0]))
    mu0 = 0.5 * (jnp.max(lame[1]) + jnp.min(lame[1]))
    strain = jnp.zeros((6,) + labels.shape, jnp.float32)
    step = fluctuation if slots_fit(full_z) else fluctuation_general
    for _ in range(ITERS):
        stress = stress_of(strain, eigen_field, lam_field, shear_field)
        strain = strain - step(stress, full_x, full_y, full_z, lam0, mu0)
    stress = stress_of(strain, eigen_field, lam_field, shear_field)
    elastic = strain - eigen_field
    trace = elastic[0] + elastic[1] + elastic[2]
    squares = (
        elastic[0] ** 2
        + elastic[1] ** 2
        + elastic[2] ** 2
        + 2.0 * (elastic[3] ** 2 + elastic[4] ** 2 + elastic[5] ** 2)
    )
    weight = jnp.array([1.0, 1.0, 1.0, 2.0, 2.0, 2.0], jnp.float32)
    coupling = jnp.einsum(
        "ap,pxyz->axyz", eigen * weight[None], stress, precision=lax.Precision.HIGHEST
    )
    stored = (
        0.5 * (column(lame[0]) * trace[None] ** 2 + 2.0 * column(lame[1]) * squares[None])
        - coupling
    )
    deviate = part - column(wells)
    energy = 0.5 * column(curvature) * deviate**2 + 0.25 * column(quartic) * deviate**4
    chemical = energy - chem[None] * part
    total_sq = jnp.sum(phase * phase, axis=0)
    barrier = 2.0 * phase * (total_sq[None] - phase * phase)
    laplacian = laplace_padded(padded)
    force = chemical + stored + barrier - laplacian[:4]
    phase_next = phase - step_phase * (force - jnp.mean(force, axis=0, keepdims=True))
    conc_next = conc + step_conc * laplacian[4]
    return (phase_next, conc_next, stress)


def solution(mesh):
    in_specs = (
        P("gx", "gy", None),
        P(None, "gx", "gy", None),
        P("gx", "gy", None),
        P(),
        P(),
        P(),
        P(),
        P(),
    )
    out_specs = (P(None, "gx", "gy", None), P("gx", "gy", None), P(None, "gx", "gy", None))
    return jax.shard_map(shards, mesh=mesh, in_specs=in_specs, out_specs=out_specs, check_vma=False)
```

```python
import functools
import math

import jax
import jax.numpy as jnp
import numpy as np
from jax import lax
from jax.experimental import pallas as pl
from jax.experimental.pallas import tpu as pltpu
from jax.sharding import PartitionSpec as P

NEWTON = 5
ITERS = 2


step_phase = 0.06
step_conc = 0.005


def with_halo(x, sides, width):
    for axis, dim in sides:
        count, length = (lax.axis_size(axis), x.shape[dim])
        up = [(i, (i + 1) % count) for i in range(count)]
        down = [(j, i) for i, j in up]
        last = lax.slice_in_dim(x, length - width, length, axis=dim)
        initial = lax.slice_in_dim(x, 0, width, axis=dim)
        before = lax.ppermute(last, axis, up)
        after = lax.ppermute(initial, axis, down)
        x = jnp.concatenate([before, x, after], axis=dim)
    return x


def column(values):
    return values.reshape(4, 1, 1, 1)


def phases_from(labels, seed_noise):
    marks = lax.broadcasted_iota(jnp.int32, (4, 1, 1, 1), 0)
    raw = seed_noise + 2.0 * (labels[None] == marks).astype(seed_noise.dtype)
    return raw / jnp.sum(raw, axis=0, keepdims=True)


def partition(phase, conc, curvature, quartic, wells):
    coef_a = column(curvature)
    coef_b = column(quartic)
    centre = column(wells)
    part = jnp.broadcast_to(conc[None], phase.shape)
    deviate = part - centre
    chem = jnp.sum(phase * (coef_a * deviate + coef_b * deviate**3), axis=0)
    for _ in range(NEWTON):
        deviate = part - centre
        slope = coef_a * deviate + coef_b * deviate**3 - chem[None]
        stiff = coef_a + 3.0 * coef_b * deviate * deviate
        shift = (
            conc - jnp.sum(phase * part, axis=0) + jnp.sum(phase * slope / stiff, axis=0)
        ) / jnp.sum(phase / stiff, axis=0)
        part = part + (shift[None] - slope) / stiff
        chem = chem + shift
    return (part, chem)


def stress_of(strain, eigen_field, lam_field, shear_field):
    elastic = strain - eigen_field
    trace = elastic[0] + elastic[1] + elastic[2]
    normal = (lax.broadcasted_iota(jnp.int32, (6, 1, 1, 1), 0) < 3).astype(strain.dtype)
    return 2.0 * shear_field[None] * elastic + (lam_field * trace)[None] * normal


def green(tau, freq_x, freq_y, freq_z, zero, lam0, mu0):
    vec_x = tau[0] * freq_x + tau[5] * freq_y + tau[4] * freq_z
    vec_y = tau[5] * freq_x + tau[1] * freq_y + tau[3] * freq_z
    vec_z = tau[4] * freq_x + tau[3] * freq_y + tau[2] * freq_z
    inner = freq_x * vec_x + freq_y * vec_y + freq_z * vec_z
    square = freq_x * freq_x + freq_y * freq_y + freq_z * freq_z + zero
    first = 1.0 / (2.0 * mu0 * square)
    second = (lam0 + mu0) / (mu0 * (lam0 + 2.0 * mu0)) * inner / (square * square)
    pairs = (
        (freq_x, vec_x, freq_x, vec_x),
        (freq_y, vec_y, freq_y, vec_y),
        (freq_z, vec_z, freq_z, vec_z),
        (freq_y, vec_y, freq_z, vec_z),
        (freq_x, vec_x, freq_z, vec_z),
        (freq_x, vec_x, freq_y, vec_y),
    )
    result = [(fk * vh + fh * vk) * first - fk * fh * second for fk, vk, fh, vh in pairs]
    return jnp.stack(result, axis=0)


def tables(length):
    grid = lax.broadcasted_iota(jnp.int32, (length, length), 0) * lax.broadcasted_iota(
        jnp.int32, (length, length), 1
    )
    angle = (grid % length).astype(jnp.float32) * (2.0 * math.pi / length)
    return (jnp.cos(angle), jnp.sin(angle))


def apply_table(table, data, axis):
    if axis == 3:
        flat = data.reshape(-1, data.shape[3])
        result = jnp.dot(
            flat, table.T, precision=lax.Precision.HIGHEST, preferred_element_type=jnp.float32
        )
        return result.reshape(data.shape[:3] + (table.shape[0],))
    moved = jnp.moveaxis(data, axis, 0)
    rest = moved.shape[1:]
    flat = moved.reshape(moved.shape[0], -1)
    result = jnp.dot(
        table, flat, precision=lax.Precision.HIGHEST, preferred_element_type=jnp.float32
    )
    return jnp.moveaxis(result.reshape((table.shape[0],) + rest), 0, axis)


def transform(pair, axis, inverse):
    real, imag = pair
    length = real.shape[axis]
    cosine, sine = tables(length)
    if inverse:
        new_real = (apply_table(cosine, real, axis) - apply_table(sine, imag, axis)) / length
        new_imag = (apply_table(cosine, imag, axis) + apply_table(sine, real, axis)) / length
    else:
        new_real = apply_table(cosine, real, axis) + apply_table(sine, imag, axis)
        new_imag = apply_table(cosine, imag, axis) - apply_table(sine, real, axis)
    return (new_real, new_imag)


def spectrum(stress):
    length = stress.shape[3]
    cosine, sine = tables(length)
    real = apply_table(cosine, stress, 3)
    imag = -apply_table(sine, stress, 3)
    real, imag = transform(
        (
            lax.all_to_all(real, "gy", split_axis=3, concat_axis=2, tiled=True),
            lax.all_to_all(imag, "gy", split_axis=3, concat_axis=2, tiled=True),
        ),
        axis=2,
        inverse=False,
    )
    real, imag = transform(
        (
            lax.all_to_all(real, "gx", split_axis=2, concat_axis=1, tiled=True),
            lax.all_to_all(imag, "gx", split_axis=2, concat_axis=1, tiled=True),
        ),
        axis=1,
        inverse=False,
    )
    return (real, imag)


def recover(pair):
    pair = transform(pair, 1, True)
    pair = transform(
        (
            lax.all_to_all(pair[0], "gx", split_axis=1, concat_axis=2, tiled=True),
            lax.all_to_all(pair[1], "gx", split_axis=1, concat_axis=2, tiled=True),
        ),
        axis=2,
        inverse=True,
    )
    result = transform(
        (
            lax.all_to_all(pair[0], "gy", split_axis=2, concat_axis=3, tiled=True),
            lax.all_to_all(pair[1], "gy", split_axis=2, concat_axis=3, tiled=True),
        ),
        axis=3,
        inverse=True,
    )
    return result


def frequencies(count, offset, length, axis):
    index = lax.iota(jnp.int32, count) + offset
    index = jnp.where(index >= length // 2, index - length, index)
    kept = jnp.where(index == -(length // 2), 0, index)
    dims_shape = [1, 1, 1]
    dims_shape[axis] = count
    return (kept.astype(jnp.float32) / length).reshape(dims_shape)


def wave_numbers(dims, full_x, full_y, full_z):
    offsets = (jnp.int32(0), lax.axis_index("gx") * dims[2], lax.axis_index("gy") * dims[3])
    freq_x = frequencies(dims[1], offsets[0], full_x, 0)
    freq_y = frequencies(dims[2], offsets[1], full_y, 1)
    freq_z = frequencies(dims[3], offsets[2], full_z, 2)
    zero = ((freq_x == 0.0) & (freq_y == 0.0) & (freq_z == 0.0)).astype(jnp.float32)
    return (freq_x, freq_y, freq_z, zero)


def slots_fit(full_z):
    count = lax.axis_size("gx") * lax.axis_size("gy")
    return full_z % 2 == 0 and (full_z // 2) % count == 0


def angles(length):
    grid = np.outer(np.arange(length), np.arange(length)) % length
    return grid * (2.0 * math.pi / length)


def z_tables(length):
    half = length // 2
    angle = angles(length)[:half]
    real = np.cos(angle)
    imag = -np.sin(angle)
    imag[0] = np.cos(math.pi * np.arange(length))
    forward = np.stack([real, imag], axis=1).astype(np.float32)
    weight = np.full((half, 1, 1), 2.0 / length)
    weight[0] = 1.0 / length
    return forward, (np.stack([real, imag], axis=1) * weight).astype(np.float32)


def complex_table(length, inverse):
    angle = angles(length)
    cosine, sine = np.cos(angle), np.sin(angle)
    if inverse:
        table = np.array([[cosine, -sine], [sine, cosine]]) / length
    else:
        table = np.array([[cosine, sine], [-sine, cosine]])
    return table.transpose(0, 2, 1, 3).astype(np.float32)


def contract(spec, *operands):
    return jnp.einsum(
        spec, *operands, precision=lax.Precision.HIGH, preferred_element_type=jnp.float32
    )


def fluctuation(stress, full_x, full_y, full_z, lam0, mu0):
    count_x, count_y = lax.axis_size("gx"), lax.axis_size("gy")
    count = count_x * count_y
    _, size_x, size_y, _ = stress.shape
    slots = full_z // 2 // count
    forward_z, inverse_z = z_tables(full_z)
    data = contract("krz,cxyz->krcxy", forward_z, stress)
    data = lax.all_to_all(data, ("gx", "gy"), split_axis=0, concat_axis=0, tiled=True)
    data = data.reshape(count_x, count_y, slots, 2, 6, size_x, size_y)
    data = data.transpose(2, 3, 4, 0, 5, 1, 6).reshape(slots, 2, 6, full_x, full_y)
    data = contract("sLrl,krcly->kscLy", complex_table(full_x, False), data)
    data = contract("sLrl,krcxl->kscxL", complex_table(full_y, False), data)
    data = data.transpose(2, 1, 3, 4, 0)
    freq_x = frequencies(full_x, 0, full_x, 0)
    freq_y = frequencies(full_y, 0, full_y, 1)
    position = lax.axis_index("gx") * count_y + lax.axis_index("gy")
    freq_z = frequencies(slots, position * slots, full_z, 2)
    zero = ((freq_x == 0.0) & (freq_y == 0.0) & (freq_z == 0.0)).astype(jnp.float32)
    data = jnp.stack([green(data[:, r], freq_x, freq_y, freq_z, zero, lam0, mu0) for r in (0, 1)], 1)
    data = data.transpose(4, 1, 0, 2, 3)
    data = contract("sLrl,krcxl->kscxL", complex_table(full_y, True), data)
    data = contract("sLrl,krcly->kscLy", complex_table(full_x, True), data)
    data = data.reshape(slots, 2, 6, count_x, size_x, count_y, size_y)
    data = data.transpose(3, 5, 0, 1, 2, 4, 6).reshape(count * slots, 2, 6, size_x, size_y)
    data = lax.all_to_all(data, ("gx", "gy"), split_axis=0, concat_axis=0, tiled=True)
    return contract("krz,krcxy->cxyz", inverse_z, data)


def fluctuation_general(stress, full_x, full_y, full_z, lam0, mu0):
    real, imag = spectrum(stress)
    freq_x, freq_y, freq_z, zero = wave_numbers(real.shape, full_x, full_y, full_z)
    upd_real = green(real, freq_x, freq_y, freq_z, zero, lam0, mu0)
    upd_imag = green(imag, freq_x, freq_y, freq_z, zero, lam0, mu0)
    packed = (upd_real[0::2] - upd_imag[1::2], upd_imag[0::2] + upd_real[1::2])
    back_real, back_imag = recover(packed)
    return jnp.stack([back_real, back_imag], axis=1).reshape(stress.shape)


MESH = pl.DeviceIdType.MESH
LANES = 128
ROWS = 8


def kernel_fits(shape):
    count_x, count_y = lax.axis_size("gx"), lax.axis_size("gy")
    size_x, size_y, full_z = shape
    return (
        full_z == 2 * count_x * count_y
        and count_x == ROWS
        and count_y * size_y == LANES
        and size_x * size_y == 2 * LANES
        and (count_x * count_y) % 16 == 0
    )


def split(value):
    high = value.astype(jnp.bfloat16)
    return high, (value - high.astype(jnp.float32)).astype(jnp.bfloat16)


def split_table(table):
    high = np.asarray(table, np.float32).astype(jnp.bfloat16)
    low = (np.asarray(table, np.float64) - high.astype(np.float64)).astype(jnp.bfloat16)
    return high, low


def table_left(table):
    high, low = split_table(table)
    return np.concatenate([high, high, low], axis=1)


def table_right(table):
    high, low = split_table(table)
    return np.stack([high, low])


def left_product(table, value):
    high, low = split(value)
    stacked = jnp.concatenate([high, low, high], axis=0)
    return jnp.dot(table, stacked, preferred_element_type=jnp.float32)


def right_product(value, table):
    high, low = split(value)
    product = functools.partial(jnp.dot, preferred_element_type=jnp.float32)
    return product(high, table[0]) + (product(low, table[0]) + product(high, table[1]))


def kernel_tables(size_x, full_x, full_y, full_z):
    forward, inverse = z_tables(full_z)
    forward = forward.transpose(1, 0, 2).reshape(full_z, full_z)
    inverse = inverse.transpose(2, 1, 0).reshape(full_z, full_z)
    count_x = full_x // size_x
    order = np.arange(full_x).reshape(count_x, size_x).T.reshape(-1)
    to_x = complex_table(full_x, False).transpose(0, 1, 2, 3)
    forward_x = to_x.transpose(0, 1, 2, 3)[:, :, :, order]
    inverse_x = complex_table(full_x, True)[:, order]
    forward_y = complex_table(full_y, False)
    inverse_y = complex_table(full_y, True)
    flat = lambda table, length: table.reshape(2 * length, 2 * length)
    return (
        table_left(forward),
        table_left(flat(forward_x, full_x)),
        table_right(flat(forward_y, full_y).T),
        table_right(flat(inverse_y, full_y).T),
        table_left(flat(inverse_x, full_x)),
        table_left(inverse),
    )


def position():
    return lax.axis_index("gx") * lax.axis_size("gy") + lax.axis_index("gy")


def for_others(action):
    count_x, count_y = lax.axis_size("gx"), lax.axis_size("gy")
    i, j = lax.axis_index("gx"), lax.axis_index("gy")
    turns = [j] + [lax.rem(j + step, count_y) for step in range(1, count_y)]
    for other in turns[1:]:
        action(i, other)

    def row(step, carry):
        far = lax.rem(i + step, count_x)
        for other in turns:
            action(far, other)
        return carry

    lax.fori_loop(1, count_x, row, 0)


def greet():
    barrier = pltpu.get_barrier_semaphore()
    for_others(
        lambda i, j: pl.semaphore_signal(barrier, inc=1, device_id=(i, j), device_id_type=MESH)
    )


def greeted():
    count = lax.axis_size("gx") * lax.axis_size("gy")
    pl.semaphore_wait(pltpu.get_barrier_semaphore(), count - 1)


def exchange_start(pack):
    sent, received, send_sem, recv_sem = pack
    count_y = lax.axis_size("gy")
    rows = sent.shape[0] // (lax.axis_size("gx") * count_y)
    own = pl.ds(pl.multiple_of(position() * rows, 8), rows)

    def send(i, j):
        pltpu.make_async_remote_copy(
            src_ref=sent.at[pl.ds(pl.multiple_of((i * count_y + j) * rows, 8), rows)],
            dst_ref=received.at[own],
            send_sem=send_sem,
            recv_sem=recv_sem,
            device_id=(i, j),
            device_id_type=MESH,
        ).start()

    for_others(send)
    received[own, :] = sent[own, :]


def exchange_all(pack):
    sent, received, send_sem, recv_sem = pack
    count_x, count_y = lax.axis_size("gx"), lax.axis_size("gy")
    rows = sent.shape[0] // (count_x * count_y) * (count_x * count_y - 1)
    return pltpu.make_async_remote_copy(
        src_ref=sent.at[pl.ds(0, rows)],
        dst_ref=received.at[pl.ds(0, rows)],
        send_sem=send_sem,
        recv_sem=recv_sem,
        device_id=(lax.rem(lax.axis_index("gx") + 1, count_x), lax.axis_index("gy")),
        device_id_type=MESH,
    )


def exchange_wait(pack, arrived):
    if arrived:
        exchange_all(pack).wait_recv()
    else:
        exchange_all(pack).wait_send()


def swap_blocks(parts):
    count = len(parts)
    width = LANES // count
    block = lax.broadcasted_iota(jnp.int32, parts[0].shape, 1) // width
    result = []
    for a in range(count):
        total = None
        for b, part in enumerate(parts):
            shift = (width * (b - a)) % LANES
            moved = pltpu.roll(part, shift, 1) if shift else part
            total = moved if total is None else jnp.where(block == b, moved, total)
        result.append(total)
    return result


GROUPS_THERE = ((0, 4), (4, 6))
GROUPS_BACK = ((0, 2), (2, 6))
GROUPS = (GROUPS_THERE, GROUPS_BACK)


def halves(z_ref, t_ref, sent, group):
    slots = z_ref.shape[0] // 2
    rows = 4 * (group[1] - group[0])
    for c in range(*group):
        result = left_product(z_ref[...], t_ref[c])
        for r in range(2):
            for h in range(2):
                piece = result[r * slots:(r + 1) * slots, h * LANES:(h + 1) * LANES]
                first = (c - group[0]) * 4 + r * 2 + h
                sent[pl.ds(first, slots, stride=rows), :] = piece


def plane_rows(received, c, r, count_y, rows):
    result = []
    for h in range(2):
        first = c * 4 + r * 2 + h
        parts = [
            received[pl.ds(j * rows + first, ROWS, stride=rows * count_y), :]
            for j in range(count_y)
        ]
        result += swap_blocks(parts)
    return jnp.concatenate(result, axis=0)


def plane_store(sent, value, c, r, count_y, rows):
    for h in range(2):
        first = c * 4 + r * 2 + h
        parts = [
            value[(h * count_y + a) * ROWS:(h * count_y + a + 1) * ROWS] for a in range(count_y)
        ]
        for j, part in enumerate(swap_blocks(parts)):
            sent[pl.ds(j * rows + first, ROWS, stride=rows * count_y), :] = part


def plane_forward(received, plane_ref, fx_ref, fy_ref, group, full_x, full_y):
    count_y = lax.axis_size("gy")
    number = group[1] - group[0]
    rows_x = []
    for c in range(number):
        both = [plane_rows(received, c, r, count_y, 4 * number) for r in range(2)]
        rows_x.append(jnp.concatenate(both, axis=0))
    spec = left_product(fx_ref[...], jnp.concatenate(rows_x, axis=1))
    lanes = []
    for c in range(number):
        part = spec[:, c * full_y:(c + 1) * full_y]
        lanes.append(jnp.concatenate([part[:full_x], part[full_x:]], axis=1))
    spec = right_product(jnp.concatenate(lanes, axis=0), fy_ref)
    plane_ref[group[0] * full_x:group[1] * full_x, :] = spec


def plane_green(plane_ref, wave_ref, full_x, full_z):
    freq_z = lax.convert_element_type(position(), jnp.float32) * (1.0 / full_z)

    def chunk(step, carry):
        start = pl.multiple_of(step * ROWS, ROWS)
        at = pl.ds(start, ROWS)
        where = [pl.ds(pl.multiple_of(c * full_x + start, ROWS), ROWS) for c in range(6)]
        first, second, freq_x, freq_y = [wave_ref[w, at, :] for w in range(4)]
        tau = [plane_ref[where[c], :] for c in range(6)]
        vec_x = tau[0] * freq_x + tau[5] * freq_y + tau[4] * freq_z
        vec_y = tau[5] * freq_x + tau[1] * freq_y + tau[3] * freq_z
        vec_z = tau[4] * freq_x + tau[3] * freq_y + tau[2] * freq_z
        inner = (freq_x * vec_x + freq_y * vec_y + freq_z * vec_z) * second
        pairs = (
            (freq_x, vec_x, freq_x, vec_x),
            (freq_y, vec_y, freq_y, vec_y),
            (freq_z, vec_z, freq_z, vec_z),
            (freq_y, vec_y, freq_z, vec_z),
            (freq_x, vec_x, freq_z, vec_z),
            (freq_x, vec_x, freq_y, vec_y),
        )
        for c, (fk, vk, fh, vh) in enumerate(pairs):
            plane_ref[where[c], :] = (fk * vh + fh * vk) * first - fk * fh * inner
        return carry

    lax.fori_loop(0, full_x // ROWS, chunk, 0)


def plane_back(plane_ref, sent, iy_ref, ix_ref, group, full_x, full_y):
    count_y = lax.axis_size("gy")
    number = group[1] - group[0]
    spec = right_product(plane_ref[group[0] * full_x:group[1] * full_x, :], iy_ref)
    lanes = []
    for c in range(number):
        part = spec[c * full_x:(c + 1) * full_x]
        lanes.append(jnp.concatenate([part[:, :full_y], part[:, full_y:]], axis=0))
    plane = left_product(ix_ref[...], jnp.concatenate(lanes, axis=1))
    for c in range(number):
        for r in range(2):
            value = plane[r * full_x:(r + 1) * full_x, c * full_y:(c + 1) * full_y]
            plane_store(sent, value, c, r, count_y, 4 * number)


def strain_update(received, wz_ref, strain_ref, group):
    slots = wz_ref.shape[0] // 2
    rows = 4 * (group[1] - group[0])
    for c in range(*group):
        value = jnp.concatenate([
            jnp.concatenate([
                received[pl.ds((c - group[0]) * 4 + r * 2 + h, slots, stride=rows), :]
                for h in range(2)
            ], axis=1) for r in range(2)
        ], axis=0)
        strain_ref[c] = strain_ref[c] - left_product(wz_ref[...], value)


def wave_parts(lame_ref, full_x, full_y, full_z):
    shape = (full_x, 2 * full_y)
    row = lax.broadcasted_iota(jnp.int32, shape, 0)
    lane = lax.broadcasted_iota(jnp.int32, shape, 1) % full_y

    def weight(index, length):
        signed = jnp.where(index >= length // 2, index - length, index)
        signed = jnp.where(signed == -(length // 2), 0, signed)
        return signed.astype(jnp.float32) * (1.0 / length)

    freq_x = weight(row, full_x)
    freq_y = weight(lane, full_y)
    freq_z = weight(jnp.full(shape, position(), jnp.int32), full_z)
    square = freq_x * freq_x + freq_y * freq_y + freq_z * freq_z
    square = jnp.where(square == 0.0, 1.0, square)

    def middle(which):
        values = [jnp.full(shape, lame_ref[which, a], jnp.float32) for a in range(4)]
        top = functools.reduce(jnp.maximum, values)
        return 0.5 * (top + functools.reduce(jnp.minimum, values))

    lam0, mu0 = middle(0), middle(1)
    first = 1.0 / (2.0 * mu0 * square)
    second = (lam0 + mu0) / (mu0 * (lam0 + 2.0 * mu0)) / (square * square)
    return first, second, freq_x, freq_y, freq_z


def elastic_chunk(at, strain_ref, field_ref):
    elastic = [strain_ref[p, at, :] - field_ref[2 + p, at, :] for p in range(6)]
    lam, shear2 = field_ref[0, at, :], 2.0 * field_ref[1, at, :]
    trace = elastic[0] + elastic[1] + elastic[2]
    stress = [shear2 * e for e in elastic]
    stress = [stress[p] + lam * trace if p < 3 else stress[p] for p in range(6)]
    return elastic, trace, stress


def half(h):
    return slice(h * LANES, (h + 1) * LANES)


def turned(value, shift):
    shift = shift % LANES
    return pltpu.roll(value, shift, 1) if shift else value


def lane_block(shape, width):
    return lax.broadcasted_iota(jnp.int32, shape, 1) // width


def lane_place(shape, width):
    return lax.broadcasted_iota(jnp.int32, shape, 1) % width


def halo_pack(phase_ref, chem_ref, x_up, x_down, y_up, y_down, width):
    full_z = phase_ref.shape[1]
    blocks = LANES // width
    fold = full_z // blocks
    block = lane_block((full_z, LANES), width)
    place = lane_place((full_z, LANES), width)
    fields = [phase_ref[f] for f in range(4)] + [chem_ref[...]]
    for face, h, own in ((x_up, 1, blocks - 1), (x_down, 0, 0)):
        total = turned(fields[0][:, half(h)], -width * own)
        for f in range(1, 4):
            total = jnp.where(block == f, turned(fields[f][:, half(h)], width * (f - own)), total)
        face[:full_z, :] = total
        parts = [fields[4][k * fold:(k + 1) * fold, half(h)] for k in range(blocks)]
        total = turned(parts[0], -width * own)
        for k in range(1, blocks):
            total = jnp.where(block[:fold] == k, turned(parts[k], width * (k - own)), total)
        face[full_z:, :] = total
    for face, own in ((y_up, width - 1), (y_down, 0)):
        total = jnp.zeros((full_z, LANES), jnp.float32)
        for f in range(5):
            for h in range(2):
                slot = 8 * h + f
                total = jnp.where(place == slot, turned(fields[f][:, half(h)], slot - own), total)
        face[...] = total


def halo_laplace(f, field, x_before, x_after, y_before, y_after, width):
    full_z = field.shape[0]
    blocks = LANES // width
    fold = full_z // blocks
    block = lane_block((full_z, LANES), width)
    place = lane_place((full_z, LANES), width)

    def face(ref, own):
        if f < 4:
            return turned(ref[:full_z, :], width * (own - f))
        folded = ref[full_z:, :]
        return jnp.concatenate([turned(folded, width * (own - k)) for k in range(blocks)], axis=0)

    sides = [field[:, half(h)] for h in range(2)]
    right = [turned(side, width) for side in sides]
    left = [turned(side, -width) for side in sides]
    last = blocks - 1
    result = []
    for h in range(2):
        slot = 8 * h + f
        side = sides[h]
        below = jnp.where(block == 0, face(x_before, 0) if h == 0 else right[0], right[h])
        above = jnp.where(block == last, left[1] if h == 0 else face(x_after, last), left[h])
        total = below + above - 6.0 * side
        total += jnp.where(place == 0, turned(y_before[...], -slot), turned(side, 1))
        after = turned(y_after[...], width - 1 - slot)
        total += jnp.where(place == width - 1, after, turned(side, -1))
        total += pltpu.roll(side, 1, 0) + pltpu.roll(side, full_z - 1, 0)
        result.append(total)
    return result


def newton_chunk(phase, conc, scalars):
    curve, quart, wells = scalars
    part = [conc for _ in range(4)]
    dev = [conc - wells[a] for a in range(4)]
    chem = sum(
        phase[a] * (curve[a] * dev[a] + quart[a] * (dev[a] * dev[a] * dev[a])) for a in range(4)
    )
    for _ in range(NEWTON):
        dev = [part[a] - wells[a] for a in range(4)]
        square = [d * d for d in dev]
        slope = [dev[a] * (curve[a] + quart[a] * square[a]) - chem for a in range(4)]
        soft = [1.0 / (curve[a] + (3.0 * quart[a]) * square[a]) for a in range(4)]
        weight = [phase[a] * soft[a] for a in range(4)]
        top = conc - sum(phase[a] * part[a] for a in range(4))
        top = top + sum(weight[a] * slope[a] for a in range(4))
        shift = top / sum(weight)
        part = [part[a] + (shift - slope[a]) * soft[a] for a in range(4)]
        chem = chem + shift
    dev = [part[a] - wells[a] for a in range(4)]
    square = [d * d for d in dev]
    total = sum(p * p for p in phase)
    local = []
    for a in range(4):
        energy = square[a] * (0.5 * curve[a] + (0.25 * quart[a]) * square[a])
        barrier = 2.0 * phase[a] * (total - phase[a] * phase[a])
        local.append(energy - chem * part[a] + barrier)
    return chem, local


def step_kernel(
    full_x, full_y, labels_in, noise_in, raw_conc_in, curve_ref, quart_ref, wells_ref, lame_ref,
    eigen_ref, mz_in, fx_in, fy_in, iy_in, ix_in, wz_in,
    next_ref, conc_next_ref, stress_ref,
    labels_ref, noise_ref, raw_conc_ref, mz_ref, fx_ref, fy_ref, iy_ref, ix_ref, wz_ref, load_sem,
    phase_ref, conc_ref, chem_ref, local_ref, field_ref, strain_ref, t_ref, plane_ref, wave_ref,
    *buffers
):
    full_z = phase_ref.shape[1]
    chunks = full_z // ROWS
    width = full_y // lax.axis_size("gy")
    number = ITERS * (len(GROUPS_THERE) + len(GROUPS_BACK))
    free = iter([buffers[4 * n:4 * n + 4] for n in range(number)])
    packs = [[next(free) for _ in GROUPS[t % 2]] for t in range(2 * ITERS)]
    halo_sent, halo_got = buffers[4 * number:4 * number + 4], buffers[4 * number + 4:4 * number + 8]
    halo_send, halo_recv = buffers[4 * number + 8:]
    loads = [
        pltpu.make_async_copy(source, target, load_sem.at[n])
        for n, (source, target) in enumerate((
            (noise_in, noise_ref), (labels_in, labels_ref), (raw_conc_in, raw_conc_ref),
            (mz_in, mz_ref), (fx_in, fx_ref), (fy_in, fy_ref), (iy_in, iy_ref), (ix_in, ix_ref),
            (wz_in, wz_ref),
        ))
    ]
    for load in loads:
        load.start()
    greet()
    for load in loads[:3]:
        load.wait()

    for h in range(2):
        at = pl.ds(h * LANES, LANES)
        label = labels_ref[at, :]
        raw = [noise_ref[a, at, :] + jnp.where(label == a, 2.0, 0.0) for a in range(4)]
        total = raw[0] + raw[1] + raw[2] + raw[3]
        for a in range(4):
            phase_ref[a, :, half(h)] = (raw[a] / total).T
        conc_ref[:, half(h)] = raw_conc_ref[at, :].T

    def rows_at(step):
        return pl.ds(pl.multiple_of(step * ROWS, ROWS), ROWS)

    def fields(step, carry):
        at = rows_at(step)
        phase = [phase_ref[a, at, :] for a in range(4)]
        for which in range(2):
            field_ref[which, at, :] = sum(phase[a] * lame_ref[which, a] for a in range(4))
        for p in range(6):
            field_ref[2 + p, at, :] = sum(phase[a] * eigen_ref[a, p] for a in range(4))
            strain_ref[p, at, :] = jnp.zeros_like(phase[0])
        _, _, stress = elastic_chunk(at, strain_ref, field_ref)
        for p in range(6):
            t_ref[p, at, :] = stress[p]
        return carry

    def stresses(step, carry):
        at = rows_at(step)
        _, _, stress = elastic_chunk(at, strain_ref, field_ref)
        for p in range(6):
            t_ref[p, at, :] = stress[p]
        return carry

    def newton(step, carry):
        at = rows_at(step)
        phase = [phase_ref[a, at, :] for a in range(4)]
        scalars = [[ref[a] for a in range(4)] for ref in (curve_ref, quart_ref, wells_ref)]
        chem, local = newton_chunk(phase, conc_ref[at, :], scalars)
        chem_ref[at, :] = chem
        for a in range(4):
            local_ref[a, at, :] = local[a]
        return carry

    def halo_copies():
        i, j = lax.axis_index("gx"), lax.axis_index("gy")
        count_x, count_y = lax.axis_size("gx"), lax.axis_size("gy")
        targets = (
            (lax.rem(i + 1, count_x), j),
            (lax.rem(i + count_x - 1, count_x), j),
            (i, lax.rem(j + 1, count_y)),
            (i, lax.rem(j + count_y - 1, count_y)),
        )
        return [
            pltpu.make_async_remote_copy(
                src_ref=halo_sent[n],
                dst_ref=halo_got[n],
                send_sem=halo_send.at[n],
                recv_sem=halo_recv.at[n],
                device_id=target,
                device_id_type=MESH,
            )
            for n, target in enumerate(targets)
        ]

    def beside_first():
        for w, value in enumerate(wave_parts(lame_ref, full_x, full_y, full_z)[:4]):
            wave_ref[w] = value
        lax.fori_loop(0, chunks, newton, 0)
        halo_pack(phase_ref, chem_ref, *halo_sent, width)
        for copy in halo_copies():
            copy.start()
        for load in loads[4:]:
            load.wait()

    def beside_second():
        for copy in halo_copies():
            copy.wait_recv()
        for f in range(5):
            field = phase_ref[f] if f < 4 else chem_ref[...]
            spread = halo_laplace(f, field, *halo_got, width)
            for h in range(2):
                if f < 4:
                    local_ref[f, :, half(h)] = local_ref[f, :, half(h)] - spread[h]
                else:
                    conc_next_ref[:, half(h)] = conc_ref[:, half(h)] + step_conc * spread[h]

    for turn in range(ITERS):
        there, back = packs[2 * turn], packs[2 * turn + 1]
        lax.fori_loop(0, chunks, stresses if turn else fields, 0)
        if turn == 0:
            loads[3].wait()
        for pack, group in zip(there, GROUPS_THERE):
            halves(mz_ref, t_ref, pack[0], group)
            if turn == 0 and group is GROUPS_THERE[0]:
                greeted()
            exchange_start(pack)
        if turn == 0:
            beside_first()
        for pack, group in zip(there, GROUPS_THERE):
            exchange_wait(pack, True)
            plane_forward(pack[1], plane_ref, fx_ref, fy_ref, group, full_x, full_y)
        plane_green(plane_ref, wave_ref, full_x, full_z)
        for pack, group in zip(back, GROUPS_BACK):
            plane_back(plane_ref, pack[0], iy_ref, ix_ref, group, full_x, full_y)
            exchange_start(pack)
        if turn == 0:
            beside_second()
        for pack, group in zip(back, GROUPS_BACK):
            exchange_wait(pack, True)
            strain_update(pack[1], wz_ref, strain_ref, group)

    def finish(step, carry):
        at = rows_at(step)
        elastic, trace, stress = elastic_chunk(at, strain_ref, field_ref)
        for p in range(6):
            stress_ref[p, at, :] = stress[p]
        squares = sum(e * e for e in elastic[:3]) + 2.0 * sum(e * e for e in elastic[3:])
        force = []
        for a in range(4):
            coupling = sum(
                stress[p] * (eigen_ref[a, p] * (1.0 if p < 3 else 2.0)) for p in range(6)
            )
            stored = 0.5 * lame_ref[0, a] * trace * trace + lame_ref[1, a] * squares
            force.append(local_ref[a, at, :] + (stored - coupling))
        mean = 0.25 * (force[0] + force[1] + force[2] + force[3])
        for a in range(4):
            next_ref[a, at, :] = phase_ref[a, at, :] - step_phase * (force[a] - mean)
        return carry

    lax.fori_loop(0, chunks, finish, 0)
    for group_packs in packs:
        for pack in group_packs:
            exchange_wait(pack, False)
    for copy in halo_copies():
        copy.wait_send()


def place_kernel(next_in, conc_in, stress_in, next_out, conc_out, stress_out, got, made, got_sem, made_sem):
    sources = [stress_in.at[p] for p in range(6)] + [next_in.at[a] for a in range(4)] + [conc_in]
    targets = [stress_out.at[p] for p in range(6)] + [next_out.at[a] for a in range(4)] + [conc_out]
    number = len(sources)
    loads = [pltpu.make_async_copy(sources[n], got.at[n], got_sem.at[n]) for n in range(number)]
    stores = [pltpu.make_async_copy(made.at[n], targets[n], made_sem.at[n]) for n in range(number)]
    for load in loads:
        load.start()
    for n in range(number):
        loads[n].wait()
        for h in range(got.shape[2] // LANES):
            made[n, half(h), :] = got[n, :, half(h)].T
        stores[n].start()
    for store in stores:
        store.wait()


def place_call(phase_next, conc_next, stress):
    full_z, cells = conc_next.shape
    hbm = pl.BlockSpec(memory_space=pl.ANY)
    turned_shape = lambda *lead: jax.ShapeDtypeStruct(lead + (cells, full_z), jnp.float32)
    return pl.pallas_call(
        place_kernel,
        out_shape=(turned_shape(4), turned_shape(), turned_shape(6)),
        in_specs=[hbm] * 3,
        out_specs=(hbm,) * 3,
        scratch_shapes=[
            pltpu.VMEM((11, full_z, cells), jnp.float32),
            pltpu.VMEM((11, cells, full_z), jnp.float32),
            pltpu.SemaphoreType.DMA((11,)),
            pltpu.SemaphoreType.DMA((11,)),
        ],
        compiler_params=pltpu.CompilerParams(vmem_limit_bytes=56 * 1024 * 1024),
    )(phase_next, conc_next, stress)


def step_call(labels, seed_noise, conc, curvature, quartic, wells, lame, eigen, full_x, full_y):
    size_x, size_y, full_z = labels.shape
    cells = size_x * size_y
    count = full_z // 2
    tables = [jnp.asarray(t) for t in kernel_tables(size_x, full_x, full_y, full_z)]
    vmem = pl.BlockSpec(memory_space=pltpu.VMEM)
    smem = pl.BlockSpec(memory_space=pltpu.SMEM)
    hbm = pl.BlockSpec(memory_space=pltpu.HBM)
    scratch = lambda *shape: pltpu.VMEM(shape, jnp.float32)
    buffers = []
    for t in range(2 * ITERS):
        for group in GROUPS[t % 2]:
            rows = 4 * (group[1] - group[0]) * count
            buffers += [scratch(rows, LANES), scratch(rows, LANES)]
            buffers += [pltpu.SemaphoreType.DMA] * 2
    x_face = scratch(full_z + full_z * size_y // LANES, LANES)
    y_face = scratch(full_z, LANES)
    buffers += [x_face, x_face, y_face, y_face] * 2 + [pltpu.SemaphoreType.DMA((4,))] * 2
    whole = lambda *lead: jax.ShapeDtypeStruct(lead + (full_z, cells), jnp.float32)
    result = pl.pallas_call(
        functools.partial(step_kernel, full_x, full_y),
        out_shape=(whole(4), whole(), whole(6)),
        in_specs=[hbm] * 3 + [smem] * 5 + [hbm] * 6,
        out_specs=(vmem, vmem, vmem),
        scratch_shapes=[pltpu.VMEM((cells, full_z), jnp.int32)]
        + [scratch(4, cells, full_z), scratch(cells, full_z)]
        + [pltpu.VMEM(table.shape, table.dtype) for table in tables]
        + [pltpu.SemaphoreType.DMA((3 + len(tables),))]
        + [
            scratch(4, full_z, cells),
            scratch(full_z, cells),
            scratch(full_z, cells),
            scratch(4, full_z, cells),
            scratch(8, full_z, cells),
            scratch(6, full_z, cells),
            scratch(6, full_z, cells),
            scratch(6 * full_x, 2 * full_y),
            scratch(4, full_x, 2 * full_y),
        ]
        + buffers,
        compiler_params=pltpu.CompilerParams(
            collective_id=0, has_side_effects=True, vmem_limit_bytes=56 * 1024 * 1024
        ),
    )(
        labels.reshape(cells, full_z), seed_noise.reshape(4, cells, full_z),
        conc.reshape(cells, full_z), curvature, quartic, wells, lame, eigen, *tables
    )
    phase_next, conc_next, stress = place_call(*result)
    shape = (size_x, size_y, full_z)
    return phase_next.reshape((4,) + shape), conc_next.reshape(shape), stress.reshape((6,) + shape)


def laplace_padded(padded):
    centre = padded[:, 1:-1, 1:-1, :]
    total = -6.0 * centre
    total = total + padded[:, 2:, 1:-1, :] + padded[:, :-2, 1:-1, :]
    total = total + padded[:, 1:-1, 2:, :] + padded[:, 1:-1, :-2, :]
    total = total + jnp.roll(centre, 1, 3) + jnp.roll(centre, -1, 3)
    return total


def shards(labels, seed_noise, conc, curvature, quartic, wells, lame, eigen):
    full_x = labels.shape[0] * lax.axis_size("gx")
    full_y = labels.shape[1] * lax.axis_size("gy")
    full_z = labels.shape[2]
    if kernel_fits(labels.shape):
        return step_call(
            labels, seed_noise, conc, curvature, quartic, wells, lame, eigen, full_x, full_y
        )
    phase = phases_from(labels, seed_noise)
    part, chem = partition(phase, conc, curvature, quartic, wells)
    stacked = jnp.concatenate([phase, chem[None]], axis=0)
    padded = with_halo(stacked, (("gx", 1), ("gy", 2)), 1)
    lam_field = jnp.sum(phase * column(lame[0]), axis=0)
    shear_field = jnp.sum(phase * column(lame[1]), axis=0)
    eigen_field = jnp.einsum("ap,axyz->pxyz", eigen, phase, precision=lax.Precision.HIGHEST)
    lam0 = 0.5 * (jnp.max(lame[0]) + jnp.min(lame[0]))
    mu0 = 0.5 * (jnp.max(lame[1]) + jnp.min(lame[1]))
    strain = jnp.zeros((6,) + labels.shape, jnp.float32)
    step = fluctuation if slots_fit(full_z) else fluctuation_general
    for _ in range(ITERS):
        stress = stress_of(strain, eigen_field, lam_field, shear_field)
        strain = strain - step(stress, full_x, full_y, full_z, lam0, mu0)
    stress = stress_of(strain, eigen_field, lam_field, shear_field)
    elastic = strain - eigen_field
    trace = elastic[0] + elastic[1] + elastic[2]
    squares = (
        elastic[0] ** 2
        + elastic[1] ** 2
        + elastic[2] ** 2
        + 2.0 * (elastic[3] ** 2 + elastic[4] ** 2 + elastic[5] ** 2)
    )
    weight = jnp.array([1.0, 1.0, 1.0, 2.0, 2.0, 2.0], jnp.float32)
    coupling = jnp.einsum(
        "ap,pxyz->axyz", eigen * weight[None], stress, precision=lax.Precision.HIGHEST
    )
    stored = (
        0.5 * (column(lame[0]) * trace[None] ** 2 + 2.0 * column(lame[1]) * squares[None])
        - coupling
    )
    deviate = part - column(wells)
    energy = 0.5 * column(curvature) * deviate**2 + 0.25 * column(quartic) * deviate**4
    chemical = energy - chem[None] * part
    total_sq = jnp.sum(phase * phase, axis=0)
    barrier = 2.0 * phase * (total_sq[None] - phase * phase)
    laplacian = laplace_padded(padded)
    force = chemical + stored + barrier - laplacian[:4]
    phase_next = phase - step_phase * (force - jnp.mean(force, axis=0, keepdims=True))
    conc_next = conc + step_conc * laplacian[4]
    return (phase_next, conc_next, stress)


def solution(mesh):
    in_specs = (
        P("gx", "gy", None),
        P(None, "gx", "gy", None),
        P("gx", "gy", None),
        P(),
        P(),
        P(),
        P(),
        P(),
    )
    out_specs = (P(None, "gx", "gy", None), P("gx", "gy", None), P(None, "gx", "gy", None))
    return jax.shard_map(shards, mesh=mesh, in_specs=in_specs, out_specs=out_specs, check_vma=False)
```

```python
import functools
import math

import jax
import jax.numpy as jnp
import numpy as np
from jax import lax
from jax.experimental import pallas as pl
from jax.experimental.pallas import tpu as pltpu
from jax.sharding import PartitionSpec as P

NEWTON = 5
ITERS = 2


step_phase = 0.06
step_conc = 0.005


def with_halo(x, sides, width):
    for axis, dim in sides:
        count, length = (lax.axis_size(axis), x.shape[dim])
        up = [(i, (i + 1) % count) for i in range(count)]
        down = [(j, i) for i, j in up]
        last = lax.slice_in_dim(x, length - width, length, axis=dim)
        initial = lax.slice_in_dim(x, 0, width, axis=dim)
        before = lax.ppermute(last, axis, up)
        after = lax.ppermute(initial, axis, down)
        x = jnp.concatenate([before, x, after], axis=dim)
    return x


def column(values):
    return values.reshape(4, 1, 1, 1)


def phases_from(labels, seed_noise):
    marks = lax.broadcasted_iota(jnp.int32, (4, 1, 1, 1), 0)
    raw = seed_noise + 2.0 * (labels[None] == marks).astype(seed_noise.dtype)
    return raw / jnp.sum(raw, axis=0, keepdims=True)


def partition(phase, conc, curvature, quartic, wells):
    coef_a = column(curvature)
    coef_b = column(quartic)
    centre = column(wells)
    part = jnp.broadcast_to(conc[None], phase.shape)
    deviate = part - centre
    chem = jnp.sum(phase * (coef_a * deviate + coef_b * deviate**3), axis=0)
    for _ in range(NEWTON):
        deviate = part - centre
        slope = coef_a * deviate + coef_b * deviate**3 - chem[None]
        stiff = coef_a + 3.0 * coef_b * deviate * deviate
        shift = (
            conc - jnp.sum(phase * part, axis=0) + jnp.sum(phase * slope / stiff, axis=0)
        ) / jnp.sum(phase / stiff, axis=0)
        part = part + (shift[None] - slope) / stiff
        chem = chem + shift
    return (part, chem)


def stress_of(strain, eigen_field, lam_field, shear_field):
    elastic = strain - eigen_field
    trace = elastic[0] + elastic[1] + elastic[2]
    normal = (lax.broadcasted_iota(jnp.int32, (6, 1, 1, 1), 0) < 3).astype(strain.dtype)
    return 2.0 * shear_field[None] * elastic + (lam_field * trace)[None] * normal


def green(tau, freq_x, freq_y, freq_z, zero, lam0, mu0):
    vec_x = tau[0] * freq_x + tau[5] * freq_y + tau[4] * freq_z
    vec_y = tau[5] * freq_x + tau[1] * freq_y + tau[3] * freq_z
    vec_z = tau[4] * freq_x + tau[3] * freq_y + tau[2] * freq_z
    inner = freq_x * vec_x + freq_y * vec_y + freq_z * vec_z
    square = freq_x * freq_x + freq_y * freq_y + freq_z * freq_z + zero
    first = 1.0 / (2.0 * mu0 * square)
    second = (lam0 + mu0) / (mu0 * (lam0 + 2.0 * mu0)) * inner / (square * square)
    pairs = (
        (freq_x, vec_x, freq_x, vec_x),
        (freq_y, vec_y, freq_y, vec_y),
        (freq_z, vec_z, freq_z, vec_z),
        (freq_y, vec_y, freq_z, vec_z),
        (freq_x, vec_x, freq_z, vec_z),
        (freq_x, vec_x, freq_y, vec_y),
    )
    result = [(fk * vh + fh * vk) * first - fk * fh * second for fk, vk, fh, vh in pairs]
    return jnp.stack(result, axis=0)


def tables(length):
    grid = lax.broadcasted_iota(jnp.int32, (length, length), 0) * lax.broadcasted_iota(
        jnp.int32, (length, length), 1
    )
    angle = (grid % length).astype(jnp.float32) * (2.0 * math.pi / length)
    return (jnp.cos(angle), jnp.sin(angle))


def apply_table(table, data, axis):
    if axis == 3:
        flat = data.reshape(-1, data.shape[3])
        result = jnp.dot(
            flat, table.T, precision=lax.Precision.HIGHEST, preferred_element_type=jnp.float32
        )
        return result.reshape(data.shape[:3] + (table.shape[0],))
    moved = jnp.moveaxis(data, axis, 0)
    rest = moved.shape[1:]
    flat = moved.reshape(moved.shape[0], -1)
    result = jnp.dot(
        table, flat, precision=lax.Precision.HIGHEST, preferred_element_type=jnp.float32
    )
    return jnp.moveaxis(result.reshape((table.shape[0],) + rest), 0, axis)


def transform(pair, axis, inverse):
    real, imag = pair
    length = real.shape[axis]
    cosine, sine = tables(length)
    if inverse:
        new_real = (apply_table(cosine, real, axis) - apply_table(sine, imag, axis)) / length
        new_imag = (apply_table(cosine, imag, axis) + apply_table(sine, real, axis)) / length
    else:
        new_real = apply_table(cosine, real, axis) + apply_table(sine, imag, axis)
        new_imag = apply_table(cosine, imag, axis) - apply_table(sine, real, axis)
    return (new_real, new_imag)


def spectrum(stress):
    length = stress.shape[3]
    cosine, sine = tables(length)
    real = apply_table(cosine, stress, 3)
    imag = -apply_table(sine, stress, 3)
    real, imag = transform(
        (
            lax.all_to_all(real, "gy", split_axis=3, concat_axis=2, tiled=True),
            lax.all_to_all(imag, "gy", split_axis=3, concat_axis=2, tiled=True),
        ),
        axis=2,
        inverse=False,
    )
    real, imag = transform(
        (
            lax.all_to_all(real, "gx", split_axis=2, concat_axis=1, tiled=True),
            lax.all_to_all(imag, "gx", split_axis=2, concat_axis=1, tiled=True),
        ),
        axis=1,
        inverse=False,
    )
    return (real, imag)


def recover(pair):
    pair = transform(pair, 1, True)
    pair = transform(
        (
            lax.all_to_all(pair[0], "gx", split_axis=1, concat_axis=2, tiled=True),
            lax.all_to_all(pair[1], "gx", split_axis=1, concat_axis=2, tiled=True),
        ),
        axis=2,
        inverse=True,
    )
    result = transform(
        (
            lax.all_to_all(pair[0], "gy", split_axis=2, concat_axis=3, tiled=True),
            lax.all_to_all(pair[1], "gy", split_axis=2, concat_axis=3, tiled=True),
        ),
        axis=3,
        inverse=True,
    )
    return result


def frequencies(count, offset, length, axis):
    index = lax.iota(jnp.int32, count) + offset
    index = jnp.where(index >= length // 2, index - length, index)
    kept = jnp.where(index == -(length // 2), 0, index)
    dims_shape = [1, 1, 1]
    dims_shape[axis] = count
    return (kept.astype(jnp.float32) / length).reshape(dims_shape)


def wave_numbers(dims, full_x, full_y, full_z):
    offsets = (jnp.int32(0), lax.axis_index("gx") * dims[2], lax.axis_index("gy") * dims[3])
    freq_x = frequencies(dims[1], offsets[0], full_x, 0)
    freq_y = frequencies(dims[2], offsets[1], full_y, 1)
    freq_z = frequencies(dims[3], offsets[2], full_z, 2)
    zero = ((freq_x == 0.0) & (freq_y == 0.0) & (freq_z == 0.0)).astype(jnp.float32)
    return (freq_x, freq_y, freq_z, zero)


def slots_fit(full_z):
    count = lax.axis_size("gx") * lax.axis_size("gy")
    return full_z % 2 == 0 and (full_z // 2) % count == 0


def angles(length):
    grid = np.outer(np.arange(length), np.arange(length)) % length
    return grid * (2.0 * math.pi / length)


def z_tables(length):
    half = length // 2
    angle = angles(length)[:half]
    real = np.cos(angle)
    imag = -np.sin(angle)
    imag[0] = np.cos(math.pi * np.arange(length))
    forward = np.stack([real, imag], axis=1).astype(np.float32)
    weight = np.full((half, 1, 1), 2.0 / length)
    weight[0] = 1.0 / length
    return forward, (np.stack([real, imag], axis=1) * weight).astype(np.float32)


def complex_table(length, inverse):
    angle = angles(length)
    cosine, sine = np.cos(angle), np.sin(angle)
    if inverse:
        table = np.array([[cosine, -sine], [sine, cosine]]) / length
    else:
        table = np.array([[cosine, sine], [-sine, cosine]])
    return table.transpose(0, 2, 1, 3).astype(np.float32)


def contract(spec, *operands):
    return jnp.einsum(
        spec, *operands, precision=lax.Precision.HIGH, preferred_element_type=jnp.float32
    )


def fluctuation(stress, full_x, full_y, full_z, lam0, mu0):
    count_x, count_y = lax.axis_size("gx"), lax.axis_size("gy")
    count = count_x * count_y
    _, size_x, size_y, _ = stress.shape
    slots = full_z // 2 // count
    forward_z, inverse_z = z_tables(full_z)
    data = contract("krz,cxyz->krcxy", forward_z, stress)
    data = lax.all_to_all(data, ("gx", "gy"), split_axis=0, concat_axis=0, tiled=True)
    data = data.reshape(count_x, count_y, slots, 2, 6, size_x, size_y)
    data = data.transpose(2, 3, 4, 0, 5, 1, 6).reshape(slots, 2, 6, full_x, full_y)
    data = contract("sLrl,krcly->kscLy", complex_table(full_x, False), data)
    data = contract("sLrl,krcxl->kscxL", complex_table(full_y, False), data)
    data = data.transpose(2, 1, 3, 4, 0)
    freq_x = frequencies(full_x, 0, full_x, 0)
    freq_y = frequencies(full_y, 0, full_y, 1)
    position = lax.axis_index("gx") * count_y + lax.axis_index("gy")
    freq_z = frequencies(slots, position * slots, full_z, 2)
    zero = ((freq_x == 0.0) & (freq_y == 0.0) & (freq_z == 0.0)).astype(jnp.float32)
    data = jnp.stack([green(data[:, r], freq_x, freq_y, freq_z, zero, lam0, mu0) for r in (0, 1)], 1)
    data = data.transpose(4, 1, 0, 2, 3)
    data = contract("sLrl,krcxl->kscxL", complex_table(full_y, True), data)
    data = contract("sLrl,krcly->kscLy", complex_table(full_x, True), data)
    data = data.reshape(slots, 2, 6, count_x, size_x, count_y, size_y)
    data = data.transpose(3, 5, 0, 1, 2, 4, 6).reshape(count * slots, 2, 6, size_x, size_y)
    data = lax.all_to_all(data, ("gx", "gy"), split_axis=0, concat_axis=0, tiled=True)
    return contract("krz,krcxy->cxyz", inverse_z, data)


def fluctuation_general(stress, full_x, full_y, full_z, lam0, mu0):
    real, imag = spectrum(stress)
    freq_x, freq_y, freq_z, zero = wave_numbers(real.shape, full_x, full_y, full_z)
    upd_real = green(real, freq_x, freq_y, freq_z, zero, lam0, mu0)
    upd_imag = green(imag, freq_x, freq_y, freq_z, zero, lam0, mu0)
    packed = (upd_real[0::2] - upd_imag[1::2], upd_imag[0::2] + upd_real[1::2])
    back_real, back_imag = recover(packed)
    return jnp.stack([back_real, back_imag], axis=1).reshape(stress.shape)


MESH = pl.DeviceIdType.MESH
LANES = 128
ROWS = 8


def kernel_fits(shape):
    count_x, count_y = lax.axis_size("gx"), lax.axis_size("gy")
    size_x, size_y, full_z = shape
    return (
        full_z == 2 * count_x * count_y
        and count_x == ROWS
        and count_y * size_y == LANES
        and size_x * size_y == 2 * LANES
        and (count_x * count_y) % 16 == 0
    )


def split(value):
    high = value.astype(jnp.bfloat16)
    return high, (value - high.astype(jnp.float32)).astype(jnp.bfloat16)


def split_table(table):
    high = np.asarray(table, np.float32).astype(jnp.bfloat16)
    low = (np.asarray(table, np.float64) - high.astype(np.float64)).astype(jnp.bfloat16)
    return high, low


def table_left(table):
    high, low = split_table(table)
    return np.concatenate([high, high, low], axis=1)


def table_right(table):
    high, low = split_table(table)
    return np.stack([high, low])


def left_product(table, value):
    high, low = split(value)
    stacked = jnp.concatenate([high, low, high], axis=0)
    return jnp.dot(table, stacked, preferred_element_type=jnp.float32)


def right_product(value, table):
    high, low = split(value)
    product = functools.partial(jnp.dot, preferred_element_type=jnp.float32)
    return product(high, table[0]) + (product(low, table[0]) + product(high, table[1]))


def kernel_tables(size_x, full_x, full_y, full_z):
    forward, inverse = z_tables(full_z)
    forward = forward.transpose(1, 0, 2).reshape(full_z, full_z)
    inverse = inverse.transpose(2, 1, 0).reshape(full_z, full_z)
    count_x = full_x // size_x
    order = np.arange(full_x).reshape(count_x, size_x).T.reshape(-1)
    to_x = complex_table(full_x, False).transpose(0, 1, 2, 3)
    forward_x = to_x.transpose(0, 1, 2, 3)[:, :, :, order]
    inverse_x = complex_table(full_x, True)[:, order]
    forward_y = complex_table(full_y, False)
    inverse_y = complex_table(full_y, True)
    flat = lambda table, length: table.reshape(2 * length, 2 * length)
    return (
        table_left(forward),
        table_left(flat(forward_x, full_x)),
        table_right(flat(forward_y, full_y).T),
        table_right(flat(inverse_y, full_y).T),
        table_left(flat(inverse_x, full_x)),
        table_left(inverse),
    )


def position():
    return lax.axis_index("gx") * lax.axis_size("gy") + lax.axis_index("gy")


def for_others(action):
    count_x, count_y = lax.axis_size("gx"), lax.axis_size("gy")
    i, j = lax.axis_index("gx"), lax.axis_index("gy")
    turns = [j] + [lax.rem(j + step, count_y) for step in range(1, count_y)]
    for other in turns[1:]:
        action(i, other)

    def row(step, carry):
        far = lax.rem(i + step, count_x)
        for other in turns:
            action(far, other)
        return carry

    lax.fori_loop(1, count_x, row, 0)


def greet():
    barrier = pltpu.get_barrier_semaphore()
    for_others(
        lambda i, j: pl.semaphore_signal(barrier, inc=1, device_id=(i, j), device_id_type=MESH)
    )


def greeted():
    count = lax.axis_size("gx") * lax.axis_size("gy")
    pl.semaphore_wait(pltpu.get_barrier_semaphore(), count - 1)


def exchange_start(pack):
    sent, received, send_sem, recv_sem = pack
    count_y = lax.axis_size("gy")
    rows = sent.shape[0] // (lax.axis_size("gx") * count_y)
    own = pl.ds(pl.multiple_of(position() * rows, 8), rows)

    def send(i, j):
        pltpu.make_async_remote_copy(
            src_ref=sent.at[pl.ds(pl.multiple_of((i * count_y + j) * rows, 8), rows)],
            dst_ref=received.at[own],
            send_sem=send_sem,
            recv_sem=recv_sem,
            device_id=(i, j),
            device_id_type=MESH,
        ).start()

    for_others(send)
    received[own, :] = sent[own, :]


def exchange_all(pack):
    sent, received, send_sem, recv_sem = pack
    count_x, count_y = lax.axis_size("gx"), lax.axis_size("gy")
    rows = sent.shape[0] // (count_x * count_y) * (count_x * count_y - 1)
    return pltpu.make_async_remote_copy(
        src_ref=sent.at[pl.ds(0, rows)],
        dst_ref=received.at[pl.ds(0, rows)],
        send_sem=send_sem,
        recv_sem=recv_sem,
        device_id=(lax.rem(lax.axis_index("gx") + 1, count_x), lax.axis_index("gy")),
        device_id_type=MESH,
    )


def exchange_wait(pack, arrived):
    if arrived:
        exchange_all(pack).wait_recv()
    else:
        exchange_all(pack).wait_send()


def swap_blocks(parts):
    count = len(parts)
    width = LANES // count
    block = lax.broadcasted_iota(jnp.int32, parts[0].shape, 1) // width
    result = []
    for a in range(count):
        total = None
        for b, part in enumerate(parts):
            shift = (width * (b - a)) % LANES
            moved = pltpu.roll(part, shift, 1) if shift else part
            total = moved if total is None else jnp.where(block == b, moved, total)
        result.append(total)
    return result


MAIN = (0, 4)
PAIR = (4, 6)
GROUPS = (MAIN, PAIR)


def halves(z_ref, t_ref, sent, group):
    slots = z_ref.shape[0] // 2
    rows = 4 * (group[1] - group[0])
    for c in range(*group):
        result = left_product(z_ref[...], t_ref[c])
        for r in range(2):
            for h in range(2):
                piece = result[r * slots:(r + 1) * slots, h * LANES:(h + 1) * LANES]
                first = (c - group[0]) * 4 + r * 2 + h
                sent[pl.ds(first, slots, stride=rows), :] = piece


def plane_rows(received, c, r, count_y, rows):
    result = []
    for h in range(2):
        first = c * 4 + r * 2 + h
        parts = [
            received[pl.ds(j * rows + first, ROWS, stride=rows * count_y), :]
            for j in range(count_y)
        ]
        result += swap_blocks(parts)
    return jnp.concatenate(result, axis=0)


def plane_store(sent, value, c, r, count_y, rows):
    for h in range(2):
        first = c * 4 + r * 2 + h
        parts = [
            value[(h * count_y + a) * ROWS:(h * count_y + a + 1) * ROWS] for a in range(count_y)
        ]
        for j, part in enumerate(swap_blocks(parts)):
            sent[pl.ds(j * rows + first, ROWS, stride=rows * count_y), :] = part


def plane_forward(received, plane_ref, fx_ref, fy_ref, group, full_x, full_y):
    count_y = lax.axis_size("gy")
    number = group[1] - group[0]
    rows_x = []
    for c in range(number):
        both = [plane_rows(received, c, r, count_y, 4 * number) for r in range(2)]
        rows_x.append(jnp.concatenate(both, axis=0))
    spec = left_product(fx_ref[...], jnp.concatenate(rows_x, axis=1))
    lanes = []
    for c in range(number):
        part = spec[:, c * full_y:(c + 1) * full_y]
        lanes.append(jnp.concatenate([part[:full_x], part[full_x:]], axis=1))
    spec = right_product(jnp.concatenate(lanes, axis=0), fy_ref)
    plane_ref[group[0] * full_x:group[1] * full_x, :] = spec


def plane_green(plane_ref, wave_ref, full_x, full_z):
    freq_z = lax.convert_element_type(position(), jnp.float32) * (1.0 / full_z)

    def chunk(step, carry):
        start = pl.multiple_of(step * ROWS, ROWS)
        at = pl.ds(start, ROWS)
        where = [pl.ds(pl.multiple_of(c * full_x + start, ROWS), ROWS) for c in range(6)]
        first, second, freq_x, freq_y = [wave_ref[w, at, :] for w in range(4)]
        tau = [plane_ref[where[c], :] for c in range(6)]
        vec_x = tau[0] * freq_x + tau[5] * freq_y + tau[4] * freq_z
        vec_y = tau[5] * freq_x + tau[1] * freq_y + tau[3] * freq_z
        vec_z = tau[4] * freq_x + tau[3] * freq_y + tau[2] * freq_z
        inner = (freq_x * vec_x + freq_y * vec_y + freq_z * vec_z) * second
        pairs = (
            (freq_x, vec_x, freq_x, vec_x),
            (freq_y, vec_y, freq_y, vec_y),
            (freq_z, vec_z, freq_z, vec_z),
            (freq_y, vec_y, freq_z, vec_z),
            (freq_x, vec_x, freq_z, vec_z),
            (freq_x, vec_x, freq_y, vec_y),
        )
        for c, (fk, vk, fh, vh) in enumerate(pairs):
            plane_ref[where[c], :] = (fk * vh + fh * vk) * first - fk * fh * inner
        return carry

    lax.fori_loop(0, full_x // ROWS, chunk, 0)


def plane_back(plane_ref, sent, iy_ref, ix_ref, group, full_x, full_y):
    count_y = lax.axis_size("gy")
    number = group[1] - group[0]
    spec = right_product(plane_ref[group[0] * full_x:group[1] * full_x, :], iy_ref)
    lanes = []
    for c in range(number):
        part = spec[c * full_x:(c + 1) * full_x]
        lanes.append(jnp.concatenate([part[:, :full_y], part[:, full_y:]], axis=0))
    plane = left_product(ix_ref[...], jnp.concatenate(lanes, axis=1))
    for c in range(number):
        for r in range(2):
            value = plane[r * full_x:(r + 1) * full_x, c * full_y:(c + 1) * full_y]
            plane_store(sent, value, c, r, count_y, 4 * number)


def strain_update(received, wz_ref, strain_ref, group):
    slots = wz_ref.shape[0] // 2
    rows = 4 * (group[1] - group[0])
    for c in range(*group):
        value = jnp.concatenate([
            jnp.concatenate([
                received[pl.ds((c - group[0]) * 4 + r * 2 + h, slots, stride=rows), :]
                for h in range(2)
            ], axis=1) for r in range(2)
        ], axis=0)
        strain_ref[c] = strain_ref[c] - left_product(wz_ref[...], value)


def wave_parts(lame_ref, full_x, full_y, full_z):
    shape = (full_x, 2 * full_y)
    row = lax.broadcasted_iota(jnp.int32, shape, 0)
    lane = lax.broadcasted_iota(jnp.int32, shape, 1) % full_y

    def weight(index, length):
        signed = jnp.where(index >= length // 2, index - length, index)
        signed = jnp.where(signed == -(length // 2), 0, signed)
        return signed.astype(jnp.float32) * (1.0 / length)

    freq_x = weight(row, full_x)
    freq_y = weight(lane, full_y)
    freq_z = weight(jnp.full(shape, position(), jnp.int32), full_z)
    square = freq_x * freq_x + freq_y * freq_y + freq_z * freq_z
    square = jnp.where(square == 0.0, 1.0, square)

    def middle(which):
        values = [jnp.full(shape, lame_ref[which, a], jnp.float32) for a in range(4)]
        top = functools.reduce(jnp.maximum, values)
        return 0.5 * (top + functools.reduce(jnp.minimum, values))

    lam0, mu0 = middle(0), middle(1)
    first = 1.0 / (2.0 * mu0 * square)
    second = (lam0 + mu0) / (mu0 * (lam0 + 2.0 * mu0)) / (square * square)
    return first, second, freq_x, freq_y, freq_z


def elastic_chunk(at, strain_ref, field_ref):
    elastic = [strain_ref[p, at, :] - field_ref[2 + p, at, :] for p in range(6)]
    lam, shear2 = field_ref[0, at, :], 2.0 * field_ref[1, at, :]
    trace = elastic[0] + elastic[1] + elastic[2]
    stress = [shear2 * e for e in elastic]
    stress = [stress[p] + lam * trace if p < 3 else stress[p] for p in range(6)]
    return elastic, trace, stress


def half(h):
    return slice(h * LANES, (h + 1) * LANES)


def turned(value, shift):
    shift = shift % LANES
    return pltpu.roll(value, shift, 1) if shift else value


def lane_block(shape, width):
    return lax.broadcasted_iota(jnp.int32, shape, 1) // width


def lane_place(shape, width):
    return lax.broadcasted_iota(jnp.int32, shape, 1) % width


def halo_pack(phase_ref, chem_ref, x_up, x_down, y_up, y_down, width):
    full_z = phase_ref.shape[1]
    blocks = LANES // width
    fold = full_z // blocks
    block = lane_block((full_z, LANES), width)
    place = lane_place((full_z, LANES), width)
    fields = [phase_ref[f] for f in range(4)] + [chem_ref[...]]
    for face, h, own in ((x_up, 1, blocks - 1), (x_down, 0, 0)):
        total = turned(fields[0][:, half(h)], -width * own)
        for f in range(1, 4):
            total = jnp.where(block == f, turned(fields[f][:, half(h)], width * (f - own)), total)
        face[:full_z, :] = total
        parts = [fields[4][k * fold:(k + 1) * fold, half(h)] for k in range(blocks)]
        total = turned(parts[0], -width * own)
        for k in range(1, blocks):
            total = jnp.where(block[:fold] == k, turned(parts[k], width * (k - own)), total)
        face[full_z:, :] = total
    for face, own in ((y_up, width - 1), (y_down, 0)):
        total = jnp.zeros((full_z, LANES), jnp.float32)
        for f in range(5):
            for h in range(2):
                slot = 8 * h + f
                total = jnp.where(place == slot, turned(fields[f][:, half(h)], slot - own), total)
        face[...] = total


def halo_laplace(f, field, x_before, x_after, y_before, y_after, width):
    full_z = field.shape[0]
    blocks = LANES // width
    fold = full_z // blocks
    block = lane_block((full_z, LANES), width)
    place = lane_place((full_z, LANES), width)

    def face(ref, own):
        if f < 4:
            return turned(ref[:full_z, :], width * (own - f))
        folded = ref[full_z:, :]
        return jnp.concatenate([turned(folded, width * (own - k)) for k in range(blocks)], axis=0)

    sides = [field[:, half(h)] for h in range(2)]
    right = [turned(side, width) for side in sides]
    left = [turned(side, -width) for side in sides]
    last = blocks - 1
    result = []
    for h in range(2):
        slot = 8 * h + f
        side = sides[h]
        below = jnp.where(block == 0, face(x_before, 0) if h == 0 else right[0], right[h])
        above = jnp.where(block == last, left[1] if h == 0 else face(x_after, last), left[h])
        total = below + above - 6.0 * side
        total += jnp.where(place == 0, turned(y_before[...], -slot), turned(side, 1))
        after = turned(y_after[...], width - 1 - slot)
        total += jnp.where(place == width - 1, after, turned(side, -1))
        total += pltpu.roll(side, 1, 0) + pltpu.roll(side, full_z - 1, 0)
        result.append(total)
    return result


def newton_chunk(phase, conc, scalars):
    curve, quart, wells = scalars
    part = [conc for _ in range(4)]
    dev = [conc - wells[a] for a in range(4)]
    chem = sum(
        phase[a] * (curve[a] * dev[a] + quart[a] * (dev[a] * dev[a] * dev[a])) for a in range(4)
    )
    for _ in range(NEWTON):
        dev = [part[a] - wells[a] for a in range(4)]
        square = [d * d for d in dev]
        slope = [dev[a] * (curve[a] + quart[a] * square[a]) - chem for a in range(4)]
        soft = [1.0 / (curve[a] + (3.0 * quart[a]) * square[a]) for a in range(4)]
        weight = [phase[a] * soft[a] for a in range(4)]
        top = conc - sum(phase[a] * part[a] for a in range(4))
        top = top + sum(weight[a] * slope[a] for a in range(4))
        shift = top / sum(weight)
        part = [part[a] + (shift - slope[a]) * soft[a] for a in range(4)]
        chem = chem + shift
    dev = [part[a] - wells[a] for a in range(4)]
    square = [d * d for d in dev]
    total = sum(p * p for p in phase)
    local = []
    for a in range(4):
        energy = square[a] * (0.5 * curve[a] + (0.25 * quart[a]) * square[a])
        barrier = 2.0 * phase[a] * (total - phase[a] * phase[a])
        local.append(energy - chem * part[a] + barrier)
    return chem, local


def step_kernel(
    full_x, full_y, labels_in, noise_in, raw_conc_in, curve_ref, quart_ref, wells_ref, lame_ref,
    eigen_ref, mz_in, fx_in, fy_in, iy_in, ix_in, wz_in,
    next_ref, conc_next_ref, stress_ref,
    labels_ref, noise_ref, raw_conc_ref, mz_ref, fx_ref, fy_ref, iy_ref, ix_ref, wz_ref, load_sem,
    phase_ref, conc_ref, chem_ref, local_ref, field_ref, strain_ref, t_ref, plane_ref, wave_ref,
    *buffers
):
    full_z = phase_ref.shape[1]
    chunks = full_z // ROWS
    width = full_y // lax.axis_size("gy")
    number = 2 * ITERS * len(GROUPS)
    free = iter([buffers[4 * n:4 * n + 4] for n in range(number)])
    packs = [{group: next(free) for group in GROUPS} for t in range(2 * ITERS)]
    halo_sent, halo_got = buffers[4 * number:4 * number + 4], buffers[4 * number + 4:4 * number + 8]
    halo_send, halo_recv = buffers[4 * number + 8:]
    loads = [
        pltpu.make_async_copy(source, target, load_sem.at[n])
        for n, (source, target) in enumerate((
            (noise_in, noise_ref), (labels_in, labels_ref), (raw_conc_in, raw_conc_ref),
            (mz_in, mz_ref), (fx_in, fx_ref), (fy_in, fy_ref), (iy_in, iy_ref), (ix_in, ix_ref),
            (wz_in, wz_ref),
        ))
    ]
    for load in loads:
        load.start()
    greet()
    for load in loads[:2]:
        load.wait()

    for h in range(2):
        at = pl.ds(h * LANES, LANES)
        label = labels_ref[at, :]
        raw = [noise_ref[a, at, :] + jnp.where(label == a, 2.0, 0.0) for a in range(4)]
        for a in range(4):
            phase_ref[a, :, half(h)] = raw[a].T

    def rows_at(step):
        return pl.ds(pl.multiple_of(step * ROWS, ROWS), ROWS)

    def fields(step, carry):
        at = rows_at(step)
        raw = [phase_ref[a, at, :] for a in range(4)]
        share = 1.0 / (raw[0] + raw[1] + raw[2] + raw[3])
        phase = [value * share for value in raw]
        for a in range(4):
            phase_ref[a, at, :] = phase[a]
        for which in range(2):
            field_ref[which, at, :] = sum(phase[a] * lame_ref[which, a] for a in range(4))
        for p in range(6):
            field_ref[2 + p, at, :] = sum(phase[a] * eigen_ref[a, p] for a in range(4))
            strain_ref[p, at, :] = jnp.zeros_like(phase[0])
        _, _, stress = elastic_chunk(at, strain_ref, field_ref)
        for p in range(6):
            t_ref[p, at, :] = stress[p]
        return carry

    def main_stresses(step, carry):
        at = rows_at(step)
        elastic = [strain_ref[p, at, :] - field_ref[2 + p, at, :] for p in range(4)]
        spread = field_ref[0, at, :] * (elastic[0] + elastic[1] + elastic[2])
        shear2 = 2.0 * field_ref[1, at, :]
        for p in range(4):
            t_ref[p, at, :] = shear2 * elastic[p] + spread if p < 3 else shear2 * elastic[p]
        return carry

    def pair_stresses(step, carry):
        at = rows_at(step)
        shear2 = 2.0 * field_ref[1, at, :]
        for p in range(*PAIR):
            t_ref[p, at, :] = shear2 * (strain_ref[p, at, :] - field_ref[2 + p, at, :])
        return carry

    def newton(step, carry):
        at = rows_at(step)
        phase = [phase_ref[a, at, :] for a in range(4)]
        scalars = [[ref[a] for a in range(4)] for ref in (curve_ref, quart_ref, wells_ref)]
        chem, local = newton_chunk(phase, conc_ref[at, :], scalars)
        chem_ref[at, :] = chem
        for a in range(4):
            local_ref[a, at, :] = local[a]
        return carry

    def halo_copies():
        i, j = lax.axis_index("gx"), lax.axis_index("gy")
        count_x, count_y = lax.axis_size("gx"), lax.axis_size("gy")
        targets = (
            (lax.rem(i + 1, count_x), j),
            (lax.rem(i + count_x - 1, count_x), j),
            (i, lax.rem(j + 1, count_y)),
            (i, lax.rem(j + count_y - 1, count_y)),
        )
        return [
            pltpu.make_async_remote_copy(
                src_ref=halo_sent[n],
                dst_ref=halo_got[n],
                send_sem=halo_send.at[n],
                recv_sem=halo_recv.at[n],
                device_id=target,
                device_id_type=MESH,
            )
            for n, target in enumerate(targets)
        ]

    def beside_first():
        loads[2].wait()
        for h in range(2):
            conc_ref[:, half(h)] = raw_conc_ref[pl.ds(h * LANES, LANES), :].T
        for w, value in enumerate(wave_parts(lame_ref, full_x, full_y, full_z)[:4]):
            wave_ref[w] = value
        lax.fori_loop(0, chunks // 2, newton, 0)
        for load in loads[4:]:
            load.wait()

    def beside_second():
        lax.fori_loop(chunks // 2, chunks, newton, 0)
        halo_pack(phase_ref, chem_ref, *halo_sent, width)
        for copy in halo_copies():
            copy.start()

    def beside_third():
        for copy in halo_copies():
            copy.wait_recv()
        for f in range(5):
            field = phase_ref[f] if f < 4 else chem_ref[...]
            spread = halo_laplace(f, field, *halo_got, width)
            for h in range(2):
                if f < 4:
                    local_ref[f, :, half(h)] = local_ref[f, :, half(h)] - spread[h]
                else:
                    conc_next_ref[:, half(h)] = conc_ref[:, half(h)] + step_conc * spread[h]

    def send_there(turn, group):
        pack = packs[2 * turn][group]
        halves(mz_ref, t_ref, pack[0], group)
        if turn == 0 and group is MAIN:
            greeted()
        exchange_start(pack)

    lax.fori_loop(0, chunks, fields, 0)
    loads[3].wait()
    send_there(0, MAIN)
    send_there(0, PAIR)
    for turn in range(ITERS):
        there, back = packs[2 * turn], packs[2 * turn + 1]
        if turn == 0:
            beside_first()
        elif turn == 1:
            beside_third()
        for group in (PAIR, MAIN) if turn else (MAIN, PAIR):
            exchange_wait(there[group], True)
            plane_forward(there[group][1], plane_ref, fx_ref, fy_ref, group, full_x, full_y)
        plane_green(plane_ref, wave_ref, full_x, full_z)
        for group in (PAIR, MAIN):
            plane_back(plane_ref, back[group][0], iy_ref, ix_ref, group, full_x, full_y)
            exchange_start(back[group])
        if turn == 0:
            beside_second()
        exchange_wait(back[PAIR], True)
        strain_update(back[PAIR][1], wz_ref, strain_ref, PAIR)
        if turn + 1 < ITERS:
            lax.fori_loop(0, chunks, pair_stresses, 0)
            send_there(turn + 1, PAIR)
        exchange_wait(back[MAIN], True)
        strain_update(back[MAIN][1], wz_ref, strain_ref, MAIN)
        if turn + 1 < ITERS:
            lax.fori_loop(0, chunks, main_stresses, 0)
            send_there(turn + 1, MAIN)

    def finish(step, carry):
        at = rows_at(step)
        elastic, trace, stress = elastic_chunk(at, strain_ref, field_ref)
        for p in range(6):
            stress_ref[p, at, :] = stress[p]
        squares = sum(e * e for e in elastic[:3]) + 2.0 * sum(e * e for e in elastic[3:])
        force = []
        for a in range(4):
            coupling = sum(
                stress[p] * (eigen_ref[a, p] * (1.0 if p < 3 else 2.0)) for p in range(6)
            )
            stored = 0.5 * lame_ref[0, a] * trace * trace + lame_ref[1, a] * squares
            force.append(local_ref[a, at, :] + (stored - coupling))
        mean = 0.25 * (force[0] + force[1] + force[2] + force[3])
        for a in range(4):
            next_ref[a, at, :] = phase_ref[a, at, :] - step_phase * (force[a] - mean)
        return carry

    lax.fori_loop(0, chunks, finish, 0)
    for group_packs in packs:
        for pack in group_packs.values():
            exchange_wait(pack, False)
    for copy in halo_copies():
        copy.wait_send()


def place_kernel(next_in, conc_in, stress_in, next_out, conc_out, stress_out, got, made, got_sem, made_sem):
    sources = [stress_in.at[p] for p in range(6)] + [next_in.at[a] for a in range(4)] + [conc_in]
    targets = [stress_out.at[p] for p in range(6)] + [next_out.at[a] for a in range(4)] + [conc_out]
    number = len(sources)
    loads = [pltpu.make_async_copy(sources[n], got.at[n], got_sem.at[n]) for n in range(number)]
    stores = [pltpu.make_async_copy(made.at[n], targets[n], made_sem.at[n]) for n in range(number)]
    for load in loads:
        load.start()
    for n in range(number):
        loads[n].wait()
        for h in range(got.shape[2] // LANES):
            made[n, half(h), :] = got[n, :, half(h)].T
        stores[n].start()
    for store in stores:
        store.wait()


def place_call(phase_next, conc_next, stress):
    full_z, cells = conc_next.shape
    hbm = pl.BlockSpec(memory_space=pl.ANY)
    turned_shape = lambda *lead: jax.ShapeDtypeStruct(lead + (cells, full_z), jnp.float32)
    return pl.pallas_call(
        place_kernel,
        out_shape=(turned_shape(4), turned_shape(), turned_shape(6)),
        in_specs=[hbm] * 3,
        out_specs=(hbm,) * 3,
        scratch_shapes=[
            pltpu.VMEM((11, full_z, cells), jnp.float32),
            pltpu.VMEM((11, cells, full_z), jnp.float32),
            pltpu.SemaphoreType.DMA((11,)),
            pltpu.SemaphoreType.DMA((11,)),
        ],
        compiler_params=pltpu.CompilerParams(vmem_limit_bytes=56 * 1024 * 1024),
    )(phase_next, conc_next, stress)


def step_call(labels, seed_noise, conc, curvature, quartic, wells, lame, eigen, full_x, full_y):
    size_x, size_y, full_z = labels.shape
    cells = size_x * size_y
    count = full_z // 2
    tables = [jnp.asarray(t) for t in kernel_tables(size_x, full_x, full_y, full_z)]
    vmem = pl.BlockSpec(memory_space=pltpu.VMEM)
    smem = pl.BlockSpec(memory_space=pltpu.SMEM)
    hbm = pl.BlockSpec(memory_space=pltpu.HBM)
    scratch = lambda *shape: pltpu.VMEM(shape, jnp.float32)
    buffers = []
    for t in range(2 * ITERS):
        for group in GROUPS:
            rows = 4 * (group[1] - group[0]) * count
            buffers += [scratch(rows, LANES), scratch(rows, LANES)]
            buffers += [pltpu.SemaphoreType.DMA] * 2
    x_face = scratch(full_z + full_z * size_y // LANES, LANES)
    y_face = scratch(full_z, LANES)
    buffers += [x_face, x_face, y_face, y_face] * 2 + [pltpu.SemaphoreType.DMA((4,))] * 2
    whole = lambda *lead: jax.ShapeDtypeStruct(lead + (full_z, cells), jnp.float32)
    result = pl.pallas_call(
        functools.partial(step_kernel, full_x, full_y),
        out_shape=(whole(4), whole(), whole(6)),
        in_specs=[hbm] * 3 + [smem] * 5 + [hbm] * 6,
        out_specs=(vmem, vmem, vmem),
        scratch_shapes=[pltpu.VMEM((cells, full_z), jnp.int32)]
        + [scratch(4, cells, full_z), scratch(cells, full_z)]
        + [pltpu.VMEM(table.shape, table.dtype) for table in tables]
        + [pltpu.SemaphoreType.DMA((3 + len(tables),))]
        + [
            scratch(4, full_z, cells),
            scratch(full_z, cells),
            scratch(full_z, cells),
            scratch(4, full_z, cells),
            scratch(8, full_z, cells),
            scratch(6, full_z, cells),
            scratch(6, full_z, cells),
            scratch(6 * full_x, 2 * full_y),
            scratch(4, full_x, 2 * full_y),
        ]
        + buffers,
        compiler_params=pltpu.CompilerParams(
            collective_id=0, has_side_effects=True, vmem_limit_bytes=56 * 1024 * 1024
        ),
    )(
        labels.reshape(cells, full_z), seed_noise.reshape(4, cells, full_z),
        conc.reshape(cells, full_z), curvature, quartic, wells, lame, eigen, *tables
    )
    phase_next, conc_next, stress = place_call(*result)
    shape = (size_x, size_y, full_z)
    return phase_next.reshape((4,) + shape), conc_next.reshape(shape), stress.reshape((6,) + shape)


def laplace_padded(padded):
    centre = padded[:, 1:-1, 1:-1, :]
    total = -6.0 * centre
    total = total + padded[:, 2:, 1:-1, :] + padded[:, :-2, 1:-1, :]
    total = total + padded[:, 1:-1, 2:, :] + padded[:, 1:-1, :-2, :]
    total = total + jnp.roll(centre, 1, 3) + jnp.roll(centre, -1, 3)
    return total


def shards(labels, seed_noise, conc, curvature, quartic, wells, lame, eigen):
    full_x = labels.shape[0] * lax.axis_size("gx")
    full_y = labels.shape[1] * lax.axis_size("gy")
    full_z = labels.shape[2]
    if kernel_fits(labels.shape):
        return step_call(
            labels, seed_noise, conc, curvature, quartic, wells, lame, eigen, full_x, full_y
        )
    phase = phases_from(labels, seed_noise)
    part, chem = partition(phase, conc, curvature, quartic, wells)
    stacked = jnp.concatenate([phase, chem[None]], axis=0)
    padded = with_halo(stacked, (("gx", 1), ("gy", 2)), 1)
    lam_field = jnp.sum(phase * column(lame[0]), axis=0)
    shear_field = jnp.sum(phase * column(lame[1]), axis=0)
    eigen_field = jnp.einsum("ap,axyz->pxyz", eigen, phase, precision=lax.Precision.HIGHEST)
    lam0 = 0.5 * (jnp.max(lame[0]) + jnp.min(lame[0]))
    mu0 = 0.5 * (jnp.max(lame[1]) + jnp.min(lame[1]))
    strain = jnp.zeros((6,) + labels.shape, jnp.float32)
    step = fluctuation if slots_fit(full_z) else fluctuation_general
    for _ in range(ITERS):
        stress = stress_of(strain, eigen_field, lam_field, shear_field)
        strain = strain - step(stress, full_x, full_y, full_z, lam0, mu0)
    stress = stress_of(strain, eigen_field, lam_field, shear_field)
    elastic = strain - eigen_field
    trace = elastic[0] + elastic[1] + elastic[2]
    squares = (
        elastic[0] ** 2
        + elastic[1] ** 2
        + elastic[2] ** 2
        + 2.0 * (elastic[3] ** 2 + elastic[4] ** 2 + elastic[5] ** 2)
    )
    weight = jnp.array([1.0, 1.0, 1.0, 2.0, 2.0, 2.0], jnp.float32)
    coupling = jnp.einsum(
        "ap,pxyz->axyz", eigen * weight[None], stress, precision=lax.Precision.HIGHEST
    )
    stored = (
        0.5 * (column(lame[0]) * trace[None] ** 2 + 2.0 * column(lame[1]) * squares[None])
        - coupling
    )
    deviate = part - column(wells)
    energy = 0.5 * column(curvature) * deviate**2 + 0.25 * column(quartic) * deviate**4
    chemical = energy - chem[None] * part
    total_sq = jnp.sum(phase * phase, axis=0)
    barrier = 2.0 * phase * (total_sq[None] - phase * phase)
    laplacian = laplace_padded(padded)
    force = chemical + stored + barrier - laplacian[:4]
    phase_next = phase - step_phase * (force - jnp.mean(force, axis=0, keepdims=True))
    conc_next = conc + step_conc * laplacian[4]
    return (phase_next, conc_next, stress)


def solution(mesh):
    in_specs = (
        P("gx", "gy", None),
        P(None, "gx", "gy", None),
        P("gx", "gy", None),
        P(),
        P(),
        P(),
        P(),
        P(),
    )
    out_specs = (P(None, "gx", "gy", None), P("gx", "gy", None), P(None, "gx", "gy", None))
    return jax.shard_map(shards, mesh=mesh, in_specs=in_specs, out_specs=out_specs, check_vma=False)
```
